128 devices in a mesh: expert: 32 (over z, x, core), tensor: 4 (over y).
Axes of the slice: x: 4, y: 4, z: 4, core: 2. Of those that a mesh axis runs over, the one named last changes fastest.
Arguments:
- tokens: bfloat16 [8192, 2048], P('expert'), may hold values from -6 to 6
- cotangent: bfloat16 [8192, 2048], P('expert'), may hold values from -6 to 6
- attn_gain: float32 [2048], replicated, may hold values from 0.5 to 1.5
- w_query: bfloat16 [2048, 3072], P(None, 'tensor'), may hold values from -0.125 to 0.125
- w_latent: bfloat16 [2048, 576], replicated, may hold values from -0.125 to 0.125
- latent_gain: float32 [512], replicated, may hold values from 0.5 to 1.5
- w_keyvalue: bfloat16 [512, 4096], P(None, 'tensor'), may hold values from -0.25 to 0.25
- w_output: bfloat16 [2048, 2048], P('tensor'), may hold values from -0.75 to 0.75
- ffn_gain: float32 [2048], replicated, may hold values from 0.5 to 1.5
- w_router: bfloat16 [2048, 64], replicated, may hold values from -0.0625 to 0.0625
- shared_gate: bfloat16 [2048, 2816], P(None, 'tensor'), may hold values from -0.125 to 0.125
- shared_up: bfloat16 [2048, 2816], P(None, 'tensor'), may hold values from -0.125 to 0.125
- shared_down: bfloat16 [2816, 2048], P('tensor'), may hold values from -0.109375 to 0.109375
- expert_gate: bfloat16 [64, 2048, 1408], P('expert', None, 'tensor'), may hold values from -0.125 to 0.125
- expert_up: bfloat16 [64, 2048, 1408], P('expert', None, 'tensor'), may hold values from -0.125 to 0.125
- expert_down: bfloat16 [64, 1408, 2048], P('expert', 'tensor'), may hold values from -0.15625 to 0.15625
- routes: int32 [8192, 6], P('expert'), may hold values from 0 to 63, all different within a row; in each aligned block of 256 rows (0 to 255, 256 to 511, ...) at most 32 rows name the same one
Outputs:
- output: bfloat16 [8192, 2048], P('expert')
- grad_tokens: bfloat16 [8192, 2048], P('expert')
- grad_attn_gain: float32 [2048], P('expert')
- grad_query: float32 [2048, 3072], P('expert', 'tensor')
- grad_latent: float32 [2048, 576], P('expert')
- grad_latent_gain: float32 [512], P('expert')
- grad_keyvalue: float32 [512, 4096], P('expert', 'tensor')
- grad_output: float32 [2048, 2048], P('tensor', 'expert')
- grad_ffn_gain: float32 [2048], P('expert')
- grad_router: float32 [2048, 64], P('expert')
- grad_shared_gate: float32 [2048, 2816], P('expert', 'tensor')
- grad_shared_up: float32 [2048, 2816], P('expert', 'tensor')
- grad_shared_down: float32 [2816, 2048], P('tensor', 'expert')
- grad_expert_gate: float32 [64, 2048, 1408], P('expert', None, 'tensor')
- grad_expert_up: float32 [64, 2048, 1408], P('expert', None, 'tensor')
- grad_expert_down: float32 [64, 1408, 2048], P('expert', 'tensor')
The draws below stay inside these ranges and needn't reach their ends.
Inputs may be any that keep to these rules, and one draw needn't show every extreme that they name: `routes`: the 6 experts of a token differ. Among the rows of one device no expert is named more than 32 times, a bound that some block reaches.
All inputs are finite; a program needn't handle non-finite values.
Results may differ from the reference program's by a relative error of at most 0.033.
Values may be sent and summed in bfloat16 or wider, within the bound.
No kernel may reach another device: no remote copies, remote signals or barrier semaphores. Data moves between devices by JAX's collectives and lax.ppermute only.
A program may use at most 256 MiB of HBM per device.

```python
import math
from functools import partial
import jax
import jax.numpy as jnp
import numpy as np
from jax import lax

D = 2048
HEADS = 16
NOPE = 128
ROPE = 64
VDIM = 128
KV_RANK = 512
EFF = 1408
SHARED_FF = 2816
TOP = 6
TOK_DEV = 256
EXPERTS = 64
TOKENS = 8192
CAP = 32
N_EXPERT = 32
N_TENSOR = 4


def levels(own_key, shape, shards, least, high):
    def one(dim, parts):
        steps = jax.random.uniform(jax.random.fold_in(jax.random.fold_in(own_key, 6), dim), (parts,), jnp.float32, least / len(shards), high / len(shards))
        return jnp.repeat(jnp.exp(steps), shape[dim] // parts).reshape((-1,) + (1,) * (len(shape) - dim - 1))

    gain = one(*shards[0])
    for cut in shards[1:]:
        gain = gain * one(*cut)
    return gain


def routed_block(key, own, number, rows, count, top, reach, lean):
    sequence = jax.random.permutation(key, count)
    packed, usual = shares(count, rows * top, reach, lean, True), shares(count, rows * top, reach, lean, False)
    places = jnp.arange(count)

    def named(lengths, rotation):
        used = int((lengths > 0).sum())
        fixed = max(1, used // 4)
        shifted = fixed + (places - fixed + rotation * (used - fixed)) % max(1, count - fixed)
        return jnp.zeros((count,), jnp.int32).at[sequence[jnp.where(places < fixed, places, shifted)]].set(jnp.asarray(lengths, jnp.int32))

    lengths = jnp.where(number % 4 == 0, named(packed, number // 4), named(usual, number - number // 4 - 1))
    mixed = jax.random.permutation(jax.random.fold_in(own, 3), count)
    giver, receiver = mixed[0:count // 2 * 2:2], mixed[1:count // 2 * 2:2]
    slack = jnp.minimum(lengths[giver] - 1, reach - lengths[receiver]) // 2
    slack = jnp.where((giver == sequence[0]) | (receiver == sequence[0]) | (lengths[receiver] == 0), 0, jnp.maximum(slack, 0))
    shifted = jax.random.randint(jax.random.fold_in(own, 4), (count // 2,), 0, 1 << 20) % (slack + 1)
    lengths = lengths.at[giver].add(-shifted).at[receiver].add(shifted)
    members = jnp.searchsorted(jnp.cumsum(lengths), jnp.arange(rows * top), side="right").astype(jnp.int32)
    listing = members.reshape(top, rows).T
    listing = listing[jax.random.permutation(jax.random.fold_in(own, 1), rows)]
    rotation = jax.random.randint(jax.random.fold_in(own, 2), (rows, 1), 0, top)
    return jnp.take_along_axis(listing, (jnp.arange(top)[None, :] + rotation) % top, axis=1)


def shares(count, total, most, slope, full):
    loads = [(1 << 20) // math.isqrt(standing ** slope) + 1 for standing in range(1, count + 1)]
    largest = most if full else min(most, max(-(-total // count), total * loads[0] // sum(loads)))
    least = 1 if total - largest >= count - 1 else 0
    holding, surplus = [largest] + [least] * (count - 1), total - largest - least * (count - 1)
    while surplus > 0:
        candidates = [i for i in range(1, count) if holding[i] < largest] or [i for i in range(1, count) if holding[i] < most]
        pool, budget = sum([loads[i] for i in candidates]), surplus
        for i in candidates:
            addition = min(most - holding[i], max(1, budget * loads[i] // pool), surplus)
            holding[i] = holding[i] + addition
            surplus = surplus - addition
    return np.array(holding)


def bell_draw(key, extent, width, reach, cuts=(), held_as=jnp.bfloat16):
    drawn = jax.random.normal(key, extent, jnp.float32) * width
    if len(cuts) > 0:
        drawn = levels(key, extent, cuts, -0.22, 0.18) * drawn
    return jnp.clip(drawn, min=-reach, max=reach).astype(held_as)


def setup_inputs(seed: int = 0) -> dict:
    key_of = jax.random.split(jax.random.key(seed), 18)
    tokens = bell_draw(key_of[0], (TOKENS, D), 1.0, 6.0, ((0, 32),))
    cotangent = bell_draw(key_of[1], (TOKENS, D), 1.0, 6.0, ((0, 32),))
    attn_gain = jnp.clip(1.0 + 0.1 * jax.random.normal(key_of[2], (D,), jnp.float32), 0.5, 1.5)
    w_query = bell_draw(key_of[3], (D, HEADS * (NOPE + ROPE)), D ** -0.5, 0.125, ((1, 4),))
    w_latent = bell_draw(key_of[4], (D, KV_RANK + ROPE), D ** -0.5, 0.125)
    latent_gain = jnp.clip(1.0 + 0.1 * jax.random.normal(key_of[5], (KV_RANK,), jnp.float32), 0.5, 1.5)
    w_keyvalue = bell_draw(key_of[6], (KV_RANK, HEADS * (NOPE + VDIM)), KV_RANK ** -0.5, 0.25, ((1, 4),))
    w_output = bell_draw(key_of[7], (HEADS * VDIM, D), (max(HEADS * VDIM * 8 // TOK_DEV, 1)) ** -0.5, 0.75, ((0, 4),))
    ffn_gain = jnp.clip(1.0 + 0.1 * jax.random.normal(key_of[8], (D,), jnp.float32), 0.5, 1.5)
    w_router = bell_draw(key_of[9], (D, EXPERTS), (4 * D) ** -0.5, 0.0625)
    shared_gate = bell_draw(key_of[10], (D, SHARED_FF), D ** -0.5, 0.125, ((1, 4),))
    shared_up = bell_draw(key_of[11], (D, SHARED_FF), D ** -0.5, 0.125, ((1, 4),))
    shared_down = bell_draw(key_of[12], (SHARED_FF, D), SHARED_FF ** -0.5, 0.109375, ((0, 4),))
    expert_gate = bell_draw(key_of[13], (EXPERTS, D, EFF), D ** -0.5, 0.125, ((0, 32), (2, 4)))
    expert_up = bell_draw(key_of[14], (EXPERTS, D, EFF), D ** -0.5, 0.125, ((0, 32), (2, 4)))
    expert_down = bell_draw(key_of[15], (EXPERTS, EFF, D), EFF ** -0.5, 0.15625, ((0, 32), (1, 4)))
    routes_keys = jax.random.split(jax.random.fold_in(key_of[16], 1), TOKENS // TOK_DEV)
    routes_turns = jax.random.permutation(jax.random.fold_in(key_of[16], 3), TOKENS // TOK_DEV)
    routes = jax.vmap(lambda own, number: routed_block(jax.random.fold_in(key_of[16], 2), own, number, TOK_DEV, EXPERTS, TOP, CAP, 1))(routes_keys, routes_turns).reshape((TOKENS, TOP))
    return {"tokens": tokens, "cotangent": cotangent, "attn_gain": attn_gain, "w_query": w_query, "w_latent": w_latent, "latent_gain": latent_gain, "w_keyvalue": w_keyvalue, "w_output": w_output, "ffn_gain": ffn_gain, "w_router": w_router, "shared_gate": shared_gate, "shared_up": shared_up, "shared_down": shared_down, "expert_gate": expert_gate, "expert_up": expert_up, "expert_down": expert_down, "routes": routes}


EPS = 1e-06
THETA = 50000.0
ROUTE_SCALE = 2.446
MASKED = -1e+30

@jax.custom_vjp
def low(v):
    return lax.optimization_barrier(v.astype(jnp.bfloat16)).astype(jnp.float32)

@jax.custom_vjp
def low_back(v):
    return v

def low_keep(v):
    return (low(v), None)

def low_pass(kept, grad):
    return (grad,)

def back_keep(v):
    return (v, None)

def back_low(kept, grad):
    return (low(grad),)
low.defvjp(low_keep, low_pass)
low_back.defvjp(back_keep, back_low)

def rms_scale(values):
    return lax.rsqrt(lax.optimization_barrier(jnp.mean(values * values, axis=-1, keepdims=True)) + EPS)

def rotary_tables(position, table_width):
    frequency = THETA ** (-2.0 * jnp.arange(table_width // 2, dtype=jnp.float32) / table_width)
    angles = position[:, None] * frequency[None, :]
    return (jnp.cos(angles), jnp.sin(angles))

def rotary(values, cosine_table, sine_table):
    half_width = values.shape[-1] // 2
    former = values[..., :half_width]
    latter = values[..., half_width:]
    return jnp.concatenate([former * cosine_table - latter * sine_table, latter * cosine_table + former * sine_table], axis=-1)

def expert_block(padded, picked, gate_mat, up_mat, down_mat):
    highest = lax.Precision.HIGHEST
    row_block = padded[picked // TOP]
    hidden_span = EFF // N_TENSOR
    running = jnp.zeros((picked.shape[0], D), jnp.float32)
    for quarter in range(N_TENSOR):
        lower_col = quarter * hidden_span
        row_copy = low_back(row_block)
        gate_pre = low_back(jnp.dot(row_copy, gate_mat[:, lower_col:lower_col + hidden_span], precision=highest))
        up_pre = low_back(jnp.dot(row_copy, up_mat[:, lower_col:lower_col + hidden_span], precision=highest))
        active = low(jax.nn.silu(gate_pre) * up_pre)
        running = running + low(low_back(jnp.dot(active, down_mat[lower_col:lower_col + hidden_span], precision=highest)))
    return running

def layer(tokens, attn_gain, w_query, w_latent, latent_gain, w_keyvalue, w_output, ffn_gain, w_router, shared_gate, shared_up, shared_down, expert_gate, expert_up, expert_down, routes, picked):
    highest = lax.Precision.HIGHEST
    qk_width = NOPE + ROPE
    position = (jnp.arange(TOKENS) % TOK_DEV).astype(jnp.float32)
    cosine_table, sine_table = rotary_tables(position, ROPE)
    scale_one = rms_scale(tokens)
    normed = low(tokens * scale_one * attn_gain)
    query_pre = low_back(jnp.dot(normed, w_query, precision=highest)).reshape(TOKENS, HEADS, qk_width)
    query_full = jnp.concatenate([query_pre[..., :NOPE], rotary(query_pre[..., NOPE:], cosine_table[:, None, :], sine_table[:, None, :])], axis=-1)
    query_low = low(low_back(query_full))
    latent = low_back(jnp.dot(normed, w_latent, precision=highest))
    compressed = latent[:, :KV_RANK]
    key_rope = rotary(latent[:, KV_RANK:], cosine_table, sine_table)
    latent_normed = low(compressed * rms_scale(compressed) * latent_gain)
    keyvalue = jnp.dot(latent_normed, w_keyvalue, precision=highest).reshape(TOKENS, HEADS, NOPE + VDIM)
    key_full = jnp.concatenate([keyvalue[..., :NOPE], jnp.broadcast_to(key_rope[:, None, :], (TOKENS, HEADS, ROPE))], axis=-1)
    key_low = low(low_back(key_full))
    value_low = low(low_back(keyvalue[..., NOPE:]))
    seq_shape = (N_EXPERT, TOK_DEV, HEADS)
    raw_scores = jnp.einsum('bthd,bshd->bhts', query_low.reshape(seq_shape + (qk_width,)), key_low.reshape(seq_shape + (qk_width,)), precision=highest)
    scores = low_back(raw_scores * qk_width ** (-0.5))
    causal = jnp.arange(TOK_DEV)[:, None] >= jnp.arange(TOK_DEV)[None, :]
    scores = jnp.where(causal, scores, MASKED)
    largest = lax.optimization_barrier(jnp.max(scores, axis=-1, keepdims=True))
    exp_terms = jnp.exp(scores - largest)
    attn_weights = low(exp_terms / lax.optimization_barrier(jnp.sum(exp_terms, axis=-1, keepdims=True)))
    attn_mixed = jnp.einsum('bhts,bshd->bthd', attn_weights, value_low.reshape(seq_shape + (VDIM,)), precision=highest)
    attn_mixed = low(low_back(attn_mixed)).reshape(TOKENS, HEADS * VDIM)
    hidden = tokens + low_back(jnp.dot(attn_mixed, w_output, precision=highest))
    scale_two = rms_scale(hidden)
    normed_two = low(hidden * scale_two * ffn_gain)
    logits = low_back(jnp.dot(normed_two, w_router, precision=highest))
    chosen = jnp.take_along_axis(logits, routes, axis=1)
    sigmas = jax.nn.sigmoid(chosen)
    gate_weights = ROUTE_SCALE * sigmas / lax.optimization_barrier(jnp.sum(sigmas, axis=-1, keepdims=True))
    shared_gate_pre = low_back(jnp.dot(normed_two, shared_gate, precision=highest))
    shared_up_pre = low_back(jnp.dot(normed_two, shared_up, precision=highest))
    shared_act = low(jax.nn.silu(shared_gate_pre) * shared_up_pre)
    shared_out = low_back(jnp.dot(shared_act, shared_down, precision=highest))
    padded = jnp.concatenate([normed_two, jnp.zeros((1, D), jnp.float32)], axis=0)
    block_fn = jax.checkpoint(partial(expert_block, padded))

    def run_expert(expert_item):
        return block_fn(expert_item[0], expert_item[1], expert_item[2], expert_item[3])
    produced = lax.map(run_expert, (picked, expert_gate, expert_up, expert_down))
    flat_count = TOKENS * TOP
    scattered = jnp.zeros((flat_count + 1, D), jnp.float32).at[picked.reshape(-1)].add(produced.reshape(-1, D))
    expert_out = scattered[:flat_count].reshape(TOKENS, TOP, D)
    routed = lax.optimization_barrier(jnp.sum(gate_weights[:, :, None] * expert_out, axis=1))
    return hidden + shared_out + routed

def reference(tokens, cotangent, attn_gain, w_query, w_latent, latent_gain, w_keyvalue, w_output, ffn_gain, w_router, shared_gate, shared_up, shared_down, expert_gate, expert_up, expert_down, routes):
    flat_routes = routes.reshape(-1)

    def locate(expert_id):
        found = jnp.nonzero(flat_routes == expert_id, size=N_EXPERT * CAP, fill_value=TOKENS * TOP)[0]
        return found.astype(jnp.int32)
    picked = lax.map(locate, jnp.arange(EXPERTS, dtype=jnp.int32))
    primals = tuple((array.astype(jnp.float32) for array in (tokens, attn_gain, w_query, w_latent, latent_gain, w_keyvalue, w_output, ffn_gain, w_router, shared_gate, shared_up, shared_down, expert_gate, expert_up, expert_down)))

    def forward(*inputs):
        return layer(*inputs, routes, picked)
    result, pullback = jax.vjp(forward, *primals)
    grads = pullback(cotangent.astype(jnp.float32))
    return (result.astype(jnp.bfloat16), grads[0].astype(jnp.bfloat16), grads[1], grads[2], grads[3], grads[4], grads[5], grads[6], grads[7], grads[8], grads[9], grads[10], grads[11], grads[12], grads[13], grads[14])
```

```python
import functools
import math

import jax
import jax.numpy as jnp
import numpy as np
from jax import lax
from jax.experimental import pallas as pl
from jax.experimental.pallas import tpu as pltpu
from jax.sharding import PartitionSpec as P

NOPE = 128
ROPE = 64
VDIM = 128
KV_RANK = 512


EPS = 1e-06
THETA = 50000.0
ROUTE_SCALE = 2.446
MASKED = -1e30
LANES = 128


def rms_scale(values):
    return lax.rsqrt(jnp.mean(values * values, axis=-1, keepdims=True) + EPS)


def unrotary(grads_in, cosine_table, sine_table):
    half_width = grads_in.shape[-1] // 2
    former = grads_in[..., :half_width]
    latter = grads_in[..., half_width:]
    return jnp.concatenate(
        [former * cosine_table + latter * sine_table, latter * cosine_table - former * sine_table],
        axis=-1,
    )


def silu_back(grad_act, gate_pre, up_pre):
    sigma_gate = jax.nn.sigmoid(gate_pre)
    grad_up = grad_act * gate_pre * sigma_gate
    grad_gate = grad_act * up_pre * sigma_gate * (1.0 + gate_pre * (1.0 - sigma_gate))
    return (grad_gate.astype(jnp.bfloat16), grad_up.astype(jnp.bfloat16))


def matmul(left_side, right_side):
    return jnp.dot(left_side, right_side, preferred_element_type=jnp.float32)


def matmul_tn(left_side, right_side):
    return lax.dot_general(
        left_side, right_side, (((0,), (0,)), ((), ())), preferred_element_type=jnp.float32
    )


def matmul_nt(left_side, right_side):
    return lax.dot_general(
        left_side, right_side, (((1,), (1,)), ((), ())), preferred_element_type=jnp.float32
    )


def two_parts(values):
    high = lax.reduce_precision(values, 8, 7)
    return (high.astype(jnp.bfloat16), (values - high).astype(jnp.bfloat16))


def after(value, *others):
    return lax.optimization_barrier((value,) + others)[0]


def shift_ranks(values, step, count):
    return lax.ppermute(values, "tensor", [(i, (i + step) % count) for i in range(count)])


def column_block(values, index, width):
    return lax.dynamic_slice_in_dim(values, index * width, width, axis=1)


def gather_columns(block, rank, count, width):
    pieces = [block] + [shift_ranks(block, step, count) for step in range(1, count)]
    ordered = [
        lax.select_n(lax.rem(rank - place + count, count), *[p[:, :width] for p in pieces])
        for place in range(count)
    ]
    return (jnp.concatenate(ordered, axis=1), [p[:, width:] for p in pieces])


def expert_rows_kernel(sideways, first_ref, x_ref, gate_ref, g_ref, wgu_ref, wgut_ref, wd_ref, wdt_ref,
                       *rest):
    produced_ref, rowgrad_ref, dgu_ref, actw_ref = rest[-4:]
    quarters, step, cap, part = g_ref.shape
    rows = step * cap
    width, model = wd_ref.shape
    half = LANES // 2
    expert = first_ref[0]
    column = lax.broadcasted_iota(jnp.int32, (rows, LANES), 1)
    chosen = (column == expert) | (column == expert + half)
    gates = gate_ref[...].reshape(rows, LANES).astype(jnp.float32)
    weight = jnp.sum(jnp.where(chosen, gates, 0.0), axis=1, keepdims=True)

    def by_quarters(values_ref, matrix_ref):
        total = matmul(values_ref[0].reshape(rows, part), matrix_ref[:part, :])
        for place in range(1, quarters):
            total += matmul(
                values_ref[place].reshape(rows, part),
                matrix_ref[place * part:(place + 1) * part, :],
            )
        return total

    pre = matmul(x_ref[...].reshape(rows, model), wgu_ref[...])
    grad_act = by_quarters(g_ref, wdt_ref)
    gate_pre = pre[:, :width]
    up_pre = pre[:, width:]
    sigma = 1.0 / (1.0 + jnp.exp(-gate_pre))
    silu = gate_pre * sigma
    act = silu * up_pre
    act_weighted = (act * weight).astype(jnp.bfloat16)
    actw_ref[...] = act_weighted
    for place in range(quarters):
        out = matmul(act_weighted, wd_ref[:, place * part:(place + 1) * part])
        produced_ref[place] = out.astype(jnp.bfloat16).reshape(step, cap, part)
    dot = jnp.sum(grad_act * act, axis=1, keepdims=True)
    grad_act = grad_act * weight
    grad_up = grad_act * silu
    grad_gate = grad_act * up_pre * (sigma + silu * (1.0 - sigma))
    row_dot = jnp.sum(grad_gate * gate_pre + grad_up * up_pre, axis=1, keepdims=True)
    row_dot_high = row_dot.astype(jnp.bfloat16).astype(jnp.float32)
    pre_grad = jnp.concatenate([grad_gate, grad_up], axis=1).astype(jnp.bfloat16)
    dgu_ref[...] = pre_grad
    row_grad = matmul(pre_grad, wgut_ref[...]).astype(jnp.bfloat16)
    sums = jnp.where(column == expert, dot, 0.0)
    sums = jnp.where(column == half, row_dot_high, sums)
    sums = jnp.where(column == half + 1, row_dot - row_dot_high, sums)
    sums = sums.astype(jnp.bfloat16).reshape(step, cap, LANES)
    if sideways:
        for place in range(quarters):
            rowgrad_ref[place, :, :, :part] = (
                row_grad[:, place * part:(place + 1) * part].reshape(step, cap, part)
            )
            rowgrad_ref[place, :, :, part:] = sums
    else:
        rowgrad_ref[:, :, :model] = row_grad.reshape(step, cap, model)
        rowgrad_ref[:, :, model:] = sums


def expert_rows(number, first, x, g, weights, sideways, produced=None):
    quarters, sources, experts, cap, part = g.shape
    wgu, wgut, wd, wdt = weights
    width, model = wd.shape[1:]
    step = 16
    rows = step * cap
    total = sources * cap

    def flat_block(columns):
        return pl.BlockSpec((rows, columns), lambda b, f: (b, 0))

    def whole(*shape):
        return pl.BlockSpec((None,) + shape, lambda b, f: (number, 0, 0))

    def kind(*shape):
        return jax.ShapeDtypeStruct(shape, jnp.bfloat16)

    def part_block(columns):
        return pl.BlockSpec((quarters, step, cap, columns), lambda b, f: (0, b, 0, 0))

    def row_block(columns):
        return pl.BlockSpec((step, cap, columns), lambda b, f: (b, 0, 0))

    expert_part = pl.BlockSpec(
        (quarters, step, None, cap, part), lambda b, f: (0, b, number, 0, 0)
    )
    last = model // LANES
    in_specs = [
        pl.BlockSpec((step, None, cap, model), lambda b, f: (b, number, 0, 0)),
        pl.BlockSpec((step, None, cap, LANES), lambda b, f: (b, number, 0, last)), expert_part,
        whole(model, 2 * width), whole(2 * width, model), whole(width, model), whole(model, width),
    ]
    inputs = ()
    aliases = {}
    if produced is not None:
        inputs = (produced,)
        in_specs.append(pl.BlockSpec(memory_space=pl.ANY))
        aliases = {len(in_specs): 0}
    return pl.pallas_call(
        functools.partial(expert_rows_kernel, sideways),
        grid_spec=pltpu.PrefetchScalarGridSpec(
            num_scalar_prefetch=1,
            grid=(sources // step,),
            in_specs=in_specs,
            out_specs=[
                expert_part, part_block(part + LANES) if sideways else row_block(model + LANES),
                flat_block(2 * width), flat_block(width),
            ],
        ),
        out_shape=[
            kind(*g.shape),
            kind(quarters, sources, cap, part + LANES) if sideways
            else kind(sources, cap, model + LANES),
            kind(total, 2 * width), kind(total, width),
        ],
        compiler_params=pltpu.CompilerParams(vmem_limit_bytes=60 * 1024 * 1024),
        cost_estimate=pl.CostEstimate(
            flops=2 * total * model * width * 6, bytes_accessed=30_000_000,
            transcendentals=total * width,
        ),
        input_output_aliases=aliases,
        name=f"expert_rows_{number}",
    )(first + number, x, x, g, wgu, wgut, wd, wdt, *inputs)


def expert_weights_kernel(x_ref, g_ref, dgu_ref, actw_ref, *rest):
    gate_ref, up_ref, down_ref = rest[-3:]
    rows, width = actw_ref.shape
    hidden = gate_ref.shape[0]
    grad = matmul_tn(dgu_ref[...], x_ref[...].reshape(rows, x_ref.shape[-1]))
    gate_ref[...] = grad[:hidden, :]
    up_ref[...] = grad[width:width + hidden, :]
    g_rows = g_ref[...].reshape(rows, g_ref.shape[-1])
    down_ref[...] = matmul_tn(actw_ref[...], g_rows)[:hidden, :]


def expert_weights(number, x, g, dgu, actw, hidden, before=()):
    quarters, sources, experts, cap, quarter = g.shape
    model = quarters * quarter
    total, width = actw.shape
    steps = 8
    part = model // steps
    per = steps // quarters
    x_block = pl.BlockSpec((sources, None, cap, part), lambda b: (0, number, 0, b))
    in_specs = [
        x_block,
        pl.BlockSpec((None, sources, None, cap, part),
                     lambda b: (b // per, 0, number, 0, b % per)),
        pl.BlockSpec((total, 2 * width), lambda b: (0, 0)),
        pl.BlockSpec((total, width), lambda b: (0, 0)),
    ] + [pl.BlockSpec(memory_space=pl.ANY)] * len(before)
    return pl.pallas_call(
        expert_weights_kernel,
        grid=(steps,),
        in_specs=in_specs,
        out_specs=[pl.BlockSpec((None, hidden, part), lambda b: (number, 0, b))] * 3,
        out_shape=[jax.ShapeDtypeStruct((experts, hidden, model), jnp.float32)] * 3,
        compiler_params=pltpu.CompilerParams(vmem_limit_bytes=56 * 1024 * 1024),
        cost_estimate=pl.CostEstimate(
            flops=2 * total * model * width * 3, bytes_accessed=22_000_000, transcendentals=0
        ),
        input_output_aliases={4 + place: place for place in range(len(before))},
        name=f"expert_weights_{number}",
    )(x, g, dgu, actw, *before)


def shared_weights_kernel(n_ref, c_ref, gate_ref, up_ref, act_ref, out_ref):
    chunk = out_ref.shape[1] // 3
    for place, (rows, grads) in enumerate(
        ((n_ref, gate_ref), (n_ref, up_ref), (c_ref, act_ref))
    ):
        grad = matmul_tn(rows[...], grads[...]).astype(jnp.bfloat16)
        for group in range(out_ref.shape[0]):
            out_ref[group, place * chunk:(place + 1) * chunk, :] = (
                grad[group * chunk:(group + 1) * chunk, :]
            )


def shared_weights(normed, cotangent, gate_grad, up_grad, act, groups):
    tokens, model = normed.shape
    width = gate_grad.shape[1]
    block = 256
    chunk = model // groups
    per = block // chunk
    rows = pl.BlockSpec((tokens, block), lambda i: (0, i))
    grads = pl.BlockSpec((tokens, width), lambda i: (0, 0))
    return pl.pallas_call(
        shared_weights_kernel,
        grid=(model // block,),
        in_specs=[rows, rows, grads, grads, grads],
        out_specs=pl.BlockSpec((per, 3 * chunk, width), lambda i: (i, 0, 0)),
        out_shape=jax.ShapeDtypeStruct((groups, 3 * chunk, width), jnp.bfloat16),
        compiler_params=pltpu.CompilerParams(vmem_limit_bytes=48 * 1024 * 1024),
        cost_estimate=pl.CostEstimate(
            flops=6 * tokens * model * width, bytes_accessed=14_000_000, transcendentals=0
        ),
        name="shared_weights",
    )(normed, cotangent, gate_grad, up_grad, act)


def combine_kernel(rank_ref, pick_ref, back_ref, sums_ref, shared_ref, dots_ref,
                   own_ref, extra_ref, *sends):
    step = pl.program_id(0)
    count = pl.num_programs(0)
    place = lax.rem(step - rank_ref[0] + count, count)
    part = own_ref.shape[1]
    value = matmul(pick_ref[...], back_ref[...]) + shared_ref[...]

    @pl.when(place == 0)
    def _():
        own_ref[...] = value

    for number, send in enumerate(sends):
        @pl.when(place == number + 1)
        def _():
            send[:, :part] = value.astype(jnp.bfloat16)

    @pl.when(step == count - 1)
    def _():
        mark = LANES // 2
        sums = matmul(pick_ref[...], sums_ref[...])
        column = lax.broadcasted_iota(jnp.int32, sums.shape, 1)
        mean = dots_ref[...] + jnp.sum(
            jnp.where((column == mark) | (column == mark + 1), sums, 0.0), axis=1, keepdims=True
        )
        mean_high = mean.astype(jnp.bfloat16).astype(jnp.float32)
        extra = jnp.where(column < mark, sums, 0.0)
        extra = jnp.where(column == mark, mean_high, extra)
        extra = jnp.where(column == mark + 1, mean - mean_high, extra).astype(jnp.bfloat16)
        extra_ref[...] = extra
        for send in sends:
            send[:, part:] = extra


def combine_rows(rank, pick, back, shared, dots, count):
    tokens, slots = pick.shape
    model = shared.shape[1]
    part = model // count
    sent = jax.ShapeDtypeStruct((tokens, part + LANES), jnp.bfloat16)
    sent_block = pl.BlockSpec((tokens, part + LANES), lambda i, r: (0, 0))
    return pl.pallas_call(
        combine_kernel,
        grid_spec=pltpu.PrefetchScalarGridSpec(
            num_scalar_prefetch=1,
            grid=(count,),
            in_specs=[
                pl.BlockSpec((tokens, slots), lambda i, r: (0, 0)),
                pl.BlockSpec((slots, part), lambda i, r: (0, i)),
                pl.BlockSpec((slots, LANES), lambda i, r: (0, model // LANES)),
                pl.BlockSpec((tokens, part), lambda i, r: (0, i)),
                pl.BlockSpec((tokens, 1), lambda i, r: (0, 0)),
            ],
            out_specs=[
                pl.BlockSpec((tokens, part), lambda i, r: (0, 0)),
                pl.BlockSpec((tokens, LANES), lambda i, r: (0, 0)),
            ] + [sent_block] * (count - 1),
        ),
        out_shape=[
            jax.ShapeDtypeStruct((tokens, part), jnp.float32),
            jax.ShapeDtypeStruct((tokens, LANES), jnp.bfloat16),
        ] + [sent] * (count - 1),
        compiler_params=pltpu.CompilerParams(vmem_limit_bytes=48 * 1024 * 1024),
        cost_estimate=pl.CostEstimate(
            flops=2 * tokens * slots * model, bytes_accessed=9_000_000, transcendentals=0
        ),
        name="combine_rows",
    )(rank.reshape(1), pick, back, back, shared, dots)


def attention_forward_kernel(rank_ref, token_ref, gain_ref, latent_gain_ref, cosine_ref, ahead_ref,
                             behind_ref, key_cosine_ref, key_sine_ref, w_latent_ref, w_query_ref,
                             w_keyvalue_ref, w_output_ref,
                             normed_ref, scale_ref, query_ref, query_low_ref, latent_ref,
                             latent_normed_ref, keyvalue_ref, key_rope_ref, weights_ref, mixed_ref,
                             own_ref, *rest):
    *sends, latent_buf, query_buf, keyvalue_buf, output_buf, sems = rest
    copies = [
        pltpu.make_async_copy(source, buffer, sems.at[number])
        for number, (source, buffer) in enumerate((
            (w_latent_ref, latent_buf), (w_query_ref, query_buf), (w_keyvalue_ref, keyvalue_buf),
            (w_output_ref, output_buf),
        ))
    ]
    for copy in copies:
        copy.start()
    tokens = token_ref[...].astype(jnp.float32)
    scale = lax.rsqrt(jnp.mean(tokens * tokens, axis=1, keepdims=True) + EPS)
    scale_ref[...] = scale
    normed = (tokens * scale * gain_ref[...]).astype(jnp.bfloat16)
    normed_ref[...] = normed
    copies[0].wait()
    latent = matmul_nt(normed, latent_buf[...])
    latent_ref[...] = latent
    compressed = latent[:, :KV_RANK]
    latent_scale = lax.rsqrt(jnp.mean(compressed * compressed, axis=1, keepdims=True) + EPS)
    latent_normed = (compressed * latent_scale * latent_gain_ref[...]).astype(jnp.bfloat16)
    latent_normed_ref[...] = latent_normed
    half = ROPE // 2
    former = latent[:, KV_RANK:KV_RANK + half]
    latter = latent[:, KV_RANK + half:]
    key_cosine, key_sine = key_cosine_ref[...], key_sine_ref[...]
    key_rope = jnp.concatenate(
        [former * key_cosine - latter * key_sine, latter * key_cosine + former * key_sine], axis=1
    ).astype(jnp.bfloat16)
    key_rope_ref[...] = key_rope
    copies[1].wait()
    query = matmul(normed, query_buf[...])
    query_ref[...] = query
    wide = query.shape[1]
    query_low_ref[...] = (
        query * cosine_ref[...] + pltpu.roll(query, wide - half, 1) * ahead_ref[...]
        + pltpu.roll(query, half, 1) * behind_ref[...]
    ).astype(jnp.bfloat16)
    copies[2].wait()
    keyvalue_ref[...] = matmul(latent_normed, keyvalue_buf[...]).astype(jnp.bfloat16)
    rows = tokens.shape[0]
    causal = (
        lax.broadcasted_iota(jnp.int32, (rows, rows), 0)
        >= lax.broadcasted_iota(jnp.int32, (rows, rows), 1)
    )
    qk_width = NOPE + ROPE
    for head in range(wide // qk_width):
        low = head * (NOPE + VDIM)
        query_head = query_low_ref[:, head * qk_width:(head + 1) * qk_width]
        key_head = jnp.concatenate([keyvalue_ref[:, low:low + NOPE], key_rope], axis=1)
        scores = matmul_nt(query_head, key_head) * (qk_width ** -0.5)
        scores = jnp.where(causal, scores, MASKED)
        terms = jnp.exp(scores - jnp.max(scores, axis=1, keepdims=True))
        weights = terms / jnp.sum(terms, axis=1, keepdims=True)
        weights_ref[head] = weights
        mixed_ref[:, head * VDIM:(head + 1) * VDIM] = matmul(
            weights.astype(jnp.bfloat16), keyvalue_ref[:, low + NOPE:low + NOPE + VDIM]
        ).astype(jnp.bfloat16)
    copies[3].wait()
    part = own_ref.shape[1]
    count = len(sends) + 1
    for number in range(count):
        value = matmul(mixed_ref[...], output_buf[:, number * part:(number + 1) * part])
        place = lax.rem(number - rank_ref[0] + count, count)

        @pl.when(place == 0)
        def _():
            own_ref[...] = value

        for index, send in enumerate(sends):
            @pl.when(place == index + 1)
            def _():
                send[...] = value.astype(jnp.bfloat16)


def rotary_constants(rows, heads):
    half = ROPE // 2
    frequency = np.float32(THETA) ** (np.arange(half, dtype=np.float32) * np.float32(-2.0 / ROPE))
    angles = np.arange(rows, dtype=np.float32)[:, None] * frequency[None, :]
    cosine, sine = np.cos(angles), np.sin(angles)
    blank = np.zeros((rows, NOPE), np.float32)
    zero = np.zeros((rows, half), np.float32)

    def tiled(*pieces):
        return np.tile(np.concatenate(pieces, axis=1), (1, heads)).astype(np.float32)

    return (
        tiled(blank + 1.0, cosine, cosine), tiled(blank, -sine, zero), tiled(blank, zero, sine),
        cosine, sine,
    )


def full_specs(arrays):
    return [pl.BlockSpec(a.shape, lambda i, r, n=len(a.shape): (0,) * n) for a in arrays]


def attention_forward(rank, tokens, gain, latent_gain, tables, w_latent, w_query, w_keyvalue, w_output,
                      count):
    rows, model = tokens.shape
    part = model // count
    latent_width = w_latent.shape[1]
    query_width = w_query.shape[1]
    heads = query_width // (NOPE + ROPE)
    bf16, f32 = jnp.bfloat16, jnp.float32
    out_shape = [
        jax.ShapeDtypeStruct(shape, kind)
        for shape, kind in (
            ((rows, model), bf16), ((rows, 1), f32), ((rows, query_width), f32),
            ((rows, query_width), bf16), ((rows, latent_width), f32), ((rows, KV_RANK), bf16),
            ((rows, w_keyvalue.shape[1]), bf16), ((rows, ROPE), bf16), ((heads, rows, rows), f32),
            ((rows, heads * VDIM), bf16), ((rows, part), f32),
        ) + (((rows, part), bf16),) * (count - 1)
    ]
    inputs = [tokens, gain.reshape(1, -1), latent_gain.reshape(1, -1), *tables]
    streamed = [w_latent.T, w_query, w_keyvalue, w_output]
    return pl.pallas_call(
        attention_forward_kernel,
        grid_spec=pltpu.PrefetchScalarGridSpec(
            num_scalar_prefetch=1,
            grid=(1,),
            in_specs=full_specs(inputs) + [pl.BlockSpec(memory_space=pl.ANY)] * len(streamed),
            out_specs=full_specs(out_shape),
            scratch_shapes=[pltpu.VMEM(a.shape, a.dtype) for a in streamed]
            + [pltpu.SemaphoreType.DMA((len(streamed),))],
        ),
        out_shape=out_shape,
        compiler_params=pltpu.CompilerParams(vmem_limit_bytes=48 * 1024 * 1024),
        cost_estimate=pl.CostEstimate(
            flops=5_000_000_000, bytes_accessed=16_000_000, transcendentals=300_000
        ),
        name="attention_forward",
    )(rank.reshape(1), *inputs, *streamed)


def attention_backward_kernel(rank_ref, *refs):
    count = 4
    pieces, refs = refs[:count], refs[count:]
    (weights_ref, keyvalue_ref, key_rope_ref, query_low_ref, query_ref, token_ref, scale_ref, cosine_ref,
     ahead_ref, behind_ref, w_output_ref, w_keyvalue_ref, w_query_ref,
     branch_ref, gain_ref, query_grad_ref, keyvalue_grad_ref, own_ref, latent_ref, *rest) = refs
    *sends, output_buf, keyvalue_buf, query_buf, grad_buf, sems = rest
    copies = [
        pltpu.make_async_copy(source, buffer, sems.at[number])
        for number, (source, buffer) in enumerate((
            (w_output_ref, output_buf), (w_keyvalue_ref, keyvalue_buf), (w_query_ref, query_buf),
        ))
    ]
    for copy in copies:
        copy.start()
    rows, model = branch_ref.shape
    part = own_ref.shape[1]
    for place in range(count):
        columns = slice(place * part, (place + 1) * part)
        turn = lax.rem(rank_ref[0] - place + count, count)
        for number, piece in enumerate(pieces):
            @pl.when(turn == number)
            def _():
                branch_ref[:, columns] = piece[:rows, :]
                sums = piece[rows:, :].astype(jnp.float32)
                gain_ref[:, columns] = sums[0:1] + sums[1:2]
    copies[0].wait()
    mixed_grad = matmul_nt(branch_ref[...], output_buf[...]).astype(jnp.bfloat16)
    qk_width = NOPE + ROPE
    soft = qk_width ** -0.5
    key_rope = key_rope_ref[...]
    rope_grad = jnp.zeros((rows, ROPE), jnp.float32)
    for head in range(weights_ref.shape[0]):
        low = head * (NOPE + VDIM)
        columns = slice(head * qk_width, (head + 1) * qk_width)
        weights = weights_ref[head]
        out_grad = mixed_grad[:, head * VDIM:(head + 1) * VDIM]
        keyvalue_grad_ref[:, low + NOPE:low + NOPE + VDIM] = matmul_tn(
            weights.astype(jnp.bfloat16), out_grad
        ).astype(jnp.bfloat16)
        prob_grad = matmul_nt(out_grad, keyvalue_ref[:, low + NOPE:low + NOPE + VDIM])
        row_term = jnp.sum(weights * prob_grad, axis=1, keepdims=True)
        score_grad = (weights * (prob_grad - row_term)).astype(jnp.bfloat16)
        key_head = jnp.concatenate([keyvalue_ref[:, low:low + NOPE], key_rope], axis=1)
        grad_buf[:, columns] = matmul(score_grad, key_head) * soft
        key_grad = matmul_tn(score_grad, query_low_ref[:, columns]) * soft
        keyvalue_grad_ref[:, low:low + NOPE] = key_grad[:, :NOPE].astype(jnp.bfloat16)
        rope_grad += key_grad[:, NOPE:]
    grad = grad_buf[...]
    wide = grad.shape[1]
    half = ROPE // 2
    query_grad = (
        grad * cosine_ref[...] - pltpu.roll(grad, wide - half, 1) * ahead_ref[...]
        - pltpu.roll(grad, half, 1) * behind_ref[...]
    ).astype(jnp.bfloat16)
    query_grad_ref[...] = query_grad
    mean = jnp.sum(query_grad.astype(jnp.float32) * query_ref[...], axis=1, keepdims=True)
    mean_high = mean.astype(jnp.bfloat16).astype(jnp.float32)
    copies[1].wait()
    latent_part = matmul_nt(keyvalue_grad_ref[...], keyvalue_buf[...])
    width = latent_part.shape[1]
    column = lax.broadcasted_iota(jnp.int32, (rows, LANES - ROPE), 1)
    sums = jnp.where(column == 0, mean_high, jnp.where(column == 1, mean - mean_high, 0.0))
    latent_ref[:rows, :width] = latent_part.astype(jnp.bfloat16)
    latent_ref[:rows, width:] = jnp.concatenate([rope_grad, sums], axis=1).astype(jnp.bfloat16)
    copies[2].wait()
    gains = []
    scale = scale_ref[...]
    for number in range(count):
        columns = slice(number * part, (number + 1) * part)
        value = matmul_nt(query_grad, query_buf[columns, :])
        unit = token_ref[:, columns].astype(jnp.float32) * scale
        gains.append(jnp.sum(value * unit, axis=0, keepdims=True))
        place = lax.rem(number - rank_ref[0] + count, count)

        @pl.when(place == 0)
        def _():
            own_ref[...] = value

        for index, send in enumerate(sends):
            @pl.when(place == index + 1)
            def _():
                send[:rows, width + LANES:] = value.astype(jnp.bfloat16)
    highs = [gain.astype(jnp.bfloat16).astype(jnp.float32) for gain in gains]
    lows = [gain - high for gain, high in zip(gains, highs)]
    spare = latent_ref.shape[0] - rows
    latent_ref[rows:, :width] = jnp.concatenate(
        highs + lows + [jnp.zeros((spare - 2 * count, part), jnp.float32)], axis=0
    ).astype(jnp.bfloat16)
    latent_ref[rows:, width:] = jnp.zeros((spare, LANES), jnp.bfloat16)
    for send in sends:
        send[:, :width + LANES] = latent_ref[...]
        send[rows:, width + LANES:] = jnp.zeros((spare, part), jnp.bfloat16)


def attention_backward(rank, pieces, weights, keyvalue, key_rope, query_low, query, tokens, scale, tables,
                       w_output, w_keyvalue, w_query):
    rows, model = tokens.shape
    count = len(pieces)
    part = model // count
    wide = query.shape[1]
    kv_width = keyvalue.shape[1]
    sent_rows = pieces[0].shape[0]
    bf16, f32 = jnp.bfloat16, jnp.float32
    sent_width = KV_RANK + LANES
    out_shape = [
        jax.ShapeDtypeStruct(shape, kind)
        for shape, kind in (
            ((rows, model), bf16), ((1, model), f32), ((rows, wide), bf16), ((rows, kv_width), bf16),
            ((rows, part), f32), ((sent_rows, sent_width), bf16),
        ) + (((sent_rows, sent_width + part), bf16),) * (count - 1)
    ]
    inputs = [*pieces, weights, keyvalue, key_rope, query_low, query, tokens, scale, *tables[:3]]
    streamed = [w_output, w_keyvalue, w_query]
    return pl.pallas_call(
        attention_backward_kernel,
        grid_spec=pltpu.PrefetchScalarGridSpec(
            num_scalar_prefetch=1,
            grid=(1,),
            in_specs=full_specs(inputs) + [pl.BlockSpec(memory_space=pl.ANY)] * len(streamed),
            out_specs=full_specs(out_shape),
            scratch_shapes=[pltpu.VMEM(a.shape, a.dtype) for a in streamed]
            + [pltpu.VMEM((rows, wide), f32), pltpu.SemaphoreType.DMA((len(streamed),))],
        ),
        out_shape=out_shape,
        compiler_params=pltpu.CompilerParams(vmem_limit_bytes=48 * 1024 * 1024),
        cost_estimate=pl.CostEstimate(
            flops=4_000_000_000, bytes_accessed=20_000_000, transcendentals=0
        ),
        name="attention_backward",
    )(rank.reshape(1), *inputs, *streamed)


def hidden_kernel(own_ref, token_ref, *rest):
    *pieces, hidden_ref, sent_ref = rest
    value = own_ref[...] + token_ref[...].astype(jnp.float32)
    for piece in pieces:
        value = value + piece[...].astype(jnp.float32)
    hidden_ref[...] = value
    part = value.shape[1]
    total = jnp.sum(value * value, axis=1, keepdims=True)
    high = total.astype(jnp.bfloat16).astype(jnp.float32)
    column = lax.broadcasted_iota(jnp.int32, (value.shape[0], LANES), 1)
    sums = jnp.where(column == 0, high, jnp.where(column == 1, total - high, 0.0))
    sent_ref[:, :part] = value.astype(jnp.bfloat16)
    sent_ref[:, part:] = sums.astype(jnp.bfloat16)


def hidden_rows(own, token_block, pieces):
    tokens, part = own.shape
    return pl.pallas_call(
        hidden_kernel,
        out_shape=[
            jax.ShapeDtypeStruct((tokens, part), jnp.float32),
            jax.ShapeDtypeStruct((tokens, part + LANES), jnp.bfloat16),
        ],
        compiler_params=pltpu.CompilerParams(vmem_limit_bytes=32 * 1024 * 1024),
        name="hidden_rows",
    )(own, token_block, *pieces)


def owner_rows_kernel(first_ref, block_ref, out_ref):
    sources, rows, _ = block_ref.shape
    _, experts, cap, part = out_ref.shape
    line = lax.broadcasted_iota(jnp.int32, (8, LANES), 0)
    column = lax.broadcasted_iota(jnp.int32, (8, LANES), 1)
    select = ((column == line + first_ref[0]) & (line < experts)).astype(jnp.bfloat16)
    earlier = (
        lax.broadcasted_iota(jnp.int32, (rows, rows), 0)
        < lax.broadcasted_iota(jnp.int32, (rows, rows), 1)
    ).astype(jnp.bfloat16)
    slot = lax.broadcasted_iota(jnp.int32, (cap, rows), 0).astype(jnp.float32)
    chosen = jnp.concatenate(
        [matmul_nt(select, block_ref[source, :, part:]) for source in range(sources)], axis=0
    )
    place = matmul(chosen.astype(jnp.bfloat16), earlier)
    for source in range(sources):
        picks = [
            jnp.where((slot == place[line:line + 1]) & (chosen[line:line + 1] > 0.5), 1.0, 0.0)
            for line in range(8 * source, 8 * source + experts)
        ]
        picks = jnp.concatenate(picks, axis=0).astype(jnp.bfloat16)
        out = matmul(picks, block_ref[source, :, :part]).astype(jnp.bfloat16)
        out_ref[source] = out.reshape(experts, cap, part)


def owner_rows(first, gathered, experts, cap):
    groups, rows, wide = gathered.shape
    part = wide - LANES
    step = 8
    return pl.pallas_call(
        owner_rows_kernel,
        grid_spec=pltpu.PrefetchScalarGridSpec(
            num_scalar_prefetch=1,
            grid=(groups // step,),
            in_specs=[pl.BlockSpec((step, rows, wide), lambda i, f: (i, 0, 0))],
            out_specs=pl.BlockSpec((step, experts, cap, part), lambda i, f: (i, 0, 0, 0)),
        ),
        out_shape=jax.ShapeDtypeStruct((groups, experts, cap, part), jnp.bfloat16),
        compiler_params=pltpu.CompilerParams(vmem_limit_bytes=60 * 1024 * 1024),
        cost_estimate=pl.CostEstimate(
            flops=2 * groups * experts * cap * rows * part, bytes_accessed=13_000_000,
            transcendentals=0,
        ),
        name="owner_rows",
    )(first, gathered)


def route_rows_kernel(rank_ref, dispatch_ref, mask_ref, gain_ref, router_ref, *rest):
    pieces, (rows_ref, wide_ref, logit_ref, scale_ref) = rest[:-4], rest[-4:]
    count = len(pieces)
    part = pieces[0].shape[1] - LANES
    model = count * part
    half = LANES // 2

    @pl.when(pl.program_id(0) == 0)
    def _():
        total = sum(jnp.sum(piece[:, part:].astype(jnp.float32), axis=1, keepdims=True)
                    for piece in pieces)
        scale = lax.rsqrt(total / model + EPS)
        scale_ref[...] = scale
        logits = jnp.zeros(logit_ref.shape, jnp.float32)
        for place in range(count):
            turn = lax.rem(rank_ref[0] - place + count, count)
            block = pieces[0][:, :part].astype(jnp.float32)
            for number in range(1, count):
                block = jnp.where(turn == number, pieces[number][:, :part].astype(jnp.float32),
                                  block)
            columns = slice(place * part, (place + 1) * part)
            block = (block * scale * gain_ref[:, columns]).astype(jnp.bfloat16)
            wide_ref[:, columns] = block
            logits += matmul(block, router_ref[columns, :])
        logit_ref[...] = logits
        sigmas = mask_ref[...] / (1.0 + jnp.exp(-logits))
        gates = ROUTE_SCALE * sigmas / jnp.sum(sigmas, axis=1, keepdims=True)
        high = gates.astype(jnp.bfloat16).astype(jnp.float32)
        wide_ref[:, model:] = jnp.concatenate([high, gates - high], axis=1).astype(jnp.bfloat16)

    rows_ref[...] = matmul(dispatch_ref[...], wide_ref[...]).astype(jnp.bfloat16)


def route_rows(rank, dispatch, mask, gain, router, pieces):
    slots, tokens = dispatch.shape
    model, experts = router.shape
    block = 256

    def whole(*shape):
        return pl.BlockSpec(shape, lambda i, r: (0, 0))

    return pl.pallas_call(
        route_rows_kernel,
        grid_spec=pltpu.PrefetchScalarGridSpec(
            num_scalar_prefetch=1,
            grid=(slots // block,),
            in_specs=[
                pl.BlockSpec((block, tokens), lambda i, r: (i, 0)),
                whole(tokens, experts), whole(1, model), whole(model, experts),
            ] + [whole(*piece.shape) for piece in pieces],
            out_specs=[
                pl.BlockSpec((block, model + LANES), lambda i, r: (i, 0)),
                whole(tokens, model + LANES), whole(tokens, experts), whole(tokens, 1),
            ],
        ),
        out_shape=[
            jax.ShapeDtypeStruct((slots, model + LANES), jnp.bfloat16),
            jax.ShapeDtypeStruct((tokens, model + LANES), jnp.bfloat16),
            jax.ShapeDtypeStruct((tokens, experts), jnp.float32),
            jax.ShapeDtypeStruct((tokens, 1), jnp.float32),
        ],
        compiler_params=pltpu.CompilerParams(vmem_limit_bytes=48 * 1024 * 1024),
        cost_estimate=pl.CostEstimate(
            flops=2 * slots * tokens * model, bytes_accessed=13_000_000, transcendentals=0
        ),
        name="route_rows",
    )(rank.reshape(1), dispatch, mask, gain.reshape(1, model), router, *pieces)


def norm_back_kernel(own_ref, extra_ref, pick_ref, back_ref, mask_ref, logit_ref, scale_ref, hidden_ref,
                     gain_ref, router_ref, cotangent_ref, *rest):
    *pieces, grad_ref, sent_ref, logit_grad_ref = rest
    part = own_ref.shape[1]
    rows, experts = mask_ref.shape
    model = part * (len(pieces) + 1)
    gathered = matmul(pick_ref[...], back_ref[...])
    norm_grad = own_ref[...] + gathered[:, :part]
    extra = extra_ref[...].astype(jnp.float32) + gathered[:, part:]
    for piece in pieces:
        norm_grad = norm_grad + piece[:, :part].astype(jnp.float32)
        extra = extra + piece[:, part:].astype(jnp.float32)
    logits = logit_ref[...]
    sigmas = mask_ref[...] / (1.0 + jnp.exp(-logits))
    total = jnp.sum(sigmas, axis=1, keepdims=True)
    gate_grad = extra[:, :experts]
    weighted_sum = jnp.sum(gate_grad * sigmas, axis=1, keepdims=True)
    sigma_grad = ROUTE_SCALE * (gate_grad / total - weighted_sum / (total * total))
    logit_grad = (sigma_grad * sigmas * (1.0 - sigmas)).astype(jnp.bfloat16)
    logit_grad_ref[...] = logit_grad
    norm_grad = norm_grad + matmul_nt(logit_grad, router_ref[...])
    mean = (
        jnp.sum(extra[:, experts:experts + 2], axis=1, keepdims=True)
        + jnp.sum(logit_grad.astype(jnp.float32) * logits, axis=1, keepdims=True)
    ) / model
    scale = scale_ref[...]
    unit = hidden_ref[...] * scale
    gain_grad = jnp.sum(norm_grad * unit, axis=0, keepdims=True)
    grad = cotangent_ref[...].astype(jnp.float32) + scale * (norm_grad * gain_ref[...] - unit * mean)
    grad_ref[...] = grad
    sent_ref[:rows, :] = grad.astype(jnp.bfloat16)
    high = gain_grad.astype(jnp.bfloat16).astype(jnp.float32)
    row = lax.broadcasted_iota(jnp.int32, (sent_ref.shape[0] - rows, part), 0)
    sums = jnp.where(row == 0, high, jnp.where(row == 1, gain_grad - high, 0.0))
    sent_ref[rows:, :] = sums.astype(jnp.bfloat16)


def norm_back(own, extra, pick, back, mask, logits, scale, hidden, gain, router, cotangent, pieces):
    rows, part = own.shape
    bf16, f32 = jnp.bfloat16, jnp.float32
    return pl.pallas_call(
        norm_back_kernel,
        out_shape=[
            jax.ShapeDtypeStruct((rows, part), f32), jax.ShapeDtypeStruct((rows + 16, part), bf16),
            jax.ShapeDtypeStruct(mask.shape, bf16),
        ],
        compiler_params=pltpu.CompilerParams(vmem_limit_bytes=32 * 1024 * 1024),
        cost_estimate=pl.CostEstimate(
            flops=400_000_000, bytes_accessed=5_000_000, transcendentals=rows * 64
        ),
        name="norm_back",
    )(own, extra, pick, back, mask, logits, scale, hidden, gain.reshape(1, part), router, cotangent, *pieces)


def put_pairs(first, grad, row, column, mine_ref, other_ref):
    rows = slice(row, row + grad.shape[2])
    columns = slice(column, column + grad.shape[3])
    even, odd = grad[:, 0], grad[:, 1]
    mine_ref[:, rows, columns] = jnp.where(first, even, odd).astype(jnp.bfloat16)
    other_ref[:, rows, columns] = jnp.where(first, odd, even).astype(jnp.bfloat16)


def late_weights_kernel(core_ref, n_ref, b_ref, t_ref, l_ref, token_ref, w_latent_ref, ffn_ref, query_ref,
                        mixed_ref, logit_ref, kv_ref, latent_ref, latent_gain_ref, cosine_ref, sine_ref,
                        scale_ref, *rest):
    *pieces, latent_grad_ref, mine_ref, other_ref, gain_buf, latent_gain_buf = rest
    step = pl.program_id(0)
    steps = pl.num_programs(0)
    pairs, chunk, _ = mine_ref.shape
    rows = latent_ref.shape[0]
    block = n_ref.shape[1]
    first = core_ref[0] == 0

    @pl.when(step == 0)
    def _():
        total = pieces[0][...].astype(jnp.float32)
        for piece in pieces[1:]:
            total = total + piece[...].astype(jnp.float32)
        count = steps
        for number in range(count):
            gain_buf[number] = (
                total[rows + number:rows + number + 1, :block]
                + total[rows + count + number:rows + count + number + 1, :block]
            )
        latent = latent_ref[...]
        compressed = latent[:, :KV_RANK]
        scale = lax.rsqrt(jnp.mean(compressed * compressed, axis=1, keepdims=True) + EPS)
        unit = compressed * scale
        grad = total[:rows, :KV_RANK]
        gains = jnp.sum(grad * unit, axis=0, keepdims=True)
        width = KV_RANK // count
        for number in range(count):
            latent_gain_buf[number] = gains[:, number * width:(number + 1) * width]
        grad = grad * latent_gain_ref[...]
        grad = scale * (grad - unit * jnp.mean(unit * grad, axis=1, keepdims=True))
        half = ROPE // 2
        former = total[:rows, KV_RANK:KV_RANK + half]
        latter = total[:rows, KV_RANK + half:KV_RANK + ROPE]
        cosine, sine = cosine_ref[...], sine_ref[...]
        latent_grad_ref[...] = jnp.concatenate(
            [grad, former * cosine + latter * sine, latter * cosine - former * sine], axis=1
        ).astype(jnp.bfloat16)

    def by_pairs(grad):
        return grad.reshape(pairs, 2, grad.shape[0] // (2 * pairs), grad.shape[1])

    low = 0
    for rows_ref, grads in (
        (n_ref, query_ref), (b_ref, mixed_ref), (n_ref, latent_grad_ref), (t_ref, logit_ref)
    ):
        grad = matmul_tn(rows_ref[...], grads[...])
        put_pairs(first, by_pairs(grad), 0, low, mine_ref, other_ref)
        low += grad.shape[1]
    grad = by_pairs(matmul_tn(l_ref[...], kv_ref[...]))
    kv_chunk = grad.shape[2]
    columns = grad.shape[3] * kv_chunk // chunk
    for place in range(chunk // kv_chunk):
        put_pairs(first, grad[:, :, :, place * columns:(place + 1) * columns], place * kv_chunk, low,
                  mine_ref, other_ref)
    unit = token_ref[...].astype(jnp.float32) * scale_ref[...]
    routed = matmul(latent_grad_ref[...], w_latent_ref[...])
    gain = gain_buf[step] + jnp.sum(routed * unit, axis=0, keepdims=True)
    line = lax.broadcasted_iota(jnp.int32, (LANES, block), 0)
    gains = by_pairs(jnp.where(line == 0, gain, jnp.where(line == 1, ffn_ref[...], 0.0)).T)
    width = latent_gain_buf.shape[2]
    line = lax.broadcasted_iota(jnp.int32, (LANES, width), 0)
    more = by_pairs(jnp.where(line == 2, latent_gain_buf[step], 0.0).T)
    gains = jnp.concatenate([gains[:, :, :kv_chunk] + more, gains[:, :, kv_chunk:]], axis=2)
    put_pairs(first, gains, 0, low + columns, mine_ref, other_ref)


def late_weights(core, groups, normed, branch, normed_two, latent_normed, tokens, w_latent, ffn_gain, query,
                 mixed, logit, kv, latent, latent_gain, cosine, sine, scale, pieces):
    rows_count, model = normed.shape
    steps = 4
    block = model // steps
    chunk = model // groups
    latent_width = latent.shape[1]
    columns = (
        query.shape[1] + mixed.shape[1] + latent_width + logit.shape[1]
        + kv.shape[1] * latent_normed.shape[1] // model + LANES
    )
    rows = pl.BlockSpec((rows_count, block), lambda i, c: (0, i))

    def whole(array):
        return pl.BlockSpec(array.shape, lambda i, c: (0, 0))

    piece_block = pl.BlockSpec(pieces[0].shape, lambda i, c: (0, 0))
    gain = latent_gain.reshape(1, -1)
    fixed = [query, mixed, logit, kv, latent, gain, cosine, sine, scale]
    return pl.pallas_call(
        late_weights_kernel,
        grid_spec=pltpu.PrefetchScalarGridSpec(
            num_scalar_prefetch=1,
            grid=(steps,),
            in_specs=[
                rows, rows, rows,
                pl.BlockSpec((rows_count, latent_normed.shape[1] // steps), lambda i, c: (0, i)),
                rows, pl.BlockSpec((latent_width, block), lambda i, c: (0, i)),
                pl.BlockSpec((1, block), lambda i, c: (0, i)),
            ] + [whole(array) for array in fixed] + [piece_block] * len(pieces),
            out_specs=[whole(latent)] + [
                pl.BlockSpec((groups // 2 // steps, chunk, columns), lambda i, c: (i, 0, 0))
            ] * 2,
            scratch_shapes=[
                pltpu.VMEM((steps, 1, block), jnp.float32),
                pltpu.VMEM((steps, 1, KV_RANK // steps), jnp.float32),
            ],
        ),
        out_shape=[jax.ShapeDtypeStruct(latent.shape, jnp.bfloat16)]
        + [jax.ShapeDtypeStruct((groups // 2, chunk, columns), jnp.bfloat16)] * 2,
        compiler_params=pltpu.CompilerParams(vmem_limit_bytes=56 * 1024 * 1024),
        cost_estimate=pl.CostEstimate(
            flops=2 * rows_count * model * columns, bytes_accessed=16_000_000, transcendentals=0
        ),
        name="late_weights",
    )(core.reshape(1), normed, branch, normed_two, latent_normed, tokens, w_latent.T, ffn_gain, *fixed,
      *pieces)


def split_kernel(place_ref, mine_ref, got_ref, *outs):
    side = len(outs) // 2
    near = outs[0].shape[1]
    for step in range(side):
        to_z = lax.rem(place_ref[0] + step, side)
        to_x = lax.rem(place_ref[1] + step, side)
        for line in range(side):
            value = mine_ref[line, to_x, :near, :].astype(jnp.float32)
            value = value + got_ref[line, to_x, :near, :].astype(jnp.float32)
            outs[step][line] = value.astype(outs[step].dtype)
            value = mine_ref[to_z, line, near:, :].astype(jnp.float32)
            value = value + got_ref[to_z, line, near:, :].astype(jnp.float32)
            outs[side + step][line] = value.astype(outs[side + step].dtype)


def turn_kernel(place_ref, *refs):
    side = len(refs) // 4
    ins, outs = refs[:2 * side], refs[2 * side:]
    for half in range(2):
        for step in range(side):
            index = lax.rem(place_ref[half] + step, side)
            value = ins[half * side][index]
            for number in range(1, side):
                value = value + ins[half * side + number][index].astype(jnp.float32)
            out = outs[half * side + step]
            out[...] = value.astype(out.dtype)


def whole_call(kernel, place, arrays, shapes, name):
    return pl.pallas_call(
        kernel,
        grid_spec=pltpu.PrefetchScalarGridSpec(
            num_scalar_prefetch=1,
            grid=(1,),
            in_specs=[
                pl.BlockSpec(a.shape, lambda i, p, n=a.ndim: (0,) * n) for a in arrays
            ],
            out_specs=[
                pl.BlockSpec(a.shape, lambda i, p, n=len(a.shape): (0,) * n) for a in shapes
            ],
        ),
        out_shape=shapes,
        compiler_params=pltpu.CompilerParams(vmem_limit_bytes=56 * 1024 * 1024),
        cost_estimate=pl.CostEstimate(
            flops=0, bytes_accessed=sum(2 * a.size for a in arrays) * 2, transcendentals=0
        ),
        name=name,
    )(place, *arrays)


def tree_scatter(mine, other, group, groups):
    side = math.isqrt(groups // 2)
    rows, columns = mine.shape[1:]
    near = rows // 2
    far = rows - near
    place = jnp.stack([group // (2 * side), lax.rem(group // 2, side)])

    def moved(array, move):
        pairs = []
        for index in range(groups):
            z, x, core = index // (2 * side), index // 2 % side, index % 2
            z, x, core = move(z, x, core)
            pairs.append((index, ((z % side) * side + x % side) * 2 + core))
        return lax.ppermute(array, "expert", pairs)

    def shape(*sizes, kind=jnp.bfloat16):
        return jax.ShapeDtypeStruct(sizes, kind)

    got = moved(other, lambda z, x, core: (z, x, 1 - core))
    square = (side, side, rows, columns)
    shapes = [shape(side, n, columns, kind=jnp.float32 if step == 0 else jnp.bfloat16)
              for n in (near, far) for step in range(side)]
    parts = list(whole_call(
        split_kernel, place, [mine.reshape(square), got.reshape(square)], shapes, "split_sum"
    ))
    sent = parts[0]
    for step in range(1, side):
        parts[step] = moved(parts[step], lambda z, x, core: (z, x + step, core))
        parts[side + step] = moved(parts[side + step], lambda z, x, core: (z + step, x, core))
    shapes = [shape(n, columns, kind=jnp.float32 if step == 0 else jnp.bfloat16)
              for n in (near, far) for step in range(side)]
    parts = list(whole_call(turn_kernel, place, parts, shapes, "turn_sum"))
    turned = parts[0]
    for step in range(1, side):
        parts[step] = moved(parts[step], lambda z, x, core: (z + step, x, core))
        parts[side + step] = moved(parts[side + step], lambda z, x, core: (z, x + step, core))
    halves = [
        sum(p.astype(jnp.float32) for p in parts[low:low + side]) for low in (0, side)
    ]
    return (jnp.concatenate(halves, axis=0), sent, turned)


def shards(
    tokens,
    cotangent,
    attn_gain,
    w_query,
    w_latent,
    latent_gain,
    w_keyvalue,
    w_output,
    ffn_gain,
    w_router,
    shared_gate,
    shared_up,
    shared_down,
    expert_gate,
    expert_up,
    expert_down,
    routes,
):
    bf16 = jnp.bfloat16
    f32 = jnp.float32
    tok_rows, model_width = tokens.shape
    top_count = routes.shape[1]
    expert_count = w_router.shape[1]
    local_experts, _, hidden_width = expert_gate.shape
    groups = lax.axis_size("expert")
    ranks = lax.axis_size("tensor")
    rank = lax.axis_index("tensor")
    group = lax.axis_index("expert")
    part = model_width // ranks
    capacity = (4 * tok_rows * top_count + 3 * expert_count - 1) // (3 * expert_count)
    slot_count = expert_count * capacity
    per_group = local_experts * capacity
    qk_width = NOPE + ROPE
    local_heads = w_query.shape[1] // qk_width

    expert_ids = jnp.arange(expert_count, dtype=jnp.int32)
    selector = routes[:, :, None] == expert_ids[None, None, :]
    chosen_mask = jnp.sum(selector.astype(f32), axis=1)

    cotangent_part = column_block(cotangent, rank, part)
    chosen_low = jnp.pad(chosen_mask.astype(bf16), ((0, 0), (0, LANES - expert_count)))
    all_grads = lax.all_gather(
        jnp.concatenate([cotangent_part, chosen_low], axis=1), "expert", axis=0
    )

    tables = rotary_constants(tok_rows, local_heads)
    (normed, scale_one, query_pre, query_low, latent, latent_normed, keyvalue, key_rope, weights_full,
     attn_mixed, attended, *sends) = attention_forward(
        rank, tokens, attn_gain, latent_gain, tables, w_latent, w_query, w_keyvalue, w_output, ranks
    )

    token_ids = jnp.arange(tok_rows, dtype=jnp.int32)
    before = (token_ids[:, None] > token_ids[None, :]).astype(bf16)
    earlier = matmul(before, after(chosen_mask, attended).astype(bf16))
    place = jnp.sum(jnp.where(selector, earlier[:, None, :], 0.0), axis=-1).astype(jnp.int32)
    expert_place = lax.rem(routes, local_experts) * groups + routes // local_experts
    slot_ids = jnp.arange(slot_count, dtype=jnp.int32)

    def one_hot(target, sideways):
        shape = (tok_rows, slot_count) if sideways else (slot_count, tok_rows)
        found = jnp.zeros(shape, jnp.bool_)
        for choice in range(top_count):
            if sideways:
                found = found | (target[:, choice][:, None] == slot_ids[None, :])
            else:
                found = found | (slot_ids[:, None] == target[:, choice][None, :])
        return found.astype(bf16)

    dispatch = one_hot(routes * capacity + place, False)
    combine = one_hot(routes * capacity + place, True)
    by_expert = one_hot(expert_place * capacity + place, True)
    by_expert = by_expert.reshape(tok_rows, local_experts, groups * capacity)

    sends = [shift_ranks(sent, step + 1, ranks) for step, sent in enumerate(sends)]
    hidden_part, sent = hidden_rows(attended, column_block(tokens, rank, part), sends)
    first = (group * local_experts).reshape(1)
    pieces = [sent] + [shift_ranks(sent, step, ranks) for step in range(1, ranks)]

    rows_sent, wide, logits, scale_two = route_rows(
        rank, dispatch, chosen_mask, ffn_gain, w_router, pieces
    )
    normed_two = wide[:, :model_width]
    unit_two_part = hidden_part * scale_two
    sigmas = jax.nn.sigmoid(logits) * chosen_mask
    sigma_total = jnp.sum(sigmas, axis=-1, keepdims=True)
    arrived = lax.all_to_all(
        rows_sent.reshape(groups, per_group, -1), "expert", split_axis=0, concat_axis=0, tiled=True
    )
    grad_quarter = owner_rows(first, after(all_grads, wide), local_experts, capacity)
    grad_arrived = lax.all_gather(grad_quarter, "tensor", axis=0)

    shared_gate_pre = matmul(normed_two, shared_gate)
    shared_up_pre = matmul(normed_two, shared_up)
    shared_act = (jax.nn.silu(shared_gate_pre) * shared_up_pre).astype(bf16)
    shared_part = matmul(shared_act, shared_down).astype(bf16)
    shared_part = lax.psum_scatter(
        shared_part.reshape(tok_rows, ranks, part).transpose(1, 0, 2), "tensor",
        scatter_dimension=0, tiled=True,
    ).reshape(tok_rows, part)
    grad_shared_act = matmul_nt(cotangent, shared_down)
    shared_gate_grad, shared_up_grad = silu_back(grad_shared_act, shared_gate_pre, shared_up_pre)
    norm_part = matmul_nt(shared_gate_grad, shared_gate) + matmul_nt(shared_up_grad, shared_up)
    shared_dot = jnp.sum(
        shared_gate_grad.astype(f32) * shared_gate_pre + shared_up_grad.astype(f32) * shared_up_pre,
        axis=-1, keepdims=True,
    )
    shared_grads = shared_weights(
        normed_two, cotangent, shared_gate_grad, shared_up_grad, shared_act, groups
    )

    width = -(-hidden_width // LANES) * LANES
    widen = ((0, 0), (0, 0), (0, width - hidden_width))
    gate_up = jnp.concatenate([jnp.pad(expert_gate, widen), jnp.pad(expert_up, widen)], axis=2)
    down = jnp.pad(expert_down, ((0, 0), (0, width - hidden_width), (0, 0)))
    gate_up_t = gate_up.transpose(0, 2, 1)
    down_t = down.transpose(0, 2, 1)
    weights = (gate_up, gate_up_t, down, down_t)
    arrived = after(
        arrived, shared_grads, shared_part, norm_part, shared_dot, combine, by_expert, *weights
    ).reshape(groups, local_experts, capacity, -1)
    produced, back, pre_grad, act_weighted = expert_rows(
        0, first, arrived, grad_arrived, weights, True
    )
    back = lax.psum_scatter(back, "tensor", scatter_dimension=0, tiled=True)[0]
    produced, direct, next_grad, next_weighted = expert_rows(
        1, first, arrived, grad_arrived, weights, False, produced
    )
    direct = lax.all_to_all(direct, "expert", split_axis=0, concat_axis=0, tiled=True)
    weight_grads = expert_weights(
        1, arrived, grad_arrived, next_grad, next_weighted, hidden_width
    )
    weight_grads = expert_weights(
        0, arrived, grad_arrived, pre_grad, act_weighted, hidden_width, weight_grads
    )
    direct = after(direct, *weight_grads).reshape(groups * capacity, -1)
    grad_expert_gate, grad_expert_up, grad_expert_down = weight_grads
    produced = lax.psum_scatter(
        produced.reshape(ranks, groups, per_group, part), "tensor", scatter_dimension=0, tiled=True
    )[0]
    back = lax.all_to_all(
        after(back, direct), "expert", split_axis=0, concat_axis=0, tiled=True
    ).reshape(groups * capacity, -1)

    norm_grad, extra_low, *sends = combine_rows(
        rank, by_expert[:, 1], direct, norm_part, shared_dot, ranks
    )
    pieces = [shift_ranks(after(sent, back), step + 1, ranks) for step, sent in enumerate(sends)]
    router_rows = lax.dynamic_slice_in_dim(w_router, rank * part, part, axis=0)
    ffn_gain_part = lax.dynamic_slice_in_dim(ffn_gain, rank * part, part, axis=0)
    hidden_grad, sent, logit_grad = norm_back(
        norm_grad, extra_low, by_expert[:, 0], back, chosen_mask, logits, scale_two, hidden_part,
        ffn_gain_part, router_rows, cotangent_part, pieces,
    )
    pieces = [sent] + [shift_ranks(sent, step, ranks) for step in range(1, ranks)]

    (branch_low, grad_ffn_gain, query_pre_grad, keyvalue_grad, normed_grad, latent_sent,
     *sends) = attention_backward(
        rank, pieces, weights_full, keyvalue, key_rope, query_low, query_pre, tokens, scale_one, tables,
        w_output, w_keyvalue, w_query,
    )
    pieces = [shift_ranks(sent, step + 1, ranks) for step, sent in enumerate(sends)]

    returned = lax.all_to_all(
        after(produced, back, branch_low), "expert", split_axis=0, concat_axis=0, tiled=True
    ).reshape(slot_count, part)

    chunk = model_width // groups
    kv_chunk = KV_RANK // groups
    latent_grad, mine, other = late_weights(
        lax.rem(group, 2), groups, normed, branch_low, normed_two, latent_normed, tokens, w_latent,
        grad_ffn_gain, query_pre_grad, attn_mixed, logit_grad, keyvalue_grad, latent, latent_gain,
        tables[3], tables[4], scale_one, [after(latent_sent, returned)] + pieces,
    )
    late, late_sent, late_turned = tree_scatter(mine, other, group, groups)

    routed_part = matmul(combine, after(returned, late_sent))
    output_part = (hidden_part + shared_part.astype(f32) + routed_part).astype(bf16)
    output = lax.all_gather(output_part, "tensor", axis=0)
    output = output.transpose(1, 0, 2).reshape(tok_rows, model_width)

    sums = latent_sent[:tok_rows, KV_RANK + ROPE:KV_RANK + ROPE + 2].astype(f32)
    for piece in pieces:
        normed_grad = normed_grad + piece[:tok_rows, -part:].astype(f32)
        sums = sums + piece[:tok_rows, KV_RANK + ROPE:KV_RANK + ROPE + 2].astype(f32)
    latent_rows = lax.dynamic_slice_in_dim(w_latent, rank * part, part, axis=0)
    normed_grad = normed_grad + matmul_nt(latent_grad, latent_rows)
    row_mean = (
        jnp.sum(sums, axis=-1, keepdims=True)
        + jnp.sum(latent_grad.astype(f32) * latent, axis=-1, keepdims=True)
    ) / model_width
    unit_one_part = column_block(tokens, rank, part).astype(f32) * scale_one
    attn_gain_part = lax.dynamic_slice_in_dim(attn_gain, rank * part, part, axis=0)
    grad_tokens = hidden_grad + scale_one * (
        normed_grad * attn_gain_part - unit_one_part * row_mean
    )
    grad_tokens = after(grad_tokens.astype(bf16), late_turned)
    grad_tokens, _ = gather_columns(grad_tokens, rank, ranks, part)

    shared_width = shared_gate.shape[1]
    early = lax.psum_scatter(
        after(shared_grads, direct).reshape(groups * 3 * chunk, shared_width), "expert",
        scatter_dimension=0, tiled=True,
    )
    early = after(early, late_turned).astype(f32)
    grad_shared_gate = early[:chunk]
    grad_shared_up = early[chunk:2 * chunk]
    grad_shared_down = early[2 * chunk:].T

    edges = [0]
    for columns in (
        query_pre_grad.shape[1], attn_mixed.shape[1], latent_grad.shape[1], expert_count,
        keyvalue_grad.shape[1] * KV_RANK // model_width, LANES,
    ):
        edges.append(edges[-1] + columns)
    grad_query, grad_output, grad_latent, grad_router, kv_rows, gains = (
        late[:, low:high] for low, high in zip(edges[:-1], edges[1:])
    )
    grad_keyvalue = jnp.concatenate(
        [kv_rows[low:low + kv_chunk] for low in range(0, chunk, kv_chunk)], axis=1
    )
    return (
        output,
        grad_tokens,
        gains[:, 0],
        grad_query,
        grad_latent,
        gains[:kv_chunk, 2],
        grad_keyvalue,
        grad_output.T,
        gains[:, 1],
        grad_router,
        grad_shared_gate,
        grad_shared_up,
        grad_shared_down,
        grad_expert_gate.transpose(0, 2, 1),
        grad_expert_up.transpose(0, 2, 1),
        grad_expert_down,
    )


def solution(mesh):
    return jax.shard_map(
        shards,
        mesh=mesh,
        in_specs=(
            P("expert", None),
            P("expert", None),
            P(),
            P(None, "tensor"),
            P(),
            P(),
            P(None, "tensor"),
            P("tensor", None),
            P(),
            P(),
            P(None, "tensor"),
            P(None, "tensor"),
            P("tensor", None),
            P("expert", None, "tensor"),
            P("expert", None, "tensor"),
            P("expert", "tensor", None),
            P("expert", None),
        ),
        out_specs=(
            P("expert", None),
            P("expert", None),
            P("expert"),
            P("expert", "tensor"),
            P("expert", None),
            P("expert"),
            P("expert", "tensor"),
            P("tensor", "expert"),
            P("expert"),
            P("expert", None),
            P("expert", "tensor"),
            P("expert", "tensor"),
            P("tensor", "expert"),
            P("expert", None, "tensor"),
            P("expert", None, "tensor"),
            P("expert", "tensor", None),
        ),
        check_vma=False,
    )
```

```python
import functools

import jax
import jax.numpy as jnp
import numpy as np
from jax import lax
from jax.experimental import pallas as pl
from jax.experimental.pallas import tpu as pltpu
from jax.sharding import PartitionSpec as P

NOPE = 128
ROPE = 64
VDIM = 128
KV_RANK = 512


EPS = 1e-06
THETA = 50000.0
ROUTE_SCALE = 2.446
MASKED = -1e30
LANES = 128
VMEM_BYTES = 60 * 1024 * 1024


def silu_back(grad_act, gate_pre, up_pre):
    sigma_gate = jax.nn.sigmoid(gate_pre)
    grad_up = grad_act * gate_pre * sigma_gate
    grad_gate = grad_act * up_pre * sigma_gate * (1.0 + gate_pre * (1.0 - sigma_gate))
    return (grad_gate.astype(jnp.bfloat16), grad_up.astype(jnp.bfloat16))


def matmul(left_side, right_side):
    return jnp.dot(left_side, right_side, preferred_element_type=jnp.float32)


def matmul_tn(left_side, right_side):
    return lax.dot_general(
        left_side, right_side, (((0,), (0,)), ((), ())), preferred_element_type=jnp.float32
    )


def matmul_nt(left_side, right_side):
    return lax.dot_general(
        left_side, right_side, (((1,), (1,)), ((), ())), preferred_element_type=jnp.float32
    )


def after(value, *others):
    return lax.optimization_barrier((value,) + others)[0]


def shift_ranks(values, step, count):
    return lax.ppermute(values, "tensor", [(i, (i + step) % count) for i in range(count)])


def column_block(values, index, width):
    return lax.dynamic_slice_in_dim(values, index * width, width, axis=1)


def expert_rows_kernel(sideways, first_ref, x_ref, mask_ref, router_ref, g_ref, wgu_ref, wgut_ref, wd_ref,
                       wdt_ref, *rest):
    dgu_ref, actw_ref, rowgrad_ref = rest[:3]
    quarters, step, cap, part = g_ref.shape
    rows = step * cap
    width, model = wd_ref.shape
    half = LANES // 2
    expert = first_ref[0]
    experts = router_ref.shape[1]
    x_rows = x_ref[...].reshape(rows, model)
    mask = mask_ref[...].reshape(rows, LANES)[:, :experts].astype(jnp.float32)
    sigmas = mask / (1.0 + jnp.exp(-matmul(x_rows, router_ref[...])))
    total = jnp.sum(sigmas, axis=1, keepdims=True)
    column = lax.broadcasted_iota(jnp.int32, sigmas.shape, 1)
    own = jnp.sum(jnp.where(column == expert, sigmas, 0.0), axis=1, keepdims=True)
    weight = jnp.where(total > 0.0, ROUTE_SCALE * own / jnp.where(total > 0.0, total, 1.0), 0.0)
    column = lax.broadcasted_iota(jnp.int32, (rows, LANES), 1)

    def by_quarters(values_ref, matrix_ref):
        total = matmul(values_ref[0].reshape(rows, part), matrix_ref[:part, :])
        for place in range(1, quarters):
            total += matmul(
                values_ref[place].reshape(rows, part),
                matrix_ref[place * part:(place + 1) * part, :],
            )
        return total

    pre = matmul(x_rows, wgu_ref[...])
    grad_act = by_quarters(g_ref, wdt_ref)
    gate_pre = pre[:, :width]
    up_pre = pre[:, width:]
    sigma = 1.0 / (1.0 + jnp.exp(-gate_pre))
    silu = gate_pre * sigma
    act = silu * up_pre
    act_weighted = (act * weight).astype(jnp.bfloat16)
    actw_ref[...] = act_weighted
    out = matmul(act_weighted, wd_ref[...]).astype(jnp.bfloat16)
    if sideways:
        for place in range(quarters):
            rowgrad_ref[place, :, :, part + LANES:] = (
                out[:, place * part:(place + 1) * part].reshape(step, cap, part)
            )
    else:
        rest[3][...] = out.reshape(step, cap, model)
    dot = jnp.sum(grad_act * act, axis=1, keepdims=True)
    grad_act = grad_act * weight
    grad_up = grad_act * silu
    grad_gate = grad_act * up_pre * (sigma + silu * (1.0 - sigma))
    row_dot = jnp.sum(grad_gate * gate_pre + grad_up * up_pre, axis=1, keepdims=True)
    row_dot_high = row_dot.astype(jnp.bfloat16).astype(jnp.float32)
    pre_grad = jnp.concatenate([grad_gate, grad_up], axis=1).astype(jnp.bfloat16)
    dgu_ref[...] = pre_grad
    row_grad = matmul(pre_grad, wgut_ref[...]).astype(jnp.bfloat16)
    sums = jnp.where(column == expert, dot, 0.0)
    sums = jnp.where(column == half, row_dot_high, sums)
    sums = jnp.where(column == half + 1, row_dot - row_dot_high, sums)
    sums = sums.astype(jnp.bfloat16).reshape(step, cap, LANES)
    if sideways:
        for place in range(quarters):
            rowgrad_ref[place, :, :, :part] = (
                row_grad[:, place * part:(place + 1) * part].reshape(step, cap, part)
            )
            rowgrad_ref[place, :, :, part:part + LANES] = sums
    else:
        rowgrad_ref[:, :, :model] = row_grad.reshape(step, cap, model)
        rowgrad_ref[:, :, model:] = sums


def expert_rows(number, first, x, mask, router, g, weights, sideways):
    sources, experts, cap, model = x.shape
    quarters, _, _, part = g.shape
    wgu, wgut, wd, wdt = weights
    width = wd.shape[1]
    step = 8
    rows = step * cap
    total = sources * cap

    def flat_block(columns):
        return pl.BlockSpec((rows, columns), lambda b, f: (b, 0))

    def whole(*shape):
        return pl.BlockSpec((None,) + shape, lambda b, f: (number, 0, 0))

    def kind(*shape):
        return jax.ShapeDtypeStruct(shape, jnp.bfloat16)

    def part_block(columns):
        return pl.BlockSpec((quarters, step, cap, columns), lambda b, f: (0, b, 0, 0))

    def row_block(columns):
        return pl.BlockSpec((step, cap, columns), lambda b, f: (b, 0, 0))

    def expert_block(columns):
        return pl.BlockSpec((step, None, cap, columns), lambda b, f: (b, number, 0, 0))

    in_specs = [
        expert_block(model), expert_block(LANES), pl.BlockSpec(router.shape, lambda b, f: (0, 0)),
        part_block(part), whole(model, 2 * width), whole(2 * width, model), whole(width, model),
        whole(model, width),
    ]
    return pl.pallas_call(
        functools.partial(expert_rows_kernel, sideways),
        grid_spec=pltpu.PrefetchScalarGridSpec(
            num_scalar_prefetch=1,
            grid=(sources // step,),
            in_specs=in_specs,
            out_specs=[flat_block(2 * width), flat_block(width)] + (
                [part_block(2 * part + LANES)] if sideways
                else [row_block(model + LANES), row_block(model)]
            ),
        ),
        out_shape=[kind(total, 2 * width), kind(total, width)] + (
            [kind(quarters, sources, cap, 2 * part + LANES)] if sideways
            else [kind(sources, cap, model + LANES), kind(sources, cap, model)]
        ),
        compiler_params=pltpu.CompilerParams(vmem_limit_bytes=VMEM_BYTES),
        cost_estimate=pl.CostEstimate(
            flops=2 * total * model * width * 6, bytes_accessed=30_000_000,
            transcendentals=total * width,
        ),
        name=f"expert_rows_{number}",
    )(first + number, x, mask, router, g, wgu, wgut, wd, wdt)


def expert_weights_kernel(x_ref, g_ref, dgu_ref, actw_ref, *rest):
    gate_ref, up_ref, down_ref = rest[-3:]
    rows, width = actw_ref.shape
    hidden = gate_ref.shape[0]
    grad = matmul_tn(dgu_ref[...], x_ref[...].reshape(rows, x_ref.shape[-1]))
    gate_ref[...] = grad[:hidden, :]
    up_ref[...] = grad[width:width + hidden, :]
    g_rows = g_ref[...].reshape(rows, g_ref.shape[-1])
    down_ref[...] = matmul_tn(actw_ref[...], g_rows)[:hidden, :]


def expert_weights(number, x, g, dgu, actw, hidden, before=()):
    quarters = g.shape[0]
    sources, experts, cap, model = x.shape
    total, width = actw.shape
    steps = 8
    part = model // steps
    per = steps // quarters
    x_block = pl.BlockSpec((sources, None, cap, part), lambda b: (0, number, 0, b))
    in_specs = [
        x_block,
        pl.BlockSpec((None, sources, cap, part), lambda b: (b // per, 0, 0, b % per)),
        pl.BlockSpec((total, 2 * width), lambda b: (0, 0)),
        pl.BlockSpec((total, width), lambda b: (0, 0)),
    ] + [pl.BlockSpec(memory_space=pl.ANY)] * len(before)
    return pl.pallas_call(
        expert_weights_kernel,
        grid=(steps,),
        in_specs=in_specs,
        out_specs=[pl.BlockSpec((None, hidden, part), lambda b: (number, 0, b))] * 3,
        out_shape=[jax.ShapeDtypeStruct((experts, hidden, model), jnp.float32)] * 3,
        compiler_params=pltpu.CompilerParams(vmem_limit_bytes=VMEM_BYTES),
        cost_estimate=pl.CostEstimate(
            flops=2 * total * model * width * 3, bytes_accessed=22_000_000, transcendentals=0
        ),
        input_output_aliases={4 + place: place for place in range(len(before))},
        name=f"expert_weights_{number}",
    )(x, g, dgu, actw, *before)


def shared_weights_kernel(n_ref, c_ref, gate_ref, up_ref, act_ref, out_ref):
    chunk = out_ref.shape[1] // 3
    for place, (rows, grads) in enumerate(
        ((n_ref, gate_ref), (n_ref, up_ref), (c_ref, act_ref))
    ):
        grad = matmul_tn(rows[...], grads[...]).astype(jnp.bfloat16)
        for group in range(out_ref.shape[0]):
            out_ref[group, place * chunk:(place + 1) * chunk, :] = (
                grad[group * chunk:(group + 1) * chunk, :]
            )


def shared_weights(normed, cotangent, gate_grad, up_grad, act, groups):
    tokens, model = normed.shape
    width = gate_grad.shape[1]
    block = 256
    chunk = model // groups
    per = block // chunk
    rows = pl.BlockSpec((tokens, block), lambda i: (0, i))
    grads = pl.BlockSpec((tokens, width), lambda i: (0, 0))
    return pl.pallas_call(
        shared_weights_kernel,
        grid=(model // block,),
        in_specs=[rows, rows, grads, grads, grads],
        out_specs=pl.BlockSpec((per, 3 * chunk, width), lambda i: (i, 0, 0)),
        out_shape=jax.ShapeDtypeStruct((groups, 3 * chunk, width), jnp.bfloat16),
        compiler_params=pltpu.CompilerParams(vmem_limit_bytes=VMEM_BYTES),
        cost_estimate=pl.CostEstimate(
            flops=6 * tokens * model * width, bytes_accessed=14_000_000, transcendentals=0
        ),
        name="shared_weights",
    )(normed, cotangent, gate_grad, up_grad, act)


def combine_kernel(rank_ref, pick_ref, back_ref, sums_ref, shared_ref, dots_ref,
                   own_ref, extra_ref, *sends):
    step = pl.program_id(0)
    count = pl.num_programs(0)
    place = lax.rem(step - rank_ref[0] + count, count)
    part = own_ref.shape[1]
    value = matmul(pick_ref[...], back_ref[...]) + shared_ref[...]

    @pl.when(place == 0)
    def _():
        own_ref[...] = value

    for number, send in enumerate(sends):
        @pl.when(place == number + 1)
        def _():
            send[:, :part] = value.astype(jnp.bfloat16)

    @pl.when(step == count - 1)
    def _():
        mark = LANES // 2
        sums = matmul(pick_ref[...], sums_ref[...])
        column = lax.broadcasted_iota(jnp.int32, sums.shape, 1)
        mean = dots_ref[...] + jnp.sum(
            jnp.where((column == mark) | (column == mark + 1), sums, 0.0), axis=1, keepdims=True
        )
        mean_high = mean.astype(jnp.bfloat16).astype(jnp.float32)
        extra = jnp.where(column < mark, sums, 0.0)
        extra = jnp.where(column == mark, mean_high, extra)
        extra = jnp.where(column == mark + 1, mean - mean_high, extra).astype(jnp.bfloat16)
        extra_ref[...] = extra
        for send in sends:
            send[:, part:] = extra


def combine_rows(rank, pick, back, shared, dots, count):
    tokens, slots = pick.shape
    model = shared.shape[1]
    part = model // count
    sent = jax.ShapeDtypeStruct((tokens, part + LANES), jnp.bfloat16)
    sent_block = pl.BlockSpec((tokens, part + LANES), lambda i, r: (0, 0))
    return pl.pallas_call(
        combine_kernel,
        grid_spec=pltpu.PrefetchScalarGridSpec(
            num_scalar_prefetch=1,
            grid=(count,),
            in_specs=[
                pl.BlockSpec((tokens, slots), lambda i, r: (0, 0)),
                pl.BlockSpec((slots, part), lambda i, r: (0, i)),
                pl.BlockSpec((slots, LANES), lambda i, r: (0, model // LANES)),
                pl.BlockSpec((tokens, part), lambda i, r: (0, i)),
                pl.BlockSpec((tokens, 1), lambda i, r: (0, 0)),
            ],
            out_specs=[
                pl.BlockSpec((tokens, part), lambda i, r: (0, 0)),
                pl.BlockSpec((tokens, LANES), lambda i, r: (0, 0)),
            ] + [sent_block] * (count - 1),
        ),
        out_shape=[
            jax.ShapeDtypeStruct((tokens, part), jnp.float32),
            jax.ShapeDtypeStruct((tokens, LANES), jnp.bfloat16),
        ] + [sent] * (count - 1),
        compiler_params=pltpu.CompilerParams(vmem_limit_bytes=VMEM_BYTES),
        cost_estimate=pl.CostEstimate(
            flops=2 * tokens * slots * model, bytes_accessed=9_000_000, transcendentals=0
        ),
        name="combine_rows",
    )(rank.reshape(1), pick, back, back, shared, dots)


def branch_kernel(rank_ref, pick_ref, back_ref, shared_ref, own_ref, *sends):
    step = pl.program_id(0)
    count = pl.num_programs(0)
    place = lax.rem(step - rank_ref[0] + count, count)
    value = matmul(pick_ref[...], back_ref[...]) + shared_ref[...]

    @pl.when(place == 0)
    def _():
        own_ref[...] = value

    for number, send in enumerate(sends):
        @pl.when(place == number + 1)
        def _():
            send[...] = value.astype(jnp.bfloat16)


def branch_rows(rank, pick, back, shared, count):
    tokens, slots = pick.shape
    model = shared.shape[1]
    part = model // count
    fixed = pl.BlockSpec((tokens, part), lambda i, r: (0, 0))
    return pl.pallas_call(
        branch_kernel,
        grid_spec=pltpu.PrefetchScalarGridSpec(
            num_scalar_prefetch=1,
            grid=(count,),
            in_specs=[
                pl.BlockSpec((tokens, slots), lambda i, r: (0, 0)),
                pl.BlockSpec((slots, part), lambda i, r: (0, i)),
                pl.BlockSpec((tokens, part), lambda i, r: (0, i)),
            ],
            out_specs=[fixed] * count,
        ),
        out_shape=[jax.ShapeDtypeStruct((tokens, part), jnp.float32)]
        + [jax.ShapeDtypeStruct((tokens, part), jnp.bfloat16)] * (count - 1),
        compiler_params=pltpu.CompilerParams(vmem_limit_bytes=VMEM_BYTES),
        cost_estimate=pl.CostEstimate(flops=0, bytes_accessed=4_000_000, transcendentals=0),
        name="branch_rows",
    )(rank.reshape(1), pick, back, shared)


def token_kernel(own_ref, latent_grad_ref, w_latent_ref, mean_ref, token_ref, scale_ref, gain_ref, hidden_ref,
                 *rest):
    *pieces, out_ref = rest
    grad = own_ref[...] + matmul_nt(latent_grad_ref[...], w_latent_ref[...])
    for piece in pieces:
        grad = grad + piece[...].astype(jnp.float32)
    scale = scale_ref[...]
    unit = token_ref[...].astype(jnp.float32) * scale
    grad = hidden_ref[...] + scale * (grad * gain_ref[...] - unit * mean_ref[...])
    out_ref[...] = grad.astype(jnp.bfloat16)


def output_kernel(own_ref, hidden_ref, pick_ref, back_ref, *rest):
    *pieces, out_ref = rest
    value = hidden_ref[...] + own_ref[...] + matmul(pick_ref[...], back_ref[...])
    for piece in pieces:
        value = value + piece[...].astype(jnp.float32)
    out_ref[...] = value.astype(jnp.bfloat16)


def attention_forward_kernel(rank_ref, token_ref, gain_ref, latent_gain_ref, cosine_ref, ahead_ref,
                             behind_ref, key_cosine_ref, key_sine_ref, w_latent_ref, w_query_ref,
                             w_keyvalue_ref, w_output_ref,
                             normed_ref, scale_ref, query_ref, query_low_ref, latent_ref,
                             latent_normed_ref, keyvalue_ref, key_rope_ref, weights_ref, mixed_ref,
                             own_ref, *rest):
    *sends, latent_buf, query_buf, keyvalue_buf, output_buf, sems = rest
    copies = [
        pltpu.make_async_copy(source, buffer, sems.at[number])
        for number, (source, buffer) in enumerate((
            (w_latent_ref, latent_buf), (w_query_ref, query_buf), (w_keyvalue_ref, keyvalue_buf),
            (w_output_ref, output_buf),
        ))
    ]
    for copy in copies:
        copy.start()
    tokens = token_ref[...].astype(jnp.float32)
    scale = lax.rsqrt(jnp.mean(tokens * tokens, axis=1, keepdims=True) + EPS)
    scale_ref[...] = scale
    normed = (tokens * scale * gain_ref[...]).astype(jnp.bfloat16)
    normed_ref[...] = normed
    copies[0].wait()
    latent = matmul_nt(normed, latent_buf[...])
    latent_ref[...] = latent
    compressed = latent[:, :KV_RANK]
    latent_scale = lax.rsqrt(jnp.mean(compressed * compressed, axis=1, keepdims=True) + EPS)
    latent_normed = (compressed * latent_scale * latent_gain_ref[...]).astype(jnp.bfloat16)
    latent_normed_ref[...] = latent_normed
    half = ROPE // 2
    former = latent[:, KV_RANK:KV_RANK + half]
    latter = latent[:, KV_RANK + half:]
    key_cosine, key_sine = key_cosine_ref[...], key_sine_ref[...]
    key_rope = jnp.concatenate(
        [former * key_cosine - latter * key_sine, latter * key_cosine + former * key_sine], axis=1
    ).astype(jnp.bfloat16)
    key_rope_ref[...] = key_rope
    copies[1].wait()
    query = matmul(normed, query_buf[...])
    query_ref[...] = query
    wide = query.shape[1]
    query_low_ref[...] = (
        query * cosine_ref[...] + pltpu.roll(query, wide - half, 1) * ahead_ref[...]
        + pltpu.roll(query, half, 1) * behind_ref[...]
    ).astype(jnp.bfloat16)
    copies[2].wait()
    keyvalue_ref[...] = matmul(latent_normed, keyvalue_buf[...]).astype(jnp.bfloat16)
    rows = tokens.shape[0]
    causal = (
        lax.broadcasted_iota(jnp.int32, (rows, rows), 0)
        >= lax.broadcasted_iota(jnp.int32, (rows, rows), 1)
    )
    qk_width = NOPE + ROPE
    for head in range(wide // qk_width):
        low = head * (NOPE + VDIM)
        query_head = query_low_ref[:, head * qk_width:(head + 1) * qk_width]
        key_head = jnp.concatenate([keyvalue_ref[:, low:low + NOPE], key_rope], axis=1)
        scores = matmul_nt(query_head, key_head) * (qk_width ** -0.5)
        scores = jnp.where(causal, scores, MASKED)
        terms = jnp.exp(scores - jnp.max(scores, axis=1, keepdims=True))
        weights = terms / jnp.sum(terms, axis=1, keepdims=True)
        weights_ref[head] = weights
        mixed_ref[:, head * VDIM:(head + 1) * VDIM] = matmul(
            weights.astype(jnp.bfloat16), keyvalue_ref[:, low + NOPE:low + NOPE + VDIM]
        ).astype(jnp.bfloat16)
    copies[3].wait()
    part = own_ref.shape[1]
    count = len(sends) + 1
    for number in range(count):
        value = matmul(mixed_ref[...], output_buf[:, number * part:(number + 1) * part])
        place = lax.rem(number - rank_ref[0] + count, count)

        @pl.when(place == 0)
        def _():
            own_ref[...] = value

        for index, send in enumerate(sends):
            @pl.when(place == index + 1)
            def _():
                send[...] = value.astype(jnp.bfloat16)


def rotary_constants(rows, heads):
    half = ROPE // 2
    frequency = np.float32(THETA) ** (np.arange(half, dtype=np.float32) * np.float32(-2.0 / ROPE))
    angles = np.arange(rows, dtype=np.float32)[:, None] * frequency[None, :]
    cosine, sine = np.cos(angles), np.sin(angles)
    blank = np.zeros((rows, NOPE), np.float32)
    zero = np.zeros((rows, half), np.float32)

    def tiled(*pieces):
        return np.tile(np.concatenate(pieces, axis=1), (1, heads)).astype(np.float32)

    return (
        tiled(blank + 1.0, cosine, cosine), tiled(blank, -sine, zero), tiled(blank, zero, sine),
        cosine, sine,
    )


def full_specs(arrays):
    return [pl.BlockSpec(a.shape, lambda i, r, n=len(a.shape): (0,) * n) for a in arrays]


def attention_forward(rank, tokens, gain, latent_gain, tables, w_latent, w_query, w_keyvalue, w_output,
                      count):
    rows, model = tokens.shape
    part = model // count
    latent_width = w_latent.shape[1]
    query_width = w_query.shape[1]
    heads = query_width // (NOPE + ROPE)
    bf16, f32 = jnp.bfloat16, jnp.float32
    out_shape = [
        jax.ShapeDtypeStruct(shape, kind)
        for shape, kind in (
            ((rows, model), bf16), ((rows, 1), f32), ((rows, query_width), f32),
            ((rows, query_width), bf16), ((rows, latent_width), f32), ((rows, KV_RANK), bf16),
            ((rows, w_keyvalue.shape[1]), bf16), ((rows, ROPE), bf16), ((heads, rows, rows), f32),
            ((rows, heads * VDIM), bf16), ((rows, part), f32),
        ) + (((rows, part), bf16),) * (count - 1)
    ]
    inputs = [tokens, gain.reshape(1, -1), latent_gain.reshape(1, -1), *tables]
    streamed = [w_latent.T, w_query, w_keyvalue, w_output]
    return pl.pallas_call(
        attention_forward_kernel,
        grid_spec=pltpu.PrefetchScalarGridSpec(
            num_scalar_prefetch=1,
            grid=(1,),
            in_specs=full_specs(inputs) + [pl.BlockSpec(memory_space=pl.ANY)] * len(streamed),
            out_specs=full_specs(out_shape),
            scratch_shapes=[pltpu.VMEM(a.shape, a.dtype) for a in streamed]
            + [pltpu.SemaphoreType.DMA((len(streamed),))],
        ),
        out_shape=out_shape,
        compiler_params=pltpu.CompilerParams(vmem_limit_bytes=VMEM_BYTES),
        cost_estimate=pl.CostEstimate(
            flops=5_000_000_000, bytes_accessed=16_000_000, transcendentals=300_000
        ),
        name="attention_forward",
    )(rank.reshape(1), *inputs, *streamed)


def attention_backward_kernel(rank_ref, *refs):
    count = 4
    pieces, refs = refs[:count], refs[count:]
    (weights_ref, keyvalue_ref, key_rope_ref, query_low_ref, query_ref, token_ref, scale_ref, cosine_ref,
     ahead_ref, behind_ref, w_output_ref, w_keyvalue_ref, w_query_ref,
     branch_ref, gain_ref, query_grad_ref, keyvalue_grad_ref, own_ref, latent_ref, *rest) = refs
    *sends, output_buf, keyvalue_buf, query_buf, grad_buf, sems = rest
    copies = [
        pltpu.make_async_copy(source, buffer, sems.at[number])
        for number, (source, buffer) in enumerate((
            (w_output_ref, output_buf), (w_keyvalue_ref, keyvalue_buf), (w_query_ref, query_buf),
        ))
    ]
    for copy in copies:
        copy.start()
    rows, model = branch_ref.shape
    part = own_ref.shape[1]
    for place in range(count):
        columns = slice(place * part, (place + 1) * part)
        turn = lax.rem(rank_ref[0] - place + count, count)
        for number, piece in enumerate(pieces):
            @pl.when(turn == number)
            def _():
                branch_ref[:, columns] = piece[:rows, :]
                sums = piece[rows:, :].astype(jnp.float32)
                gain_ref[:, columns] = sums[0:1] + sums[1:2]
    copies[0].wait()
    mixed_grad = matmul_nt(branch_ref[...], output_buf[...]).astype(jnp.bfloat16)
    qk_width = NOPE + ROPE
    soft = qk_width ** -0.5
    key_rope = key_rope_ref[...]
    rope_grad = jnp.zeros((rows, ROPE), jnp.float32)
    for head in range(weights_ref.shape[0]):
        low = head * (NOPE + VDIM)
        columns = slice(head * qk_width, (head + 1) * qk_width)
        weights = weights_ref[head]
        out_grad = mixed_grad[:, head * VDIM:(head + 1) * VDIM]
        keyvalue_grad_ref[:, low + NOPE:low + NOPE + VDIM] = matmul_tn(
            weights.astype(jnp.bfloat16), out_grad
        ).astype(jnp.bfloat16)
        prob_grad = matmul_nt(out_grad, keyvalue_ref[:, low + NOPE:low + NOPE + VDIM])
        row_term = jnp.sum(weights * prob_grad, axis=1, keepdims=True)
        score_grad = (weights * (prob_grad - row_term)).astype(jnp.bfloat16)
        key_head = jnp.concatenate([keyvalue_ref[:, low:low + NOPE], key_rope], axis=1)
        grad_buf[:, columns] = matmul(score_grad, key_head) * soft
        key_grad = matmul_tn(score_grad, query_low_ref[:, columns]) * soft
        keyvalue_grad_ref[:, low:low + NOPE] = key_grad[:, :NOPE].astype(jnp.bfloat16)
        rope_grad += key_grad[:, NOPE:]
    grad = grad_buf[...]
    wide = grad.shape[1]
    half = ROPE // 2
    query_grad = (
        grad * cosine_ref[...] - pltpu.roll(grad, wide - half, 1) * ahead_ref[...]
        - pltpu.roll(grad, half, 1) * behind_ref[...]
    ).astype(jnp.bfloat16)
    query_grad_ref[...] = query_grad
    mean = jnp.sum(query_grad.astype(jnp.float32) * query_ref[...], axis=1, keepdims=True)
    mean_high = mean.astype(jnp.bfloat16).astype(jnp.float32)
    copies[1].wait()
    latent_part = matmul_nt(keyvalue_grad_ref[...], keyvalue_buf[...])
    width = latent_part.shape[1]
    column = lax.broadcasted_iota(jnp.int32, (rows, LANES - ROPE), 1)
    sums = jnp.where(column == 0, mean_high, jnp.where(column == 1, mean - mean_high, 0.0))
    latent_ref[:rows, :width] = latent_part.astype(jnp.bfloat16)
    latent_ref[:rows, width:] = jnp.concatenate([rope_grad, sums], axis=1).astype(jnp.bfloat16)
    copies[2].wait()
    gains = []
    scale = scale_ref[...]
    for number in range(count):
        columns = slice(number * part, (number + 1) * part)
        value = matmul_nt(query_grad, query_buf[columns, :])
        unit = token_ref[:, columns].astype(jnp.float32) * scale
        gains.append(jnp.sum(value * unit, axis=0, keepdims=True))
        place = lax.rem(number - rank_ref[0] + count, count)

        @pl.when(place == 0)
        def _():
            own_ref[...] = value

        for index, send in enumerate(sends):
            @pl.when(place == index + 1)
            def _():
                send[...] = value.astype(jnp.bfloat16)
    highs = [gain.astype(jnp.bfloat16).astype(jnp.float32) for gain in gains]
    lows = [gain - high for gain, high in zip(gains, highs)]
    spare = latent_ref.shape[0] - rows
    latent_ref[rows:, :width] = jnp.concatenate(
        highs + lows + [jnp.zeros((spare - 2 * count, part), jnp.float32)], axis=0
    ).astype(jnp.bfloat16)
    latent_ref[rows:, width:] = jnp.zeros((spare, LANES), jnp.bfloat16)


def attention_backward(rank, pieces, weights, keyvalue, key_rope, query_low, query, tokens, scale, tables,
                       w_output, w_keyvalue, w_query):
    rows, model = tokens.shape
    count = len(pieces)
    part = model // count
    wide = query.shape[1]
    kv_width = keyvalue.shape[1]
    sent_rows = pieces[0].shape[0]
    bf16, f32 = jnp.bfloat16, jnp.float32
    sent_width = KV_RANK + LANES
    out_shape = [
        jax.ShapeDtypeStruct(shape, kind)
        for shape, kind in (
            ((rows, model), bf16), ((1, model), f32), ((rows, wide), bf16), ((rows, kv_width), bf16),
            ((rows, part), f32), ((sent_rows, sent_width), bf16),
        ) + (((rows, part), bf16),) * (count - 1)
    ]
    inputs = [*pieces, weights, keyvalue, key_rope, query_low, query, tokens, scale, *tables[:3]]
    streamed = [w_output, w_keyvalue, w_query]
    return pl.pallas_call(
        attention_backward_kernel,
        grid_spec=pltpu.PrefetchScalarGridSpec(
            num_scalar_prefetch=1,
            grid=(1,),
            in_specs=full_specs(inputs) + [pl.BlockSpec(memory_space=pl.ANY)] * len(streamed),
            out_specs=full_specs(out_shape),
            scratch_shapes=[pltpu.VMEM(a.shape, a.dtype) for a in streamed]
            + [pltpu.VMEM((rows, wide), f32), pltpu.SemaphoreType.DMA((len(streamed),))],
        ),
        out_shape=out_shape,
        compiler_params=pltpu.CompilerParams(vmem_limit_bytes=VMEM_BYTES),
        cost_estimate=pl.CostEstimate(
            flops=4_000_000_000, bytes_accessed=20_000_000, transcendentals=0
        ),
        name="attention_backward",
    )(rank.reshape(1), *inputs, *streamed)


def single_call(kernel, arrays, shapes, name):
    def specs(values):
        return [pl.BlockSpec(a.shape, lambda i, n=len(a.shape): (0,) * n) for a in values]

    return pl.pallas_call(
        kernel,
        grid=(1,),
        in_specs=specs(arrays),
        out_specs=specs(shapes),
        out_shape=shapes,
        compiler_params=pltpu.CompilerParams(vmem_limit_bytes=VMEM_BYTES),
        cost_estimate=pl.CostEstimate(flops=0, bytes_accessed=4_000_000, transcendentals=0),
        name=name,
    )(*arrays)


def hidden_kernel(own_ref, token_ref, *rest):
    *pieces, hidden_ref, sent_ref = rest
    value = own_ref[...] + token_ref[...].astype(jnp.float32)
    for piece in pieces:
        value = value + piece[...].astype(jnp.float32)
    hidden_ref[...] = value
    part = value.shape[1]
    total = jnp.sum(value * value, axis=1, keepdims=True)
    high = total.astype(jnp.bfloat16).astype(jnp.float32)
    column = lax.broadcasted_iota(jnp.int32, (value.shape[0], LANES), 1)
    sums = jnp.where(column == 0, high, jnp.where(column == 1, total - high, 0.0))
    sent_ref[:, :part] = value.astype(jnp.bfloat16)
    sent_ref[:, part:] = sums.astype(jnp.bfloat16)


def hidden_rows(own, token_block, pieces):
    tokens, part = own.shape
    shapes = [
        jax.ShapeDtypeStruct((tokens, part), jnp.float32),
        jax.ShapeDtypeStruct((tokens, part + LANES), jnp.bfloat16),
    ]
    return single_call(hidden_kernel, [own, token_block, *pieces], shapes, "hidden_rows")


def owner_rows_kernel(first_ref, block_ref, mask_ref, *out_refs):
    sources, rows, _ = block_ref.shape
    _, cap, part = out_refs[0].shape
    experts = len(out_refs)
    line = lax.broadcasted_iota(jnp.int32, (8, LANES), 0)
    column = lax.broadcasted_iota(jnp.int32, (8, LANES), 1)
    select = ((column == line + first_ref[0]) & (line < experts)).astype(jnp.bfloat16)
    earlier = (
        lax.broadcasted_iota(jnp.int32, (rows, rows), 0)
        < lax.broadcasted_iota(jnp.int32, (rows, rows), 1)
    ).astype(jnp.bfloat16)
    slot = lax.broadcasted_iota(jnp.int32, (cap, rows), 0).astype(jnp.float32)
    chosen = jnp.concatenate(
        [matmul_nt(select, block_ref[source, :, part:]) for source in range(sources)], axis=0
    )
    place = matmul(chosen.astype(jnp.bfloat16), earlier)
    for source in range(sources):
        picks = [
            jnp.where((slot == place[line:line + 1]) & (chosen[line:line + 1] > 0.5), 1.0, 0.0)
            for line in range(8 * source, 8 * source + experts)
        ]
        picks = jnp.concatenate(picks, axis=0).astype(jnp.bfloat16)
        out = matmul(picks, block_ref[source]).astype(jnp.bfloat16)
        mask_ref[source] = out[:, part:].reshape(experts, cap, LANES)
        for number, out_ref in enumerate(out_refs):
            out_ref[source] = out[number * cap:(number + 1) * cap, :part]


def owner_rows(first, gathered, experts, cap):
    groups, rows, wide = gathered.shape
    part = wide - LANES
    step = 8
    return pl.pallas_call(
        owner_rows_kernel,
        grid_spec=pltpu.PrefetchScalarGridSpec(
            num_scalar_prefetch=1,
            grid=(groups // step,),
            in_specs=[pl.BlockSpec((step, rows, wide), lambda i, f: (i, 0, 0))],
            out_specs=[pl.BlockSpec((step, experts, cap, LANES), lambda i, f: (i, 0, 0, 0))]
            + [pl.BlockSpec((step, cap, part), lambda i, f: (i, 0, 0))] * experts,
        ),
        out_shape=[jax.ShapeDtypeStruct((groups, experts, cap, LANES), jnp.bfloat16)]
        + [jax.ShapeDtypeStruct((groups, cap, part), jnp.bfloat16)] * experts,
        compiler_params=pltpu.CompilerParams(vmem_limit_bytes=VMEM_BYTES),
        cost_estimate=pl.CostEstimate(
            flops=2 * groups * experts * cap * rows * part, bytes_accessed=13_000_000,
            transcendentals=0,
        ),
        name="owner_rows",
    )(first, gathered)


def route_rows_kernel(rank_ref, dispatch_ref, gain_ref, router_ref, *rest):
    pieces, (rows_ref, wide_ref, logit_ref, scale_ref) = rest[:-4], rest[-4:]
    count = len(pieces)
    part = pieces[0].shape[1] - LANES
    model = count * part

    @pl.when(pl.program_id(0) == 0)
    def _():
        total = sum(jnp.sum(piece[:, part:].astype(jnp.float32), axis=1, keepdims=True)
                    for piece in pieces)
        scale = lax.rsqrt(total / model + EPS)
        scale_ref[...] = scale
        logits = jnp.zeros(logit_ref.shape, jnp.float32)
        for place in range(count):
            turn = lax.rem(rank_ref[0] - place + count, count)
            block = pieces[0][:, :part].astype(jnp.float32)
            for number in range(1, count):
                block = jnp.where(turn == number, pieces[number][:, :part].astype(jnp.float32),
                                  block)
            columns = slice(place * part, (place + 1) * part)
            block = (block * scale * gain_ref[:, columns]).astype(jnp.bfloat16)
            wide_ref[:, columns] = block
            logits += matmul(block, router_ref[columns, :])
        logit_ref[...] = logits

    rows_ref[...] = matmul(dispatch_ref[...], wide_ref[...]).astype(jnp.bfloat16)


def route_rows(rank, dispatch, gain, router, pieces):
    slots, tokens = dispatch.shape
    model, experts = router.shape
    block = 256

    def whole(*shape):
        return pl.BlockSpec(shape, lambda i, r: (0, 0))

    return pl.pallas_call(
        route_rows_kernel,
        grid_spec=pltpu.PrefetchScalarGridSpec(
            num_scalar_prefetch=1,
            grid=(slots // block,),
            in_specs=[
                pl.BlockSpec((block, tokens), lambda i, r: (i, 0)),
                whole(1, model), whole(model, experts),
            ] + [whole(*piece.shape) for piece in pieces],
            out_specs=[
                pl.BlockSpec((block, model), lambda i, r: (i, 0)),
                whole(tokens, model), whole(tokens, experts), whole(tokens, 1),
            ],
        ),
        out_shape=[
            jax.ShapeDtypeStruct((slots, model), jnp.bfloat16),
            jax.ShapeDtypeStruct((tokens, model), jnp.bfloat16),
            jax.ShapeDtypeStruct((tokens, experts), jnp.float32),
            jax.ShapeDtypeStruct((tokens, 1), jnp.float32),
        ],
        compiler_params=pltpu.CompilerParams(vmem_limit_bytes=VMEM_BYTES),
        cost_estimate=pl.CostEstimate(
            flops=2 * slots * tokens * model, bytes_accessed=13_000_000, transcendentals=0
        ),
        name="route_rows",
    )(rank.reshape(1), dispatch, gain.reshape(1, model), router, *pieces)


def norm_back_kernel(own_ref, extra_ref, pick_ref, back_ref, mask_ref, logit_ref, scale_ref, hidden_ref,
                     gain_ref, router_ref, cotangent_ref, *rest):
    *pieces, grad_ref, sent_ref, logit_grad_ref = rest
    part = own_ref.shape[1]
    rows, experts = mask_ref.shape
    model = part * (len(pieces) + 1)
    gathered = matmul(pick_ref[...], back_ref[...])
    norm_grad = own_ref[...] + gathered[:, :part]
    extra = extra_ref[...].astype(jnp.float32) + gathered[:, part:]
    for piece in pieces:
        norm_grad = norm_grad + piece[:, :part].astype(jnp.float32)
        extra = extra + piece[:, part:].astype(jnp.float32)
    logits = logit_ref[...]
    sigmas = mask_ref[...] / (1.0 + jnp.exp(-logits))
    total = jnp.sum(sigmas, axis=1, keepdims=True)
    gate_grad = extra[:, :experts]
    weighted_sum = jnp.sum(gate_grad * sigmas, axis=1, keepdims=True)
    sigma_grad = ROUTE_SCALE * (gate_grad / total - weighted_sum / (total * total))
    logit_grad = (sigma_grad * sigmas * (1.0 - sigmas)).astype(jnp.bfloat16)
    logit_grad_ref[...] = logit_grad
    norm_grad = norm_grad + matmul_nt(logit_grad, router_ref[...])
    mean = (
        jnp.sum(extra[:, experts:experts + 2], axis=1, keepdims=True)
        + jnp.sum(logit_grad.astype(jnp.float32) * logits, axis=1, keepdims=True)
    ) / model
    scale = scale_ref[...]
    unit = hidden_ref[...] * scale
    gain_grad = jnp.sum(norm_grad * unit, axis=0, keepdims=True)
    grad = cotangent_ref[...].astype(jnp.float32) + scale * (norm_grad * gain_ref[...] - unit * mean)
    grad_ref[...] = grad
    sent_ref[:rows, :] = grad.astype(jnp.bfloat16)
    high = gain_grad.astype(jnp.bfloat16).astype(jnp.float32)
    row = lax.broadcasted_iota(jnp.int32, (sent_ref.shape[0] - rows, part), 0)
    sums = jnp.where(row == 0, high, jnp.where(row == 1, gain_grad - high, 0.0))
    sent_ref[rows:, :] = sums.astype(jnp.bfloat16)


def norm_back(own, extra, pick, back, mask, logits, scale, hidden, gain, router, cotangent, pieces):
    rows, part = own.shape
    bf16, f32 = jnp.bfloat16, jnp.float32
    shapes = [
        jax.ShapeDtypeStruct((rows, part), f32), jax.ShapeDtypeStruct((rows + 16, part), bf16),
        jax.ShapeDtypeStruct(mask.shape, bf16),
    ]
    inputs = [own, extra, pick, back, mask, logits, scale, hidden, gain.reshape(1, part), router, cotangent]
    return single_call(norm_back_kernel, inputs + list(pieces), shapes, "norm_back")


def put_pairs(first, grad, row, column, mine_ref, other_ref):
    rows = slice(row, row + grad.shape[2])
    columns = slice(column, column + grad.shape[3])
    even, odd = grad[:, 0], grad[:, 1]
    mine_ref[:, rows, columns] = jnp.where(first, even, odd).astype(jnp.bfloat16)
    other_ref[:, rows, columns] = jnp.where(first, odd, even).astype(jnp.bfloat16)


def branch_weights_kernel(core_ref, n_ref, b_ref, l_ref, query_ref, mixed_ref, kv_ref, mine_ref, other_ref):
    pairs, chunk, _ = mine_ref.shape
    first = core_ref[0] == 0

    def by_pairs(grad):
        return grad.reshape(pairs, 2, grad.shape[0] // (2 * pairs), grad.shape[1])

    low = 0
    for rows_ref, grads in ((n_ref, query_ref), (b_ref, mixed_ref)):
        grad = matmul_tn(rows_ref[...], grads[...])
        put_pairs(first, by_pairs(grad), 0, low, mine_ref, other_ref)
        low += grad.shape[1]
    grad = by_pairs(matmul_tn(l_ref[...], kv_ref[...]))
    kv_chunk = grad.shape[2]
    columns = grad.shape[3] * kv_chunk // chunk
    for place in range(chunk // kv_chunk):
        put_pairs(first, grad[:, :, :, place * columns:(place + 1) * columns], place * kv_chunk, low,
                  mine_ref, other_ref)


def paired_call(kernel, core, groups, columns, blocked, whole, extra_shapes, scratch, name):
    steps = 4
    model = blocked[0].shape[1]
    chunk = model // groups
    out = pl.BlockSpec((groups // 2 // steps, chunk, columns), lambda i, c: (i, 0, 0))

    def fixed(array):
        return pl.BlockSpec(array.shape, lambda i, c: (0, 0))

    return pl.pallas_call(
        kernel,
        grid_spec=pltpu.PrefetchScalarGridSpec(
            num_scalar_prefetch=1,
            grid=(steps,),
            in_specs=[
                pl.BlockSpec((a.shape[0], a.shape[1] // steps), lambda i, c: (0, i)) for a in blocked
            ] + [fixed(a) for a in whole],
            out_specs=[fixed(a) for a in extra_shapes] + [out] * 2,
            scratch_shapes=scratch,
        ),
        out_shape=list(extra_shapes)
        + [jax.ShapeDtypeStruct((groups // 2, chunk, columns), jnp.bfloat16)] * 2,
        compiler_params=pltpu.CompilerParams(vmem_limit_bytes=VMEM_BYTES),
        cost_estimate=pl.CostEstimate(flops=0, bytes_accessed=10_000_000, transcendentals=0),
        name=name,
    )(core.reshape(1), *blocked, *whole)


def branch_weights(core, groups, normed, branch, latent_normed, query, mixed, kv):
    columns = (
        query.shape[1] + mixed.shape[1] + kv.shape[1] * latent_normed.shape[1] // normed.shape[1]
    )
    return paired_call(
        branch_weights_kernel, core, groups, columns, [normed, branch, latent_normed],
        [query, mixed, kv], [], [], "branch_weights",
    )


def latent_weights_kernel(core_ref, n_ref, t_ref, token_ref, w_latent_ref, ffn_ref, logit_ref, latent_ref,
                          latent_gain_ref, cosine_ref, sine_ref, scale_ref, *rest):
    *pieces, latent_grad_ref, mean_ref, mine_ref, other_ref, gain_buf, latent_gain_buf = rest
    step = pl.program_id(0)
    count = len(pieces)
    pairs, chunk, _ = mine_ref.shape
    rows = latent_ref.shape[0]
    block = n_ref.shape[1]
    first = core_ref[0] == 0

    @pl.when(step == 0)
    def _():
        total = sum(piece[...].astype(jnp.float32) for piece in pieces)
        for number in range(count):
            gain_buf[number] = (
                total[rows + number:rows + number + 1, :block]
                + total[rows + count + number:rows + count + number + 1, :block]
            )
        latent = latent_ref[...]
        compressed = latent[:, :KV_RANK]
        scale = lax.rsqrt(jnp.mean(compressed * compressed, axis=1, keepdims=True) + EPS)
        unit = compressed * scale
        grad = total[:rows, :KV_RANK]
        gains = jnp.sum(grad * unit, axis=0, keepdims=True)
        width = KV_RANK // count
        for number in range(count):
            latent_gain_buf[number] = gains[:, number * width:(number + 1) * width]
        grad = grad * latent_gain_ref[...]
        grad = scale * (grad - unit * jnp.mean(unit * grad, axis=1, keepdims=True))
        half = ROPE // 2
        former = total[:rows, KV_RANK:KV_RANK + half]
        latter = total[:rows, KV_RANK + half:KV_RANK + ROPE]
        cosine, sine = cosine_ref[...], sine_ref[...]
        latent_grad = jnp.concatenate(
            [grad, former * cosine + latter * sine, latter * cosine - former * sine], axis=1
        ).astype(jnp.bfloat16)
        latent_grad_ref[...] = latent_grad
        sums = total[:rows, KV_RANK + ROPE:KV_RANK + ROPE + 2]
        mean_ref[...] = (
            jnp.sum(sums, axis=1, keepdims=True)
            + jnp.sum(latent_grad.astype(jnp.float32) * latent, axis=1, keepdims=True)
        ) / (block * count)

    def by_pairs(grad):
        return grad.reshape(pairs, 2, grad.shape[0] // (2 * pairs), grad.shape[1])

    low = 0
    for rows_ref, grads in ((n_ref, latent_grad_ref), (t_ref, logit_ref)):
        grad = matmul_tn(rows_ref[...], grads[...])
        put_pairs(first, by_pairs(grad), 0, low, mine_ref, other_ref)
        low += grad.shape[1]
    unit = token_ref[...].astype(jnp.float32) * scale_ref[...]
    routed = matmul(latent_grad_ref[...], w_latent_ref[...])
    gain = gain_buf[step] + jnp.sum(routed * unit, axis=0, keepdims=True)
    line = lax.broadcasted_iota(jnp.int32, (LANES, block), 0)
    gains = by_pairs(jnp.where(line == 0, gain, jnp.where(line == 1, ffn_ref[...], 0.0)).T)
    width = latent_gain_buf.shape[2]
    kv_chunk = width // (2 * pairs)
    line = lax.broadcasted_iota(jnp.int32, (LANES, width), 0)
    more = by_pairs(jnp.where(line == 2, latent_gain_buf[step], 0.0).T)
    gains = jnp.concatenate([gains[:, :, :kv_chunk] + more, gains[:, :, kv_chunk:]], axis=2)
    put_pairs(first, gains, 0, low, mine_ref, other_ref)


def latent_weights(core, groups, normed, normed_two, tokens, w_latent, ffn_gain, logit, latent, latent_gain,
                   cosine, sine, scale, pieces):
    count = len(pieces)
    shapes = [
        jax.ShapeDtypeStruct(latent.shape, jnp.bfloat16),
        jax.ShapeDtypeStruct(scale.shape, jnp.float32),
    ]
    scratch = [
        pltpu.VMEM((count, 1, normed.shape[1] // count), jnp.float32),
        pltpu.VMEM((count, 1, KV_RANK // count), jnp.float32),
    ]
    return paired_call(
        latent_weights_kernel, core, groups, latent.shape[1] + logit.shape[1] + LANES,
        [normed, normed_two, tokens, w_latent.T, ffn_gain],
        [logit, latent, latent_gain.reshape(1, -1), cosine, sine, scale, *pieces], shapes, scratch,
        "latent_weights",
    )


def pair_kernel(mine_ref, got_ref, *rest):
    rest[-1][...] = (
        mine_ref[...].astype(jnp.float32) + got_ref[...].astype(jnp.float32)
    ).astype(jnp.bfloat16)


def pair_sum(mine, got, columns, place, whole=None):
    chips, rows, width = mine.shape
    steps = 4
    block = pl.BlockSpec((chips // steps, rows, width), lambda i: (i, 0, 0))
    before = () if whole is None else (whole,)
    return pl.pallas_call(
        pair_kernel,
        grid=(steps,),
        in_specs=[block, block] + [pl.BlockSpec(memory_space=pl.ANY)] * len(before),
        out_specs=pl.BlockSpec((chips // steps, rows, width), lambda i: (i, 0, place)),
        out_shape=jax.ShapeDtypeStruct((chips, rows, columns), jnp.bfloat16),
        input_output_aliases={2: 0} if before else {},
        compiler_params=pltpu.CompilerParams(vmem_limit_bytes=VMEM_BYTES),
        cost_estimate=pl.CostEstimate(flops=0, bytes_accessed=14_000_000, transcendentals=0),
        name="pair_sum",
    )(mine, got, *before)


def final_kernel(edges, part_ref, query_ref, output_ref, kv_ref, latent_ref, router_ref, gain_ref,
                 total_ref):
    step = pl.program_id(0)

    @pl.when(step == 0)
    def _():
        total_ref[...] = jnp.zeros_like(total_ref)

    total = total_ref[...]
    for number in range(part_ref.shape[0]):
        total = total + part_ref[number].astype(jnp.float32)
    total_ref[...] = total

    @pl.when(step == pl.num_programs(0) - 1)
    def _():
        outs = (query_ref, output_ref, kv_ref, latent_ref, router_ref)
        for out, low, high in zip(outs, edges[:5], edges[1:6]):
            if out is not kv_ref:
                out[...] = total_ref[:, low:high]
                continue
            chunk = out.shape[0]
            for place in range(total_ref.shape[0] // chunk):
                out[:, place * (high - low):(place + 1) * (high - low)] = (
                    total_ref[place * chunk:(place + 1) * chunk, low:high]
                )
        gain_ref[...] = total_ref[:, edges[5]:].T


def final_sums(parts, edges, shapes):
    chips, rows, columns = parts.shape
    step = 4
    return pl.pallas_call(
        functools.partial(final_kernel, edges),
        grid=(chips // step,),
        in_specs=[pl.BlockSpec((step, rows, columns), lambda i: (i, 0, 0))],
        out_specs=[pl.BlockSpec(a.shape, lambda i: (0, 0)) for a in shapes],
        out_shape=shapes,
        scratch_shapes=[pltpu.VMEM((rows, columns), jnp.float32)],
        compiler_params=pltpu.CompilerParams(vmem_limit_bytes=VMEM_BYTES),
        cost_estimate=pl.CostEstimate(flops=0, bytes_accessed=6_000_000, transcendentals=0),
        name="final_sums",
    )(parts)


def ordered_kernel(rank_ref, *refs):
    *pieces, out_ref = refs
    count = len(pieces)
    part = pieces[0].shape[1]
    for place in range(count):
        turn = lax.rem(rank_ref[0] - place + count, count)
        for number, piece in enumerate(pieces):
            @pl.when(turn == number)
            def _():
                out_ref[:, place * part:(place + 1) * part] = piece[...]


def ordered_columns(rank, pieces):
    rows, part = pieces[0].shape
    shape = jax.ShapeDtypeStruct((rows, part * len(pieces)), pieces[0].dtype)
    return pl.pallas_call(
        ordered_kernel,
        grid_spec=pltpu.PrefetchScalarGridSpec(
            num_scalar_prefetch=1, grid=(1,), in_specs=full_specs(pieces),
            out_specs=full_specs([shape])[0],
        ),
        out_shape=shape,
        compiler_params=pltpu.CompilerParams(vmem_limit_bytes=VMEM_BYTES),
        cost_estimate=pl.CostEstimate(flops=0, bytes_accessed=2_000_000, transcendentals=0),
        name="ordered_columns",
    )(rank.reshape(1), *pieces)


def swap_cores(rows, groups):
    return lax.ppermute(rows, "expert", [(index, index ^ 1) for index in range(groups)])


def shards(
    tokens,
    cotangent,
    attn_gain,
    w_query,
    w_latent,
    latent_gain,
    w_keyvalue,
    w_output,
    ffn_gain,
    w_router,
    shared_gate,
    shared_up,
    shared_down,
    expert_gate,
    expert_up,
    expert_down,
    routes,
):
    bf16 = jnp.bfloat16
    f32 = jnp.float32
    tok_rows, model_width = tokens.shape
    top_count = routes.shape[1]
    expert_count = w_router.shape[1]
    local_experts, _, hidden_width = expert_gate.shape
    groups = lax.axis_size("expert")
    ranks = lax.axis_size("tensor")
    rank = lax.axis_index("tensor")
    group = lax.axis_index("expert")
    part = model_width // ranks
    capacity = (4 * tok_rows * top_count + 3 * expert_count - 1) // (3 * expert_count)
    slot_count = expert_count * capacity
    per_group = local_experts * capacity
    qk_width = NOPE + ROPE
    local_heads = w_query.shape[1] // qk_width

    expert_ids = jnp.arange(expert_count, dtype=jnp.int32)
    selector = routes[:, :, None] == expert_ids[None, None, :]
    chosen_mask = jnp.sum(selector.astype(f32), axis=1)

    cotangent_part = column_block(cotangent, rank, part)
    chosen_low = jnp.pad(chosen_mask.astype(bf16), ((0, 0), (0, LANES - expert_count)))
    all_grads = lax.all_gather(
        jnp.concatenate([cotangent_part, chosen_low], axis=1), "expert", axis=0
    )

    tables = rotary_constants(tok_rows, local_heads)
    (normed, scale_one, query_pre, query_low, latent, latent_normed, keyvalue, key_rope, weights_full,
     attn_mixed, attended, *sends) = attention_forward(
        rank, tokens, attn_gain, latent_gain, tables, w_latent, w_query, w_keyvalue, w_output, ranks
    )

    token_ids = jnp.arange(tok_rows, dtype=jnp.int32)
    before = (token_ids[:, None] > token_ids[None, :]).astype(bf16)
    earlier = matmul(before, after(chosen_mask, attended).astype(bf16))
    place = jnp.sum(jnp.where(selector, earlier[:, None, :], 0.0), axis=-1).astype(jnp.int32)
    expert_place = lax.rem(routes, local_experts) * groups + routes // local_experts
    slot_ids = jnp.arange(slot_count, dtype=jnp.int32)

    def one_hot(target, sideways):
        shape = (tok_rows, slot_count) if sideways else (slot_count, tok_rows)
        found = jnp.zeros(shape, jnp.bool_)
        for choice in range(top_count):
            if sideways:
                found = found | (target[:, choice][:, None] == slot_ids[None, :])
            else:
                found = found | (slot_ids[:, None] == target[:, choice][None, :])
        return found.astype(bf16)

    dispatch = one_hot(routes * capacity + place, False)
    by_expert = one_hot(expert_place * capacity + place, True)
    by_expert = by_expert.reshape(tok_rows, local_experts, groups * capacity)

    sends = [shift_ranks(sent, step + 1, ranks) for step, sent in enumerate(sends)]
    hidden_part, sent = hidden_rows(attended, column_block(tokens, rank, part), sends)
    first = (group * local_experts).reshape(1)
    pieces = [sent] + [shift_ranks(sent, step, ranks) for step in range(1, ranks)]

    rows_sent, normed_two, logits, scale_two = route_rows(
        rank, dispatch, ffn_gain, w_router, pieces
    )
    unit_two_part = hidden_part * scale_two
    sigmas = jax.nn.sigmoid(logits) * chosen_mask
    sigma_total = jnp.sum(sigmas, axis=-1, keepdims=True)
    arrived = lax.all_to_all(
        rows_sent.reshape(groups, per_group, -1), "expert", split_axis=0, concat_axis=0, tiled=True
    )
    chosen_rows, *grad_quarters = owner_rows(
        first, after(all_grads, normed_two), local_experts, capacity
    )
    grads_arrived = [lax.all_gather(rows, "tensor", axis=0) for rows in grad_quarters]

    shared_gate_pre = matmul(normed_two, shared_gate)
    shared_up_pre = matmul(normed_two, shared_up)
    shared_act = (jax.nn.silu(shared_gate_pre) * shared_up_pre).astype(bf16)
    shared_part = matmul(shared_act, shared_down)
    grad_shared_act = matmul_nt(cotangent, shared_down)
    shared_gate_grad, shared_up_grad = silu_back(grad_shared_act, shared_gate_pre, shared_up_pre)
    norm_part = matmul_nt(shared_gate_grad, shared_gate) + matmul_nt(shared_up_grad, shared_up)
    shared_dot = jnp.sum(
        shared_gate_grad.astype(f32) * shared_gate_pre + shared_up_grad.astype(f32) * shared_up_pre,
        axis=-1, keepdims=True,
    )
    shared_grads = shared_weights(
        normed_two, cotangent, shared_gate_grad, shared_up_grad, shared_act, groups
    )

    width = -(-hidden_width // LANES) * LANES
    widen = ((0, 0), (0, 0), (0, width - hidden_width))
    gate_up = jnp.concatenate([jnp.pad(expert_gate, widen), jnp.pad(expert_up, widen)], axis=2)
    down = jnp.pad(expert_down, ((0, 0), (0, width - hidden_width), (0, 0)))
    gate_up_t = gate_up.transpose(0, 2, 1)
    down_t = down.transpose(0, 2, 1)
    weights = (gate_up, gate_up_t, down, down_t)
    arrived = after(
        arrived, shared_grads, shared_part, norm_part, shared_dot, by_expert, *weights
    ).reshape(groups, local_experts, capacity, -1)
    pre_grad, act_weighted, back = expert_rows(
        0, first, arrived, chosen_rows, w_router, grads_arrived[0], weights, True
    )
    back = lax.psum_scatter(back, "tensor", scatter_dimension=0, tiled=True)[0]
    next_grad, next_weighted, direct, next_produced = expert_rows(
        1, first, arrived, chosen_rows, w_router, grads_arrived[1], weights, False
    )
    direct = lax.all_to_all(direct, "expert", split_axis=0, concat_axis=0, tiled=True)
    weight_grads = expert_weights(
        1, arrived, grads_arrived[1], next_grad, next_weighted, hidden_width
    )
    weight_grads = expert_weights(
        0, arrived, grads_arrived[0], pre_grad, act_weighted, hidden_width, weight_grads
    )
    direct = after(direct, *weight_grads).reshape(groups * capacity, -1)
    grad_expert_gate, grad_expert_up, grad_expert_down = weight_grads
    outputs_sent = jnp.concatenate([next_produced, back[:, :, part + LANES:]], axis=2)
    back = lax.all_to_all(
        after(back[:, :, :part + LANES], direct), "expert", split_axis=0, concat_axis=0, tiled=True
    ).reshape(groups * capacity, -1)

    norm_grad, extra_low, *sends = combine_rows(
        rank, by_expert[:, 1], direct, norm_part, shared_dot, ranks
    )
    norm_pieces = [shift_ranks(sent, step + 1, ranks) for step, sent in enumerate(sends)]
    router_rows = lax.dynamic_slice_in_dim(w_router, rank * part, part, axis=0)
    ffn_gain_part = lax.dynamic_slice_in_dim(ffn_gain, rank * part, part, axis=0)
    hidden_grad, sent, logit_grad = norm_back(
        norm_grad, extra_low, by_expert[:, 0], back, chosen_mask, logits, scale_two, hidden_part,
        ffn_gain_part, router_rows, cotangent_part, norm_pieces,
    )
    pieces = [sent] + [shift_ranks(sent, step, ranks) for step in range(1, ranks)]

    (branch_low, grad_ffn_gain, query_pre_grad, keyvalue_grad, normed_grad, latent_sent,
     *sends) = attention_backward(
        rank, pieces, weights_full, keyvalue, key_rope, query_low, query_pre, tokens, scale_one, tables,
        w_output, w_keyvalue, w_query,
    )
    pieces = [latent_sent] + [shift_ranks(latent_sent, step, ranks) for step in range(1, ranks)]
    normed_pieces = [
        shift_ranks(after(sent, *pieces), step + 1, ranks) for step, sent in enumerate(sends)
    ]

    returned = lax.all_to_all(
        after(outputs_sent, back, *norm_pieces), "expert", split_axis=0, concat_axis=0, tiled=True
    ).reshape(groups * capacity, -1)
    latent_sent = after(latent_sent, returned)

    chunk = model_width // groups
    kv_chunk = KV_RANK // groups
    core = lax.rem(group, 2)
    mine, other = branch_weights(
        core, groups, normed, branch_low, latent_normed, query_pre_grad, attn_mixed, keyvalue_grad
    )
    late_columns = mine.shape[2] + w_latent.shape[1] + expert_count + LANES
    late = pair_sum(mine, swap_cores(other, groups), late_columns, 0)
    latent_grad, row_mean, mine, other = latent_weights(
        core, groups, normed, normed_two, tokens, w_latent, grad_ffn_gain, logit_grad, latent,
        latent_gain, tables[3], tables[4], scale_one, pieces,
    )
    shared_width = shared_gate.shape[1]
    early = lax.psum_scatter(
        after(shared_grads, direct).reshape(groups * 3 * chunk, shared_width), "expert",
        scatter_dimension=0, tiled=True,
    )
    branch, *sends = branch_rows(rank, by_expert[:, 1], after(returned, mine), shared_part, ranks)
    late = pair_sum(
        after(mine, branch), swap_cores(after(other, returned), groups), late_columns,
        2, late,
    )
    late = lax.all_to_all(
        late, "expert", split_axis=0, concat_axis=0, tiled=True,
        axis_index_groups=[list(range(first_core, groups, 2)) for first_core in range(2)],
    )

    latent_rows = lax.dynamic_slice_in_dim(w_latent, rank * part, part, axis=0)
    attn_gain_part = lax.dynamic_slice_in_dim(attn_gain, rank * part, part, axis=0)
    block = jax.ShapeDtypeStruct((tok_rows, part), bf16)
    grad_tokens = single_call(
        token_kernel,
        [normed_grad, latent_grad, latent_rows, row_mean, column_block(tokens, rank, part), scale_one,
         attn_gain_part.reshape(1, part), hidden_grad, *normed_pieces],
        [block], "token_rows",
    )[0]
    grad_tokens = ordered_columns(
        rank, [grad_tokens] + [shift_ranks(grad_tokens, step, ranks) for step in range(1, ranks)]
    )
    sends = [shift_ranks(sent, step + 1, ranks) for step, sent in enumerate(sends)]
    output = single_call(
        output_kernel, [branch, hidden_part, by_expert[:, 0], returned[:, model_width:], *sends],
        [block], "output_rows",
    )[0]
    output = ordered_columns(
        rank, [output] + [shift_ranks(output, step, ranks) for step in range(1, ranks)]
    )

    early = early.astype(f32)
    grad_shared_gate = early[:chunk]
    grad_shared_up = early[chunk:2 * chunk]
    grad_shared_down = early[2 * chunk:].T

    edges = [0]
    for columns in (
        query_pre_grad.shape[1], attn_mixed.shape[1],
        keyvalue_grad.shape[1] * KV_RANK // model_width, latent_grad.shape[1], expert_count, LANES,
    ):
        edges.append(edges[-1] + columns)
    shapes = [
        jax.ShapeDtypeStruct((chunk, high - low), f32) for low, high in zip(edges[:-1], edges[1:])
    ]
    shapes[2] = jax.ShapeDtypeStruct((kv_chunk, keyvalue_grad.shape[1]), f32)
    shapes[5] = jax.ShapeDtypeStruct((LANES, chunk), f32)
    grad_query, grad_output, grad_keyvalue, grad_latent, grad_router, gains = final_sums(
        after(late, grad_shared_gate, grad_shared_up, grad_shared_down), tuple(edges), shapes
    )
    return (
        output,
        grad_tokens,
        gains[0],
        grad_query,
        grad_latent,
        gains[2, :kv_chunk],
        grad_keyvalue,
        grad_output.T,
        gains[1],
        grad_router,
        grad_shared_gate,
        grad_shared_up,
        grad_shared_down,
        grad_expert_gate.transpose(0, 2, 1),
        grad_expert_up.transpose(0, 2, 1),
        grad_expert_down,
    )


def solution(mesh):
    return jax.shard_map(
        shards,
        mesh=mesh,
        in_specs=(
            P("expert", None),
            P("expert", None),
            P(),
            P(None, "tensor"),
            P(),
            P(),
            P(None, "tensor"),
            P("tensor", None),
            P(),
            P(),
            P(None, "tensor"),
            P(None, "tensor"),
            P("tensor", None),
            P("expert", None, "tensor"),
            P("expert", None, "tensor"),
            P("expert", "tensor", None),
            P("expert", None),
        ),
        out_specs=(
            P("expert", None),
            P("expert", None),
            P("expert"),
            P("expert", "tensor"),
            P("expert", None),
            P("expert"),
            P("expert", "tensor"),
            P("tensor", "expert"),
            P("expert"),
            P("expert", None),
            P("expert", "tensor"),
            P("expert", "tensor"),
            P("tensor", "expert"),
            P("expert", None, "tensor"),
            P("expert", None, "tensor"),
            P("expert", "tensor", None),
        ),
        check_vma=False,
    )
```

```python
import functools

import jax
import jax.numpy as jnp
import numpy as np
from jax import lax
from jax.experimental import pallas as pl
from jax.experimental.pallas import tpu as pltpu
from jax.sharding import PartitionSpec as P

NOPE = 128
ROPE = 64
VDIM = 128
KV_RANK = 512


EPS = 1e-06
THETA = 50000.0
ROUTE_SCALE = 2.446
MASKED = -1e30
LANES = 128
VMEM_BYTES = 60 * 1024 * 1024


def silu_back(grad_act, gate_pre, up_pre):
    sigma_gate = jax.nn.sigmoid(gate_pre)
    grad_up = grad_act * gate_pre * sigma_gate
    grad_gate = grad_act * up_pre * sigma_gate * (1.0 + gate_pre * (1.0 - sigma_gate))
    return (grad_gate.astype(jnp.bfloat16), grad_up.astype(jnp.bfloat16))


def matmul(left_side, right_side):
    return jnp.dot(left_side, right_side, preferred_element_type=jnp.float32)


def matmul_tn(left_side, right_side):
    return lax.dot_general(
        left_side, right_side, (((0,), (0,)), ((), ())), preferred_element_type=jnp.float32
    )


def matmul_nt(left_side, right_side):
    return lax.dot_general(
        left_side, right_side, (((1,), (1,)), ((), ())), preferred_element_type=jnp.float32
    )


def after(value, *others):
    return lax.optimization_barrier((value,) + others)[0]


def shift_ranks(values, step, count):
    return lax.ppermute(values, "tensor", [(i, (i + step) % count) for i in range(count)])


def column_block(values, index, width):
    return lax.dynamic_slice_in_dim(values, index * width, width, axis=1)


def expert_rows_kernel(sideways, first_ref, x_ref, mask_ref, router_ref, g_ref, wgu_ref, wd_ref, *rest):
    dgu_ref, actw_ref, rowgrad_ref = rest[:3]
    quarters, step, cap, part = g_ref.shape
    rows = step * cap
    width, model = wd_ref.shape
    half = LANES // 2
    expert = first_ref[0]
    experts = router_ref.shape[1]
    x_rows = x_ref[...].reshape(rows, model)
    mask = mask_ref[...].reshape(rows, LANES)[:, :experts].astype(jnp.float32)
    sigmas = mask / (1.0 + jnp.exp(-matmul(x_rows, router_ref[...])))
    total = jnp.sum(sigmas, axis=1, keepdims=True)
    column = lax.broadcasted_iota(jnp.int32, sigmas.shape, 1)
    own = jnp.sum(jnp.where(column == expert, sigmas, 0.0), axis=1, keepdims=True)
    weight = jnp.where(total > 0.0, ROUTE_SCALE * own / jnp.where(total > 0.0, total, 1.0), 0.0)
    column = lax.broadcasted_iota(jnp.int32, (rows, LANES), 1)

    pre = matmul_nt(x_rows, wgu_ref[...])
    grad_act = matmul_nt(g_ref[0].reshape(rows, part), wd_ref[:, :part])
    for place in range(1, quarters):
        grad_act += matmul_nt(
            g_ref[place].reshape(rows, part), wd_ref[:, place * part:(place + 1) * part]
        )
    gate_pre = pre[:, :width]
    up_pre = pre[:, width:]
    sigma = 1.0 / (1.0 + jnp.exp(-gate_pre))
    silu = gate_pre * sigma
    act = silu * up_pre
    act_weighted = (act * weight).astype(jnp.bfloat16)
    actw_ref[...] = act_weighted
    out = matmul(act_weighted, wd_ref[...]).astype(jnp.bfloat16)
    if sideways:
        for place in range(quarters):
            rowgrad_ref[place, :, :, part + LANES:] = (
                out[:, place * part:(place + 1) * part].reshape(step, cap, part)
            )
    else:
        rest[3][...] = out.reshape(step, cap, model)
    dot = jnp.sum(grad_act * act, axis=1, keepdims=True)
    grad_act = grad_act * weight
    grad_up = grad_act * silu
    grad_gate = grad_act * up_pre * (sigma + silu * (1.0 - sigma))
    row_dot = jnp.sum(grad_gate * gate_pre + grad_up * up_pre, axis=1, keepdims=True)
    row_dot_high = row_dot.astype(jnp.bfloat16).astype(jnp.float32)
    pre_grad = jnp.concatenate([grad_gate, grad_up], axis=1).astype(jnp.bfloat16)
    dgu_ref[...] = pre_grad
    row_grad = matmul(pre_grad, wgu_ref[...]).astype(jnp.bfloat16)
    sums = jnp.where(column == expert, dot, 0.0)
    sums = jnp.where(column == half, row_dot_high, sums)
    sums = jnp.where(column == half + 1, row_dot - row_dot_high, sums)
    sums = sums.astype(jnp.bfloat16).reshape(step, cap, LANES)
    if sideways:
        for place in range(quarters):
            rowgrad_ref[place, :, :, :part] = (
                row_grad[:, place * part:(place + 1) * part].reshape(step, cap, part)
            )
            rowgrad_ref[place, :, :, part:part + LANES] = sums
    else:
        rowgrad_ref[:, :, :model] = row_grad.reshape(step, cap, model)
        rowgrad_ref[:, :, model:] = sums


def expert_rows(number, first, x, mask, router, g, weights, sideways):
    sources, experts, cap, model = x.shape
    quarters, _, _, part = g.shape
    gate_up, down = weights
    width = down.shape[1]
    step = 8
    rows = step * cap
    total = sources * cap

    def flat_block(columns):
        return pl.BlockSpec((rows, columns), lambda b, f: (b, 0))

    def whole(*shape):
        return pl.BlockSpec((None,) + shape, lambda b, f: (number, 0, 0))

    def kind(*shape):
        return jax.ShapeDtypeStruct(shape, jnp.bfloat16)

    def part_block(columns):
        return pl.BlockSpec((quarters, step, cap, columns), lambda b, f: (0, b, 0, 0))

    def row_block(columns):
        return pl.BlockSpec((step, cap, columns), lambda b, f: (b, 0, 0))

    def expert_block(columns):
        return pl.BlockSpec((step, None, cap, columns), lambda b, f: (b, number, 0, 0))

    in_specs = [
        expert_block(model), expert_block(LANES), pl.BlockSpec(router.shape, lambda b, f: (0, 0)),
        part_block(part), whole(2 * width, model), whole(width, model),
    ]
    return pl.pallas_call(
        functools.partial(expert_rows_kernel, sideways),
        grid_spec=pltpu.PrefetchScalarGridSpec(
            num_scalar_prefetch=1,
            grid=(sources // step,),
            in_specs=in_specs,
            out_specs=[flat_block(2 * width), flat_block(width)] + (
                [part_block(2 * part + LANES)] if sideways
                else [row_block(model + LANES), row_block(model)]
            ),
        ),
        out_shape=[kind(total, 2 * width), kind(total, width)] + (
            [kind(quarters, sources, cap, 2 * part + LANES)] if sideways
            else [kind(sources, cap, model + LANES), kind(sources, cap, model)]
        ),
        compiler_params=pltpu.CompilerParams(vmem_limit_bytes=VMEM_BYTES),
        cost_estimate=pl.CostEstimate(
            flops=2 * total * model * width * 6, bytes_accessed=30_000_000,
            transcendentals=total * width,
        ),
        name=f"expert_rows_{number}",
    )(first + number, x, mask, router, g, gate_up, down)


def expert_weights_kernel(x_ref, g_ref, dgu_ref, actw_ref, *rest):
    gate_ref, up_ref, down_ref = rest[-3:]
    rows, width = actw_ref.shape
    hidden = gate_ref.shape[0]
    grad = matmul_tn(dgu_ref[...], x_ref[...].reshape(rows, x_ref.shape[-1]))
    gate_ref[...] = grad[:hidden, :]
    up_ref[...] = grad[width:width + hidden, :]
    g_rows = g_ref[...].reshape(rows, g_ref.shape[-1])
    down_ref[...] = matmul_tn(actw_ref[...], g_rows)[:hidden, :]


def expert_weights(number, x, g, dgu, actw, hidden, before=()):
    quarters = g.shape[0]
    sources, experts, cap, model = x.shape
    total, width = actw.shape
    steps = 8
    part = model // steps
    per = steps // quarters
    x_block = pl.BlockSpec((sources, None, cap, part), lambda b: (0, number, 0, b))
    in_specs = [
        x_block,
        pl.BlockSpec((None, sources, cap, part), lambda b: (b // per, 0, 0, b % per)),
        pl.BlockSpec((total, 2 * width), lambda b: (0, 0)),
        pl.BlockSpec((total, width), lambda b: (0, 0)),
    ] + [pl.BlockSpec(memory_space=pl.ANY)] * len(before)
    return pl.pallas_call(
        expert_weights_kernel,
        grid=(steps,),
        in_specs=in_specs,
        out_specs=[pl.BlockSpec((None, hidden, part), lambda b: (number, 0, b))] * 3,
        out_shape=[jax.ShapeDtypeStruct((experts, hidden, model), jnp.float32)] * 3,
        compiler_params=pltpu.CompilerParams(vmem_limit_bytes=VMEM_BYTES),
        cost_estimate=pl.CostEstimate(
            flops=2 * total * model * width * 3, bytes_accessed=22_000_000, transcendentals=0
        ),
        input_output_aliases={4 + place: place for place in range(len(before))},
        name=f"expert_weights_{number}",
    )(x, g, dgu, actw, *before)


def shared_weights_kernel(n_ref, c_ref, gate_ref, up_ref, act_ref, out_ref):
    chunk = out_ref.shape[1] // 3
    for place, (rows, grads) in enumerate(
        ((n_ref, gate_ref), (n_ref, up_ref), (c_ref, act_ref))
    ):
        grad = matmul_tn(rows[...], grads[...]).astype(jnp.bfloat16)
        for group in range(out_ref.shape[0]):
            out_ref[group, place * chunk:(place + 1) * chunk, :] = (
                grad[group * chunk:(group + 1) * chunk, :]
            )


def shared_weights(normed, cotangent, gate_grad, up_grad, act, groups):
    tokens, model = normed.shape
    width = gate_grad.shape[1]
    block = 256
    chunk = model // groups
    per = block // chunk
    rows = pl.BlockSpec((tokens, block), lambda i: (0, i))
    grads = pl.BlockSpec((tokens, width), lambda i: (0, 0))
    return pl.pallas_call(
        shared_weights_kernel,
        grid=(model // block,),
        in_specs=[rows, rows, grads, grads, grads],
        out_specs=pl.BlockSpec((per, 3 * chunk, width), lambda i: (i, 0, 0)),
        out_shape=jax.ShapeDtypeStruct((groups, 3 * chunk, width), jnp.bfloat16),
        compiler_params=pltpu.CompilerParams(vmem_limit_bytes=VMEM_BYTES),
        cost_estimate=pl.CostEstimate(
            flops=6 * tokens * model * width, bytes_accessed=14_000_000, transcendentals=0
        ),
        name="shared_weights",
    )(normed, cotangent, gate_grad, up_grad, act)


def combine_kernel(rank_ref, pick_ref, back_ref, sums_ref, shared_ref, dots_ref,
                   own_ref, extra_ref, *sends):
    step = pl.program_id(0)
    count = pl.num_programs(0)
    place = lax.rem(step - rank_ref[0] + count, count)
    part = own_ref.shape[1]
    value = matmul(pick_ref[...], back_ref[...]) + shared_ref[...]

    @pl.when(place == 0)
    def _():
        own_ref[...] = value

    for number, send in enumerate(sends):
        @pl.when(place == number + 1)
        def _():
            send[:, :part] = value.astype(jnp.bfloat16)

    @pl.when(step == count - 1)
    def _():
        mark = LANES // 2
        sums = matmul(pick_ref[...], sums_ref[...])
        column = lax.broadcasted_iota(jnp.int32, sums.shape, 1)
        mean = dots_ref[...] + jnp.sum(
            jnp.where((column == mark) | (column == mark + 1), sums, 0.0), axis=1, keepdims=True
        )
        mean_high = mean.astype(jnp.bfloat16).astype(jnp.float32)
        extra = jnp.where(column < mark, sums, 0.0)
        extra = jnp.where(column == mark, mean_high, extra)
        extra = jnp.where(column == mark + 1, mean - mean_high, extra).astype(jnp.bfloat16)
        extra_ref[...] = extra
        for send in sends:
            send[:, part:] = extra


def combine_rows(rank, pick, back, shared, dots, count):
    tokens, slots = pick.shape
    model = shared.shape[1]
    part = model // count
    sent = jax.ShapeDtypeStruct((tokens, part + LANES), jnp.bfloat16)
    sent_block = pl.BlockSpec((tokens, part + LANES), lambda i, r: (0, 0))
    return pl.pallas_call(
        combine_kernel,
        grid_spec=pltpu.PrefetchScalarGridSpec(
            num_scalar_prefetch=1,
            grid=(count,),
            in_specs=[
                pl.BlockSpec((tokens, slots), lambda i, r: (0, 0)),
                pl.BlockSpec((slots, part), lambda i, r: (0, i)),
                pl.BlockSpec((slots, LANES), lambda i, r: (0, model // LANES)),
                pl.BlockSpec((tokens, part), lambda i, r: (0, i)),
                pl.BlockSpec((tokens, 1), lambda i, r: (0, 0)),
            ],
            out_specs=[
                pl.BlockSpec((tokens, part), lambda i, r: (0, 0)),
                pl.BlockSpec((tokens, LANES), lambda i, r: (0, 0)),
            ] + [sent_block] * (count - 1),
        ),
        out_shape=[
            jax.ShapeDtypeStruct((tokens, part), jnp.float32),
            jax.ShapeDtypeStruct((tokens, LANES), jnp.bfloat16),
        ] + [sent] * (count - 1),
        compiler_params=pltpu.CompilerParams(vmem_limit_bytes=VMEM_BYTES),
        cost_estimate=pl.CostEstimate(
            flops=2 * tokens * slots * model, bytes_accessed=9_000_000, transcendentals=0
        ),
        name="combine_rows",
    )(rank.reshape(1), pick, back, back, shared, dots)


def branch_kernel(rank_ref, pick_ref, back_ref, shared_ref, own_ref, *sends):
    step = pl.program_id(0)
    count = pl.num_programs(0)
    place = lax.rem(step - rank_ref[0] + count, count)
    value = matmul(pick_ref[...], back_ref[...]) + shared_ref[...]

    @pl.when(place == 0)
    def _():
        own_ref[...] = value

    for number, send in enumerate(sends):
        @pl.when(place == number + 1)
        def _():
            send[...] = value.astype(jnp.bfloat16)


def branch_rows(rank, pick, back, shared, count):
    tokens, slots = pick.shape
    model = shared.shape[1]
    part = model // count
    fixed = pl.BlockSpec((tokens, part), lambda i, r: (0, 0))
    return pl.pallas_call(
        branch_kernel,
        grid_spec=pltpu.PrefetchScalarGridSpec(
            num_scalar_prefetch=1,
            grid=(count,),
            in_specs=[
                pl.BlockSpec((tokens, slots), lambda i, r: (0, 0)),
                pl.BlockSpec((slots, part), lambda i, r: (0, i)),
                pl.BlockSpec((tokens, part), lambda i, r: (0, i)),
            ],
            out_specs=[fixed] * count,
        ),
        out_shape=[jax.ShapeDtypeStruct((tokens, part), jnp.float32)]
        + [jax.ShapeDtypeStruct((tokens, part), jnp.bfloat16)] * (count - 1),
        compiler_params=pltpu.CompilerParams(vmem_limit_bytes=VMEM_BYTES),
        cost_estimate=pl.CostEstimate(flops=0, bytes_accessed=4_000_000, transcendentals=0),
        name="branch_rows",
    )(rank.reshape(1), pick, back, shared)


def token_kernel(own_ref, latent_grad_ref, w_latent_ref, mean_ref, token_ref, scale_ref, gain_ref, hidden_ref,
                 *rest):
    *pieces, out_ref = rest
    grad = own_ref[...] + matmul_nt(latent_grad_ref[...], w_latent_ref[...])
    for piece in pieces:
        grad = grad + piece[...].astype(jnp.float32)
    scale = scale_ref[...]
    unit = token_ref[...].astype(jnp.float32) * scale
    grad = hidden_ref[...] + scale * (grad * gain_ref[...] - unit * mean_ref[...])
    out_ref[...] = grad.astype(jnp.bfloat16)


def output_kernel(own_ref, hidden_ref, pick_ref, back_ref, *rest):
    *pieces, out_ref = rest
    low = back_ref.shape[1] - out_ref.shape[1]
    value = hidden_ref[...] + own_ref[...] + matmul(pick_ref[...], back_ref[:, low:])
    for piece in pieces:
        value = value + piece[...].astype(jnp.float32)
    out_ref[...] = value.astype(jnp.bfloat16)


def attention_forward_kernel(rank_ref, token_ref, gain_ref, latent_gain_ref, cosine_ref, ahead_ref,
                             behind_ref, key_cosine_ref, key_sine_ref, w_latent_ref, w_query_ref,
                             w_keyvalue_ref, w_output_ref,
                             normed_ref, scale_ref, query_ref, query_low_ref, latent_ref,
                             latent_normed_ref, keyvalue_ref, key_rope_ref, weights_ref, mixed_ref,
                             own_ref, *rest):
    *sends, latent_buf, query_buf, keyvalue_buf, output_buf, sems = rest
    copies = [
        pltpu.make_async_copy(source, buffer, sems.at[number])
        for number, (source, buffer) in enumerate((
            (w_latent_ref, latent_buf), (w_query_ref, query_buf), (w_keyvalue_ref, keyvalue_buf),
            (w_output_ref, output_buf),
        ))
    ]
    for copy in copies:
        copy.start()
    tokens = token_ref[...].astype(jnp.float32)
    scale = lax.rsqrt(jnp.mean(tokens * tokens, axis=1, keepdims=True) + EPS)
    scale_ref[...] = scale
    normed = (tokens * scale * gain_ref[...]).astype(jnp.bfloat16)
    normed_ref[...] = normed
    copies[0].wait()
    latent = matmul_nt(normed, latent_buf[...])
    latent_ref[...] = latent
    compressed = latent[:, :KV_RANK]
    latent_scale = lax.rsqrt(jnp.mean(compressed * compressed, axis=1, keepdims=True) + EPS)
    latent_normed = (compressed * latent_scale * latent_gain_ref[...]).astype(jnp.bfloat16)
    latent_normed_ref[...] = latent_normed
    half = ROPE // 2
    former = latent[:, KV_RANK:KV_RANK + half]
    latter = latent[:, KV_RANK + half:]
    key_cosine, key_sine = key_cosine_ref[...], key_sine_ref[...]
    key_rope = jnp.concatenate(
        [former * key_cosine - latter * key_sine, latter * key_cosine + former * key_sine], axis=1
    ).astype(jnp.bfloat16)
    key_rope_ref[...] = key_rope
    copies[1].wait()
    query = matmul(normed, query_buf[...])
    query_ref[...] = query
    wide = query.shape[1]
    query_low_ref[...] = (
        query * cosine_ref[...] + pltpu.roll(query, wide - half, 1) * ahead_ref[...]
        + pltpu.roll(query, half, 1) * behind_ref[...]
    ).astype(jnp.bfloat16)
    copies[2].wait()
    keyvalue_ref[...] = matmul(latent_normed, keyvalue_buf[...]).astype(jnp.bfloat16)
    rows = tokens.shape[0]
    causal = (
        lax.broadcasted_iota(jnp.int32, (rows, rows), 0)
        >= lax.broadcasted_iota(jnp.int32, (rows, rows), 1)
    )
    qk_width = NOPE + ROPE
    for head in range(wide // qk_width):
        low = head * (NOPE + VDIM)
        query_head = query_low_ref[:, head * qk_width:(head + 1) * qk_width]
        key_head = jnp.concatenate([keyvalue_ref[:, low:low + NOPE], key_rope], axis=1)
        scores = matmul_nt(query_head, key_head) * (qk_width ** -0.5)
        scores = jnp.where(causal, scores, MASKED)
        terms = jnp.exp(scores - jnp.max(scores, axis=1, keepdims=True))
        weights = terms / jnp.sum(terms, axis=1, keepdims=True)
        weights_ref[head] = weights
        mixed_ref[:, head * VDIM:(head + 1) * VDIM] = matmul(
            weights.astype(jnp.bfloat16), keyvalue_ref[:, low + NOPE:low + NOPE + VDIM]
        ).astype(jnp.bfloat16)
    copies[3].wait()
    part = own_ref.shape[1]
    count = len(sends) + 1
    for number in range(count):
        value = matmul(mixed_ref[...], output_buf[:, number * part:(number + 1) * part])
        place = lax.rem(number - rank_ref[0] + count, count)

        @pl.when(place == 0)
        def _():
            own_ref[...] = value

        for index, send in enumerate(sends):
            @pl.when(place == index + 1)
            def _():
                send[...] = value.astype(jnp.bfloat16)


def rotary_constants(rows, heads):
    half = ROPE // 2
    frequency = np.float32(THETA) ** (np.arange(half, dtype=np.float32) * np.float32(-2.0 / ROPE))
    angles = np.arange(rows, dtype=np.float32)[:, None] * frequency[None, :]
    cosine, sine = np.cos(angles), np.sin(angles)
    blank = np.zeros((rows, NOPE), np.float32)
    zero = np.zeros((rows, half), np.float32)

    def tiled(*pieces):
        return np.tile(np.concatenate(pieces, axis=1), (1, heads)).astype(np.float32)

    return (
        tiled(blank + 1.0, cosine, cosine), tiled(blank, -sine, zero), tiled(blank, zero, sine),
        cosine, sine,
    )


def full_specs(arrays):
    return [pl.BlockSpec(a.shape, lambda i, r, n=len(a.shape): (0,) * n) for a in arrays]


def attention_forward(rank, tokens, gain, latent_gain, tables, w_latent, w_query, w_keyvalue, w_output,
                      count):
    rows, model = tokens.shape
    part = model // count
    latent_width = w_latent.shape[1]
    query_width = w_query.shape[1]
    heads = query_width // (NOPE + ROPE)
    bf16, f32 = jnp.bfloat16, jnp.float32
    out_shape = [
        jax.ShapeDtypeStruct(shape, kind)
        for shape, kind in (
            ((rows, model), bf16), ((rows, 1), f32), ((rows, query_width), f32),
            ((rows, query_width), bf16), ((rows, latent_width), f32), ((rows, KV_RANK), bf16),
            ((rows, w_keyvalue.shape[1]), bf16), ((rows, ROPE), bf16), ((heads, rows, rows), f32),
            ((rows, heads * VDIM), bf16), ((rows, part), f32),
        ) + (((rows, part), bf16),) * (count - 1)
    ]
    inputs = [tokens, gain.reshape(1, -1), latent_gain.reshape(1, -1), *tables]
    streamed = [w_latent.T, w_query, w_keyvalue, w_output]
    return pl.pallas_call(
        attention_forward_kernel,
        grid_spec=pltpu.PrefetchScalarGridSpec(
            num_scalar_prefetch=1,
            grid=(1,),
            in_specs=full_specs(inputs) + [pl.BlockSpec(memory_space=pl.ANY)] * len(streamed),
            out_specs=full_specs(out_shape),
            scratch_shapes=[pltpu.VMEM(a.shape, a.dtype) for a in streamed]
            + [pltpu.SemaphoreType.DMA((len(streamed),))],
        ),
        out_shape=out_shape,
        compiler_params=pltpu.CompilerParams(vmem_limit_bytes=VMEM_BYTES),
        cost_estimate=pl.CostEstimate(
            flops=5_000_000_000, bytes_accessed=16_000_000, transcendentals=300_000
        ),
        name="attention_forward",
    )(rank.reshape(1), *inputs, *streamed)


def attention_backward_kernel(rank_ref, *refs):
    count = 4
    pieces, refs = refs[:count], refs[count:]
    (weights_ref, keyvalue_ref, key_rope_ref, query_low_ref, query_ref, token_ref, scale_ref, cosine_ref,
     ahead_ref, behind_ref, w_output_ref, w_keyvalue_ref, w_query_ref,
     branch_ref, gain_ref, query_grad_ref, keyvalue_grad_ref, own_ref, latent_ref, *rest) = refs
    *sends, output_buf, keyvalue_buf, query_buf, grad_buf, sems = rest
    copies = [
        pltpu.make_async_copy(source, buffer, sems.at[number])
        for number, (source, buffer) in enumerate((
            (w_output_ref, output_buf), (w_keyvalue_ref, keyvalue_buf), (w_query_ref, query_buf),
        ))
    ]
    for copy in copies:
        copy.start()
    rows, model = branch_ref.shape
    part = own_ref.shape[1]
    for place in range(count):
        columns = slice(place * part, (place + 1) * part)
        turn = lax.rem(rank_ref[0] - place + count, count)
        for number, piece in enumerate(pieces):
            @pl.when(turn == number)
            def _():
                branch_ref[:, columns] = piece[:rows, :]
                sums = piece[rows:, :].astype(jnp.float32)
                gain_ref[:, columns] = sums[0:1] + sums[1:2]
    copies[0].wait()
    mixed_grad = matmul_nt(branch_ref[...], output_buf[...]).astype(jnp.bfloat16)
    qk_width = NOPE + ROPE
    soft = qk_width ** -0.5
    key_rope = key_rope_ref[...]
    rope_grad = jnp.zeros((rows, ROPE), jnp.float32)
    for head in range(weights_ref.shape[0]):
        low = head * (NOPE + VDIM)
        columns = slice(head * qk_width, (head + 1) * qk_width)
        weights = weights_ref[head]
        out_grad = mixed_grad[:, head * VDIM:(head + 1) * VDIM]
        keyvalue_grad_ref[:, low + NOPE:low + NOPE + VDIM] = matmul_tn(
            weights.astype(jnp.bfloat16), out_grad
        ).astype(jnp.bfloat16)
        prob_grad = matmul_nt(out_grad, keyvalue_ref[:, low + NOPE:low + NOPE + VDIM])
        row_term = jnp.sum(weights * prob_grad, axis=1, keepdims=True)
        score_grad = (weights * (prob_grad - row_term)).astype(jnp.bfloat16)
        key_head = jnp.concatenate([keyvalue_ref[:, low:low + NOPE], key_rope], axis=1)
        grad_buf[:, columns] = matmul(score_grad, key_head) * soft
        key_grad = matmul_tn(score_grad, query_low_ref[:, columns]) * soft
        keyvalue_grad_ref[:, low:low + NOPE] = key_grad[:, :NOPE].astype(jnp.bfloat16)
        rope_grad += key_grad[:, NOPE:]
    grad = grad_buf[...]
    wide = grad.shape[1]
    half = ROPE // 2
    query_grad = (
        grad * cosine_ref[...] - pltpu.roll(grad, wide - half, 1) * ahead_ref[...]
        - pltpu.roll(grad, half, 1) * behind_ref[...]
    ).astype(jnp.bfloat16)
    query_grad_ref[...] = query_grad
    mean = jnp.sum(query_grad.astype(jnp.float32) * query_ref[...], axis=1, keepdims=True)
    mean_high = mean.astype(jnp.bfloat16).astype(jnp.float32)
    copies[1].wait()
    latent_part = matmul_nt(keyvalue_grad_ref[...], keyvalue_buf[...])
    width = latent_part.shape[1]
    column = lax.broadcasted_iota(jnp.int32, (rows, LANES - ROPE), 1)
    sums = jnp.where(column == 0, mean_high, jnp.where(column == 1, mean - mean_high, 0.0))
    latent_ref[:rows, :width] = latent_part.astype(jnp.bfloat16)
    latent_ref[:rows, width:] = jnp.concatenate([rope_grad, sums], axis=1).astype(jnp.bfloat16)
    copies[2].wait()
    gains = []
    scale = scale_ref[...]
    for number in range(count):
        columns = slice(number * part, (number + 1) * part)
        value = matmul_nt(query_grad, query_buf[columns, :])
        unit = token_ref[:, columns].astype(jnp.float32) * scale
        gains.append(jnp.sum(value * unit, axis=0, keepdims=True))
        place = lax.rem(number - rank_ref[0] + count, count)

        @pl.when(place == 0)
        def _():
            own_ref[...] = value

        for index, send in enumerate(sends):
            @pl.when(place == index + 1)
            def _():
                send[...] = value.astype(jnp.bfloat16)
    highs = [gain.astype(jnp.bfloat16).astype(jnp.float32) for gain in gains]
    lows = [gain - high for gain, high in zip(gains, highs)]
    spare = latent_ref.shape[0] - rows
    latent_ref[rows:, :width] = jnp.concatenate(
        highs + lows + [jnp.zeros((spare - 2 * count, part), jnp.float32)], axis=0
    ).astype(jnp.bfloat16)
    latent_ref[rows:, width:] = jnp.zeros((spare, LANES), jnp.bfloat16)


def attention_backward(rank, pieces, weights, keyvalue, key_rope, query_low, query, tokens, scale, tables,
                       w_output, w_keyvalue, w_query):
    rows, model = tokens.shape
    count = len(pieces)
    part = model // count
    wide = query.shape[1]
    kv_width = keyvalue.shape[1]
    sent_rows = pieces[0].shape[0]
    bf16, f32 = jnp.bfloat16, jnp.float32
    sent_width = KV_RANK + LANES
    out_shape = [
        jax.ShapeDtypeStruct(shape, kind)
        for shape, kind in (
            ((rows, model), bf16), ((1, model), f32), ((rows, wide), bf16), ((rows, kv_width), bf16),
            ((rows, part), f32), ((sent_rows, sent_width), bf16),
        ) + (((rows, part), bf16),) * (count - 1)
    ]
    inputs = [*pieces, weights, keyvalue, key_rope, query_low, query, tokens, scale, *tables[:3]]
    streamed = [w_output, w_keyvalue, w_query]
    return pl.pallas_call(
        attention_backward_kernel,
        grid_spec=pltpu.PrefetchScalarGridSpec(
            num_scalar_prefetch=1,
            grid=(1,),
            in_specs=full_specs(inputs) + [pl.BlockSpec(memory_space=pl.ANY)] * len(streamed),
            out_specs=full_specs(out_shape),
            scratch_shapes=[pltpu.VMEM(a.shape, a.dtype) for a in streamed]
            + [pltpu.VMEM((rows, wide), f32), pltpu.SemaphoreType.DMA((len(streamed),))],
        ),
        out_shape=out_shape,
        compiler_params=pltpu.CompilerParams(vmem_limit_bytes=VMEM_BYTES),
        cost_estimate=pl.CostEstimate(
            flops=4_000_000_000, bytes_accessed=20_000_000, transcendentals=0
        ),
        name="attention_backward",
    )(rank.reshape(1), *inputs, *streamed)


def single_call(kernel, arrays, shapes, name):
    def specs(values):
        return [pl.BlockSpec(a.shape, lambda i, n=len(a.shape): (0,) * n) for a in values]

    return pl.pallas_call(
        kernel,
        grid=(1,),
        in_specs=specs(arrays),
        out_specs=specs(shapes),
        out_shape=shapes,
        compiler_params=pltpu.CompilerParams(vmem_limit_bytes=VMEM_BYTES),
        cost_estimate=pl.CostEstimate(flops=0, bytes_accessed=4_000_000, transcendentals=0),
        name=name,
    )(*arrays)


def hidden_kernel(own_ref, token_ref, *rest):
    *pieces, hidden_ref, sent_ref = rest
    value = own_ref[...] + token_ref[...].astype(jnp.float32)
    for piece in pieces:
        value = value + piece[...].astype(jnp.float32)
    hidden_ref[...] = value
    part = value.shape[1]
    total = jnp.sum(value * value, axis=1, keepdims=True)
    high = total.astype(jnp.bfloat16).astype(jnp.float32)
    column = lax.broadcasted_iota(jnp.int32, (value.shape[0], LANES), 1)
    sums = jnp.where(column == 0, high, jnp.where(column == 1, total - high, 0.0))
    sent_ref[:, :part] = value.astype(jnp.bfloat16)
    sent_ref[:, part:] = sums.astype(jnp.bfloat16)


def hidden_rows(own, token_block, pieces):
    tokens, part = own.shape
    shapes = [
        jax.ShapeDtypeStruct((tokens, part), jnp.float32),
        jax.ShapeDtypeStruct((tokens, part + LANES), jnp.bfloat16),
    ]
    return single_call(hidden_kernel, [own, token_block, *pieces], shapes, "hidden_rows")


def owner_rows_kernel(first_ref, block_ref, mask_ref, *out_refs):
    sources, rows, _ = block_ref.shape
    _, cap, part = out_refs[0].shape
    experts = len(out_refs)
    line = lax.broadcasted_iota(jnp.int32, (8, LANES), 0)
    column = lax.broadcasted_iota(jnp.int32, (8, LANES), 1)
    select = ((column == line + first_ref[0]) & (line < experts)).astype(jnp.bfloat16)
    earlier = (
        lax.broadcasted_iota(jnp.int32, (rows, rows), 0)
        < lax.broadcasted_iota(jnp.int32, (rows, rows), 1)
    ).astype(jnp.bfloat16)
    slot = lax.broadcasted_iota(jnp.int32, (cap, rows), 0).astype(jnp.float32)
    chosen = jnp.concatenate(
        [matmul_nt(select, block_ref[source, :, part:]) for source in range(sources)], axis=0
    )
    place = matmul(chosen.astype(jnp.bfloat16), earlier)
    for source in range(sources):
        picks = [
            jnp.where((slot == place[line:line + 1]) & (chosen[line:line + 1] > 0.5), 1.0, 0.0)
            for line in range(8 * source, 8 * source + experts)
        ]
        picks = jnp.concatenate(picks, axis=0).astype(jnp.bfloat16)
        out = matmul(picks, block_ref[source]).astype(jnp.bfloat16)
        mask_ref[source] = out[:, part:].reshape(experts, cap, LANES)
        for number, out_ref in enumerate(out_refs):
            out_ref[source] = out[number * cap:(number + 1) * cap, :part]


def owner_rows(first, gathered, experts, cap):
    groups, rows, wide = gathered.shape
    part = wide - LANES
    step = 16
    return pl.pallas_call(
        owner_rows_kernel,
        grid_spec=pltpu.PrefetchScalarGridSpec(
            num_scalar_prefetch=1,
            grid=(groups // step,),
            in_specs=[pl.BlockSpec((step, rows, wide), lambda i, f: (i, 0, 0))],
            out_specs=[pl.BlockSpec((step, experts, cap, LANES), lambda i, f: (i, 0, 0, 0))]
            + [pl.BlockSpec((step, cap, part), lambda i, f: (i, 0, 0))] * experts,
        ),
        out_shape=[jax.ShapeDtypeStruct((groups, experts, cap, LANES), jnp.bfloat16)]
        + [jax.ShapeDtypeStruct((groups, cap, part), jnp.bfloat16)] * experts,
        compiler_params=pltpu.CompilerParams(vmem_limit_bytes=VMEM_BYTES),
        cost_estimate=pl.CostEstimate(
            flops=2 * groups * experts * cap * rows * part, bytes_accessed=13_000_000,
            transcendentals=0,
        ),
        name="owner_rows",
    )(first, gathered)


def route_rows_kernel(rank_ref, dispatch_ref, gain_ref, router_ref, *rest):
    pieces, (rows_ref, wide_ref, logit_ref, scale_ref) = rest[:-4], rest[-4:]
    count = len(pieces)
    part = pieces[0].shape[1] - LANES
    model = count * part

    @pl.when(pl.program_id(0) == 0)
    def _():
        total = sum(jnp.sum(piece[:, part:].astype(jnp.float32), axis=1, keepdims=True)
                    for piece in pieces)
        scale = lax.rsqrt(total / model + EPS)
        scale_ref[...] = scale
        logits = jnp.zeros(logit_ref.shape, jnp.float32)
        for place in range(count):
            turn = lax.rem(rank_ref[0] - place + count, count)
            block = pieces[0][:, :part].astype(jnp.float32)
            for number in range(1, count):
                block = jnp.where(turn == number, pieces[number][:, :part].astype(jnp.float32),
                                  block)
            columns = slice(place * part, (place + 1) * part)
            block = (block * scale * gain_ref[:, columns]).astype(jnp.bfloat16)
            wide_ref[:, columns] = block
            logits += matmul(block, router_ref[columns, :])
        logit_ref[...] = logits

    rows_ref[...] = matmul(dispatch_ref[...], wide_ref[...]).astype(jnp.bfloat16)


def route_rows(rank, dispatch, gain, router, pieces):
    slots, tokens = dispatch.shape
    model, experts = router.shape
    block = 512

    def whole(*shape):
        return pl.BlockSpec(shape, lambda i, r: (0, 0))

    return pl.pallas_call(
        route_rows_kernel,
        grid_spec=pltpu.PrefetchScalarGridSpec(
            num_scalar_prefetch=1,
            grid=(slots // block,),
            in_specs=[
                pl.BlockSpec((block, tokens), lambda i, r: (i, 0)),
                whole(1, model), whole(model, experts),
            ] + [whole(*piece.shape) for piece in pieces],
            out_specs=[
                pl.BlockSpec((block, model), lambda i, r: (i, 0)),
                whole(tokens, model), whole(tokens, experts), whole(tokens, 1),
            ],
        ),
        out_shape=[
            jax.ShapeDtypeStruct((slots, model), jnp.bfloat16),
            jax.ShapeDtypeStruct((tokens, model), jnp.bfloat16),
            jax.ShapeDtypeStruct((tokens, experts), jnp.float32),
            jax.ShapeDtypeStruct((tokens, 1), jnp.float32),
        ],
        compiler_params=pltpu.CompilerParams(vmem_limit_bytes=VMEM_BYTES),
        cost_estimate=pl.CostEstimate(
            flops=2 * slots * tokens * model, bytes_accessed=13_000_000, transcendentals=0
        ),
        name="route_rows",
    )(rank.reshape(1), dispatch, gain.reshape(1, model), router, *pieces)


def norm_back_kernel(own_ref, extra_ref, pick_ref, back_ref, mask_ref, logit_ref, scale_ref, hidden_ref,
                     gain_ref, router_ref, cotangent_ref, *rest):
    *pieces, grad_ref, sent_ref, logit_grad_ref = rest
    part = own_ref.shape[1]
    rows, experts = mask_ref.shape
    model = part * (len(pieces) + 1)
    gathered = matmul(pick_ref[...], back_ref[:, :part + LANES])
    norm_grad = own_ref[...] + gathered[:, :part]
    extra = extra_ref[...].astype(jnp.float32) + gathered[:, part:]
    for piece in pieces:
        norm_grad = norm_grad + piece[:, :part].astype(jnp.float32)
        extra = extra + piece[:, part:].astype(jnp.float32)
    logits = logit_ref[...]
    sigmas = mask_ref[...] / (1.0 + jnp.exp(-logits))
    total = jnp.sum(sigmas, axis=1, keepdims=True)
    gate_grad = extra[:, :experts]
    weighted_sum = jnp.sum(gate_grad * sigmas, axis=1, keepdims=True)
    sigma_grad = ROUTE_SCALE * (gate_grad / total - weighted_sum / (total * total))
    logit_grad = (sigma_grad * sigmas * (1.0 - sigmas)).astype(jnp.bfloat16)
    logit_grad_ref[...] = logit_grad
    norm_grad = norm_grad + matmul_nt(logit_grad, router_ref[...])
    mean = (
        jnp.sum(extra[:, experts:experts + 2], axis=1, keepdims=True)
        + jnp.sum(logit_grad.astype(jnp.float32) * logits, axis=1, keepdims=True)
    ) / model
    scale = scale_ref[...]
    unit = hidden_ref[...] * scale
    gain_grad = jnp.sum(norm_grad * unit, axis=0, keepdims=True)
    grad = cotangent_ref[...].astype(jnp.float32) + scale * (norm_grad * gain_ref[...] - unit * mean)
    grad_ref[...] = grad
    sent_ref[:rows, :] = grad.astype(jnp.bfloat16)
    high = gain_grad.astype(jnp.bfloat16).astype(jnp.float32)
    row = lax.broadcasted_iota(jnp.int32, (sent_ref.shape[0] - rows, part), 0)
    sums = jnp.where(row == 0, high, jnp.where(row == 1, gain_grad - high, 0.0))
    sent_ref[rows:, :] = sums.astype(jnp.bfloat16)


def norm_back(own, extra, pick, back, mask, logits, scale, hidden, gain, router, cotangent, pieces):
    rows, part = own.shape
    bf16, f32 = jnp.bfloat16, jnp.float32
    shapes = [
        jax.ShapeDtypeStruct((rows, part), f32), jax.ShapeDtypeStruct((rows + 16, part), bf16),
        jax.ShapeDtypeStruct(mask.shape, bf16),
    ]
    inputs = [own, extra, pick, back, mask, logits, scale, hidden, gain.reshape(1, part), router, cotangent]
    return single_call(norm_back_kernel, inputs + list(pieces), shapes, "norm_back")


def put_pairs(first, grad, row, column, mine_ref, other_ref):
    rows = slice(row, row + grad.shape[2])
    columns = slice(column, column + grad.shape[3])
    even, odd = grad[:, 0], grad[:, 1]
    mine_ref[:, rows, columns] = jnp.where(first, even, odd).astype(jnp.bfloat16)
    other_ref[:, rows, columns] = jnp.where(first, odd, even).astype(jnp.bfloat16)


def branch_weights_kernel(core_ref, n_ref, b_ref, l_ref, query_ref, mixed_ref, kv_ref, mine_ref, other_ref):
    pairs, chunk, _ = mine_ref.shape
    first = core_ref[0] == 0

    def by_pairs(grad):
        return grad.reshape(pairs, 2, grad.shape[0] // (2 * pairs), grad.shape[1])

    low = 0
    for rows_ref, grads in ((n_ref, query_ref), (b_ref, mixed_ref)):
        grad = matmul_tn(rows_ref[...], grads[...])
        put_pairs(first, by_pairs(grad), 0, low, mine_ref, other_ref)
        low += grad.shape[1]
    grad = by_pairs(matmul_tn(l_ref[...], kv_ref[...]))
    kv_chunk = grad.shape[2]
    columns = grad.shape[3] * kv_chunk // chunk
    for place in range(chunk // kv_chunk):
        put_pairs(first, grad[:, :, :, place * columns:(place + 1) * columns], place * kv_chunk, low,
                  mine_ref, other_ref)


def paired_call(kernel, core, groups, columns, blocked, whole, extra_shapes, scratch, name):
    steps = 4
    model = blocked[0].shape[1]
    chunk = model // groups
    out = pl.BlockSpec((groups // 2 // steps, chunk, columns), lambda i, c: (i, 0, 0))

    def fixed(array):
        return pl.BlockSpec(array.shape, lambda i, c: (0, 0))

    return pl.pallas_call(
        kernel,
        grid_spec=pltpu.PrefetchScalarGridSpec(
            num_scalar_prefetch=1,
            grid=(steps,),
            in_specs=[
                pl.BlockSpec((a.shape[0], a.shape[1] // steps), lambda i, c: (0, i)) for a in blocked
            ] + [fixed(a) for a in whole],
            out_specs=[fixed(a) for a in extra_shapes] + [out] * 2,
            scratch_shapes=scratch,
        ),
        out_shape=list(extra_shapes)
        + [jax.ShapeDtypeStruct((groups // 2, chunk, columns), jnp.bfloat16)] * 2,
        compiler_params=pltpu.CompilerParams(vmem_limit_bytes=VMEM_BYTES),
        cost_estimate=pl.CostEstimate(flops=0, bytes_accessed=10_000_000, transcendentals=0),
        name=name,
    )(core.reshape(1), *blocked, *whole)


def branch_weights(core, groups, normed, branch, latent_normed, query, mixed, kv):
    columns = (
        query.shape[1] + mixed.shape[1] + kv.shape[1] * latent_normed.shape[1] // normed.shape[1]
    )
    return paired_call(
        branch_weights_kernel, core, groups, columns, [normed, branch, latent_normed],
        [query, mixed, kv], [], [], "branch_weights",
    )


def latent_weights_kernel(core_ref, n_ref, t_ref, token_ref, w_latent_ref, ffn_ref, logit_ref, latent_ref,
                          latent_gain_ref, cosine_ref, sine_ref, scale_ref, *rest):
    *pieces, latent_grad_ref, mean_ref, mine_ref, other_ref, gain_buf, latent_gain_buf = rest
    step = pl.program_id(0)
    count = len(pieces)
    pairs, chunk, _ = mine_ref.shape
    rows = latent_ref.shape[0]
    block = n_ref.shape[1]
    first = core_ref[0] == 0

    @pl.when(step == 0)
    def _():
        total = sum(piece[...].astype(jnp.float32) for piece in pieces)
        for number in range(count):
            gain_buf[number] = (
                total[rows + number:rows + number + 1, :block]
                + total[rows + count + number:rows + count + number + 1, :block]
            )
        latent = latent_ref[...]
        compressed = latent[:, :KV_RANK]
        scale = lax.rsqrt(jnp.mean(compressed * compressed, axis=1, keepdims=True) + EPS)
        unit = compressed * scale
        grad = total[:rows, :KV_RANK]
        gains = jnp.sum(grad * unit, axis=0, keepdims=True)
        width = KV_RANK // count
        for number in range(count):
            latent_gain_buf[number] = gains[:, number * width:(number + 1) * width]
        grad = grad * latent_gain_ref[...]
        grad = scale * (grad - unit * jnp.mean(unit * grad, axis=1, keepdims=True))
        half = ROPE // 2
        former = total[:rows, KV_RANK:KV_RANK + half]
        latter = total[:rows, KV_RANK + half:KV_RANK + ROPE]
        cosine, sine = cosine_ref[...], sine_ref[...]
        latent_grad = jnp.concatenate(
            [grad, former * cosine + latter * sine, latter * cosine - former * sine], axis=1
        ).astype(jnp.bfloat16)
        latent_grad_ref[...] = latent_grad
        sums = total[:rows, KV_RANK + ROPE:KV_RANK + ROPE + 2]
        mean_ref[...] = (
            jnp.sum(sums, axis=1, keepdims=True)
            + jnp.sum(latent_grad.astype(jnp.float32) * latent, axis=1, keepdims=True)
        ) / (block * count)

    def by_pairs(grad):
        return grad.reshape(pairs, 2, grad.shape[0] // (2 * pairs), grad.shape[1])

    low = 0
    for rows_ref, grads in ((n_ref, latent_grad_ref), (t_ref, logit_ref)):
        grad = matmul_tn(rows_ref[...], grads[...])
        put_pairs(first, by_pairs(grad), 0, low, mine_ref, other_ref)
        low += grad.shape[1]
    unit = token_ref[...].astype(jnp.float32) * scale_ref[...]
    routed = matmul(latent_grad_ref[...], w_latent_ref[...])
    gain = gain_buf[step] + jnp.sum(routed * unit, axis=0, keepdims=True)
    line = lax.broadcasted_iota(jnp.int32, (LANES, block), 0)
    gains = by_pairs(jnp.where(line == 0, gain, jnp.where(line == 1, ffn_ref[...], 0.0)).T)
    width = latent_gain_buf.shape[2]
    kv_chunk = width // (2 * pairs)
    line = lax.broadcasted_iota(jnp.int32, (LANES, width), 0)
    more = by_pairs(jnp.where(line == 2, latent_gain_buf[step], 0.0).T)
    gains = jnp.concatenate([gains[:, :, :kv_chunk] + more, gains[:, :, kv_chunk:]], axis=2)
    put_pairs(first, gains, 0, low, mine_ref, other_ref)


def latent_weights(core, groups, normed, normed_two, tokens, w_latent, ffn_gain, logit, latent, latent_gain,
                   cosine, sine, scale, pieces):
    count = len(pieces)
    shapes = [
        jax.ShapeDtypeStruct(latent.shape, jnp.bfloat16),
        jax.ShapeDtypeStruct(scale.shape, jnp.float32),
    ]
    scratch = [
        pltpu.VMEM((count, 1, normed.shape[1] // count), jnp.float32),
        pltpu.VMEM((count, 1, KV_RANK // count), jnp.float32),
    ]
    return paired_call(
        latent_weights_kernel, core, groups, latent.shape[1] + logit.shape[1] + LANES,
        [normed, normed_two, tokens, w_latent.T, ffn_gain],
        [logit, latent, latent_gain.reshape(1, -1), cosine, sine, scale, *pieces], shapes, scratch,
        "latent_weights",
    )


def pair_kernel(mine_ref, got_ref, *rest):
    rest[-1][...] = (
        mine_ref[...].astype(jnp.float32) + got_ref[...].astype(jnp.float32)
    ).astype(jnp.bfloat16)


def pair_sum(mine, got, columns, place, whole=None):
    chips, rows, width = mine.shape
    steps = 4
    block = pl.BlockSpec((chips // steps, rows, width), lambda i: (i, 0, 0))
    before = () if whole is None else (whole,)
    return pl.pallas_call(
        pair_kernel,
        grid=(steps,),
        in_specs=[block, block] + [pl.BlockSpec(memory_space=pl.ANY)] * len(before),
        out_specs=pl.BlockSpec((chips // steps, rows, width), lambda i: (i, 0, place)),
        out_shape=jax.ShapeDtypeStruct((chips, rows, columns), jnp.bfloat16),
        input_output_aliases={2: 0} if before else {},
        compiler_params=pltpu.CompilerParams(vmem_limit_bytes=VMEM_BYTES),
        cost_estimate=pl.CostEstimate(flops=0, bytes_accessed=14_000_000, transcendentals=0),
        name="pair_sum",
    )(mine, got, *before)


def final_kernel(edges, part_ref, query_ref, output_ref, kv_ref, latent_ref, router_ref,
                 *rest):
    *gain_refs, total_ref = rest
    step = pl.program_id(0)

    @pl.when(step == 0)
    def _():
        total_ref[...] = jnp.zeros_like(total_ref)

    total = total_ref[...]
    for number in range(part_ref.shape[0]):
        total = total + part_ref[number].astype(jnp.float32)
    total_ref[...] = total

    @pl.when(step == pl.num_programs(0) - 1)
    def _():
        outs = (query_ref, output_ref, kv_ref, latent_ref, router_ref)
        for out, low, high in zip(outs, edges[:5], edges[1:6]):
            if out is not kv_ref:
                out[...] = total_ref[:, low:high]
                continue
            chunk = out.shape[0]
            for place in range(total_ref.shape[0] // chunk):
                out[:, place * (high - low):(place + 1) * (high - low)] = (
                    total_ref[place * chunk:(place + 1) * chunk, low:high]
                )
        gains = total_ref[:, edges[5]:].T
        for number, gain_ref in enumerate(gain_refs):
            gain_ref[...] = gains[number:number + 1, :]


def final_sums(parts, edges, shapes):
    chips, rows, columns = parts.shape
    step = 4
    return pl.pallas_call(
        functools.partial(final_kernel, edges),
        grid=(chips // step,),
        in_specs=[pl.BlockSpec((step, rows, columns), lambda i: (i, 0, 0))],
        out_specs=[pl.BlockSpec(a.shape, lambda i: (0, 0)) for a in shapes],
        out_shape=shapes,
        scratch_shapes=[pltpu.VMEM((rows, columns), jnp.float32)],
        compiler_params=pltpu.CompilerParams(vmem_limit_bytes=VMEM_BYTES),
        cost_estimate=pl.CostEstimate(flops=0, bytes_accessed=6_000_000, transcendentals=0),
        name="final_sums",
    )(parts)


def ordered_kernel(rank_ref, *refs):
    *pieces, out_ref = refs
    count = len(pieces)
    part = pieces[0].shape[1]
    for place in range(count):
        turn = lax.rem(rank_ref[0] - place + count, count)
        for number, piece in enumerate(pieces):
            @pl.when(turn == number)
            def _():
                out_ref[:, place * part:(place + 1) * part] = piece[...]


def ordered_columns(rank, pieces):
    rows, part = pieces[0].shape
    shape = jax.ShapeDtypeStruct((rows, part * len(pieces)), pieces[0].dtype)
    return pl.pallas_call(
        ordered_kernel,
        grid_spec=pltpu.PrefetchScalarGridSpec(
            num_scalar_prefetch=1, grid=(1,), in_specs=full_specs(pieces),
            out_specs=full_specs([shape])[0],
        ),
        out_shape=shape,
        compiler_params=pltpu.CompilerParams(vmem_limit_bytes=VMEM_BYTES),
        cost_estimate=pl.CostEstimate(flops=0, bytes_accessed=2_000_000, transcendentals=0),
        name="ordered_columns",
    )(rank.reshape(1), *pieces)


def swap_cores(rows, groups):
    return lax.ppermute(rows, "expert", [(index, index ^ 1) for index in range(groups)])


def shards(
    tokens,
    cotangent,
    attn_gain,
    w_query,
    w_latent,
    latent_gain,
    w_keyvalue,
    w_output,
    ffn_gain,
    w_router,
    shared_gate,
    shared_up,
    shared_down,
    expert_gate,
    expert_up,
    expert_down,
    routes,
):
    bf16 = jnp.bfloat16
    f32 = jnp.float32
    tok_rows, model_width = tokens.shape
    top_count = routes.shape[1]
    expert_count = w_router.shape[1]
    local_experts, _, hidden_width = expert_gate.shape
    groups = lax.axis_size("expert")
    ranks = lax.axis_size("tensor")
    rank = lax.axis_index("tensor")
    group = lax.axis_index("expert")
    part = model_width // ranks
    capacity = (4 * tok_rows * top_count + 3 * expert_count - 1) // (3 * expert_count)
    slot_count = expert_count * capacity
    per_group = local_experts * capacity
    qk_width = NOPE + ROPE
    local_heads = w_query.shape[1] // qk_width

    expert_ids = jnp.arange(expert_count, dtype=jnp.int32)
    selector = routes[:, :, None] == expert_ids[None, None, :]
    chosen_mask = jnp.sum(selector.astype(f32), axis=1)

    cotangent_part = column_block(cotangent, rank, part)
    chosen_low = jnp.pad(chosen_mask.astype(bf16), ((0, 0), (0, LANES - expert_count)))
    all_grads = lax.all_gather(
        jnp.concatenate([cotangent_part, chosen_low], axis=1), "expert", axis=0
    )

    tables = rotary_constants(tok_rows, local_heads)
    (normed, scale_one, query_pre, query_low, latent, latent_normed, keyvalue, key_rope, weights_full,
     attn_mixed, attended, *sends) = attention_forward(
        rank, tokens, attn_gain, latent_gain, tables, w_latent, w_query, w_keyvalue, w_output, ranks
    )

    token_ids = jnp.arange(tok_rows, dtype=jnp.int32)
    before = (token_ids[:, None] > token_ids[None, :]).astype(bf16)
    earlier = matmul(before, after(chosen_mask, attended).astype(bf16))
    place = jnp.sum(jnp.where(selector, earlier[:, None, :], 0.0), axis=-1).astype(jnp.int32)
    expert_place = lax.rem(routes, local_experts) * groups + routes // local_experts
    slot_ids = jnp.arange(slot_count, dtype=jnp.int32)

    def one_hot(target, sideways):
        shape = (tok_rows, slot_count) if sideways else (slot_count, tok_rows)
        found = jnp.zeros(shape, jnp.bool_)
        for choice in range(top_count):
            if sideways:
                found = found | (target[:, choice][:, None] == slot_ids[None, :])
            else:
                found = found | (slot_ids[:, None] == target[:, choice][None, :])
        return found.astype(bf16)

    dispatch = one_hot(routes * capacity + place, False)
    by_expert = one_hot(expert_place * capacity + place, True)
    by_expert = by_expert.reshape(tok_rows, local_experts, groups * capacity)

    sends = [shift_ranks(sent, step + 1, ranks) for step, sent in enumerate(sends)]
    hidden_part, sent = hidden_rows(attended, column_block(tokens, rank, part), sends)
    first = (group * local_experts).reshape(1)
    pieces = [sent] + [shift_ranks(sent, step, ranks) for step in range(1, ranks)]

    rows_sent, normed_two, logits, scale_two = route_rows(
        rank, dispatch, ffn_gain, w_router, pieces
    )
    unit_two_part = hidden_part * scale_two
    sigmas = jax.nn.sigmoid(logits) * chosen_mask
    sigma_total = jnp.sum(sigmas, axis=-1, keepdims=True)
    arrived = lax.all_to_all(
        rows_sent.reshape(groups, per_group, -1), "expert", split_axis=0, concat_axis=0, tiled=True
    )
    chosen_rows, *grad_quarters = owner_rows(
        first, after(all_grads, normed_two), local_experts, capacity
    )
    grads_arrived = [lax.all_gather(rows, "tensor", axis=0) for rows in grad_quarters]

    shared_gate_pre = matmul(normed_two, shared_gate)
    shared_up_pre = matmul(normed_two, shared_up)
    shared_act = (jax.nn.silu(shared_gate_pre) * shared_up_pre).astype(bf16)
    shared_part = matmul(shared_act, shared_down)
    grad_shared_act = matmul_nt(cotangent, shared_down)
    shared_gate_grad, shared_up_grad = silu_back(grad_shared_act, shared_gate_pre, shared_up_pre)
    norm_part = matmul_nt(shared_gate_grad, shared_gate) + matmul_nt(shared_up_grad, shared_up)
    shared_dot = jnp.sum(
        shared_gate_grad.astype(f32) * shared_gate_pre + shared_up_grad.astype(f32) * shared_up_pre,
        axis=-1, keepdims=True,
    )
    shared_grads = shared_weights(
        normed_two, cotangent, shared_gate_grad, shared_up_grad, shared_act, groups
    )

    width = -(-hidden_width // LANES) * LANES
    widen = ((0, 0), (0, width - hidden_width), (0, 0))
    gate_up = jnp.concatenate(
        [jnp.pad(expert_gate.transpose(0, 2, 1), widen), jnp.pad(expert_up.transpose(0, 2, 1), widen)],
        axis=1,
    )
    weights = (gate_up, jnp.pad(expert_down, widen))
    arrived = after(
        arrived, shared_grads, shared_part, norm_part, shared_dot, by_expert, *weights
    ).reshape(groups, local_experts, capacity, -1)
    pre_grad, act_weighted, back = expert_rows(
        0, first, arrived, chosen_rows, w_router, grads_arrived[0], weights, True
    )
    back = lax.psum_scatter(back, "tensor", scatter_dimension=0, tiled=True)[0]
    next_grad, next_weighted, direct, next_produced = expert_rows(
        1, first, arrived, chosen_rows, w_router, grads_arrived[1], weights, False
    )
    direct = lax.all_to_all(direct, "expert", split_axis=0, concat_axis=0, tiled=True)
    weight_grads = expert_weights(
        1, arrived, grads_arrived[1], next_grad, next_weighted, hidden_width
    )
    weight_grads = expert_weights(
        0, arrived, grads_arrived[0], pre_grad, act_weighted, hidden_width, weight_grads
    )
    direct = after(direct, *weight_grads).reshape(groups * capacity, -1)
    grad_expert_gate, grad_expert_up, grad_expert_down = weight_grads
    back = lax.all_to_all(
        after(back, direct), "expert", split_axis=0, concat_axis=0, tiled=True
    ).reshape(groups * capacity, -1)

    norm_grad, extra_low, *sends = combine_rows(
        rank, by_expert[:, 1], direct, norm_part, shared_dot, ranks
    )
    norm_pieces = [shift_ranks(sent, step + 1, ranks) for step, sent in enumerate(sends)]
    router_rows = lax.dynamic_slice_in_dim(w_router, rank * part, part, axis=0)
    ffn_gain_part = lax.dynamic_slice_in_dim(ffn_gain, rank * part, part, axis=0)
    hidden_grad, sent, logit_grad = norm_back(
        norm_grad, extra_low, by_expert[:, 0], back, chosen_mask, logits, scale_two, hidden_part,
        ffn_gain_part, router_rows, cotangent_part, norm_pieces,
    )
    pieces = [sent] + [shift_ranks(sent, step, ranks) for step in range(1, ranks)]

    (branch_low, grad_ffn_gain, query_pre_grad, keyvalue_grad, normed_grad, latent_sent,
     *sends) = attention_backward(
        rank, pieces, weights_full, keyvalue, key_rope, query_low, query_pre, tokens, scale_one, tables,
        w_output, w_keyvalue, w_query,
    )
    pieces = [latent_sent] + [shift_ranks(latent_sent, step, ranks) for step in range(1, ranks)]
    normed_pieces = [
        shift_ranks(after(sent, *pieces), step + 1, ranks) for step, sent in enumerate(sends)
    ]

    returned = lax.all_to_all(
        after(next_produced, back, *norm_pieces), "expert", split_axis=0, concat_axis=0, tiled=True
    ).reshape(groups * capacity, -1)
    latent_sent = after(latent_sent, returned)

    chunk = model_width // groups
    kv_chunk = KV_RANK // groups
    core = lax.rem(group, 2)
    mine, other = branch_weights(
        core, groups, normed, branch_low, latent_normed, query_pre_grad, attn_mixed, keyvalue_grad
    )
    late_columns = mine.shape[2] + w_latent.shape[1] + expert_count + LANES
    late = pair_sum(mine, swap_cores(other, groups), late_columns, 0)
    latent_grad, row_mean, mine, other = latent_weights(
        core, groups, normed, normed_two, tokens, w_latent, grad_ffn_gain, logit_grad, latent,
        latent_gain, tables[3], tables[4], scale_one, pieces,
    )
    shared_width = shared_gate.shape[1]
    early = lax.psum_scatter(
        after(shared_grads, direct).reshape(groups * 3 * chunk, shared_width), "expert",
        scatter_dimension=0, tiled=True,
    )
    branch, *sends = branch_rows(rank, by_expert[:, 1], after(returned, mine), shared_part, ranks)
    late = pair_sum(
        mine, swap_cores(after(other, returned), groups), late_columns,
        2, late,
    )
    late = lax.all_to_all(
        late, "expert", split_axis=0, concat_axis=0, tiled=True,
        axis_index_groups=[list(range(first_core, groups, 2)) for first_core in range(2)],
    )

    latent_rows = lax.dynamic_slice_in_dim(w_latent, rank * part, part, axis=0)
    attn_gain_part = lax.dynamic_slice_in_dim(attn_gain, rank * part, part, axis=0)
    block = jax.ShapeDtypeStruct((tok_rows, part), bf16)
    grad_tokens = single_call(
        token_kernel,
        [normed_grad, latent_grad, latent_rows, row_mean, column_block(tokens, rank, part), scale_one,
         attn_gain_part.reshape(1, part), hidden_grad, *normed_pieces],
        [block], "token_rows",
    )[0]
    grad_tokens = ordered_columns(
        rank, [grad_tokens] + [shift_ranks(grad_tokens, step, ranks) for step in range(1, ranks)]
    )
    sends = [shift_ranks(sent, step + 1, ranks) for step, sent in enumerate(sends)]
    output = single_call(
        output_kernel, [branch, hidden_part, by_expert[:, 0], back, *sends],
        [block], "output_rows",
    )[0]
    output = ordered_columns(
        rank, [output] + [shift_ranks(output, step, ranks) for step in range(1, ranks)]
    )

    early = after(early, output).astype(f32)
    grad_shared_gate = early[:chunk]
    grad_shared_up = early[chunk:2 * chunk]
    grad_shared_down = early[2 * chunk:].T

    edges = [0]
    for columns in (
        query_pre_grad.shape[1], attn_mixed.shape[1],
        keyvalue_grad.shape[1] * KV_RANK // model_width, latent_grad.shape[1], expert_count, LANES,
    ):
        edges.append(edges[-1] + columns)
    shapes = [
        jax.ShapeDtypeStruct((chunk, high - low), f32) for low, high in zip(edges[:-1], edges[1:])
    ]
    shapes[2] = jax.ShapeDtypeStruct((kv_chunk, keyvalue_grad.shape[1]), f32)
    shapes[5:] = [jax.ShapeDtypeStruct((1, chunk), f32)] * 3
    grad_query, grad_output, grad_keyvalue, grad_latent, grad_router, *gains = final_sums(
        after(late, grad_shared_gate, grad_shared_up, grad_shared_down), tuple(edges), shapes
    )
    return (
        output,
        grad_tokens,
        gains[0].reshape(chunk),
        grad_query,
        grad_latent,
        gains[2][0, :kv_chunk],
        grad_keyvalue,
        grad_output.T,
        gains[1].reshape(chunk),
        grad_router,
        grad_shared_gate,
        grad_shared_up,
        grad_shared_down,
        grad_expert_gate.transpose(0, 2, 1),
        grad_expert_up.transpose(0, 2, 1),
        grad_expert_down,
    )


def solution(mesh):
    return jax.shard_map(
        shards,
        mesh=mesh,
        in_specs=(
            P("expert", None),
            P("expert", None),
            P(),
            P(None, "tensor"),
            P(),
            P(),
            P(None, "tensor"),
            P("tensor", None),
            P(),
            P(),
            P(None, "tensor"),
            P(None, "tensor"),
            P("tensor", None),
            P("expert", None, "tensor"),
            P("expert", None, "tensor"),
            P("expert", "tensor", None),
            P("expert", None),
        ),
        out_specs=(
            P("expert", None),
            P("expert", None),
            P("expert"),
            P("expert", "tensor"),
            P("expert", None),
            P("expert"),
            P("expert", "tensor"),
            P("tensor", "expert"),
            P("expert"),
            P("expert", None),
            P("expert", "tensor"),
            P("expert", "tensor"),
            P("tensor", "expert"),
            P("expert", None, "tensor"),
            P("expert", None, "tensor"),
            P("expert", "tensor", None),
        ),
        check_vma=False,
    )
```

```python
import functools

import jax
import jax.numpy as jnp
import numpy as np
from jax import lax
from jax.experimental import pallas as pl
from jax.experimental.pallas import tpu as pltpu
from jax.sharding import PartitionSpec as P

NOPE = 128
ROPE = 64
VDIM = 128
KV_RANK = 512


EPS = 1e-06
THETA = 50000.0
ROUTE_SCALE = 2.446
MASKED = -1e30
LANES = 128
VMEM_BYTES = 60 * 1024 * 1024


def silu_back(grad_act, gate_pre, up_pre):
    sigma_gate = jax.nn.sigmoid(gate_pre)
    grad_up = grad_act * gate_pre * sigma_gate
    grad_gate = grad_act * up_pre * sigma_gate * (1.0 + gate_pre * (1.0 - sigma_gate))
    return (grad_gate.astype(jnp.bfloat16), grad_up.astype(jnp.bfloat16))


def matmul(left_side, right_side):
    return jnp.dot(left_side, right_side, preferred_element_type=jnp.float32)


def matmul_tn(left_side, right_side):
    return lax.dot_general(
        left_side, right_side, (((0,), (0,)), ((), ())), preferred_element_type=jnp.float32
    )


def matmul_nt(left_side, right_side):
    return lax.dot_general(
        left_side, right_side, (((1,), (1,)), ((), ())), preferred_element_type=jnp.float32
    )


def after(value, *others):
    return lax.optimization_barrier((value,) + others)[0]


def shift_ranks(values, step, count):
    return lax.ppermute(values, "tensor", [(i, (i + step) % count) for i in range(count)])


def column_block(values, index, width):
    return lax.dynamic_slice_in_dim(values, index * width, width, axis=1)


def expert_rows_kernel(sideways, first_ref, x_ref, mask_ref, router_ref, g_ref, wgu_ref, wd_ref, *rest):
    dgu_ref, actw_ref, rowgrad_ref, other_ref = rest[-4:]
    quarters, step, cap, part = g_ref.shape
    rows = step * cap
    width, model = wd_ref.shape
    half = LANES // 2
    expert = first_ref[0]
    experts = router_ref.shape[1]
    x_rows = x_ref[...].reshape(rows, model)
    mask = mask_ref[...].reshape(rows, LANES)[:, :experts].astype(jnp.float32)
    sigmas = mask / (1.0 + jnp.exp(-matmul(x_rows, router_ref[...])))
    total = jnp.sum(sigmas, axis=1, keepdims=True)
    column = lax.broadcasted_iota(jnp.int32, sigmas.shape, 1)
    own = jnp.sum(jnp.where(column == expert, sigmas, 0.0), axis=1, keepdims=True)
    weight = jnp.where(total > 0.0, ROUTE_SCALE * own / jnp.where(total > 0.0, total, 1.0), 0.0)
    column = lax.broadcasted_iota(jnp.int32, (rows, LANES), 1)

    pre = matmul_nt(x_rows, wgu_ref[...])
    grad_act = matmul_nt(g_ref[0].reshape(rows, part), wd_ref[:, :part])
    for place in range(1, quarters):
        grad_act += matmul_nt(
            g_ref[place].reshape(rows, part), wd_ref[:, place * part:(place + 1) * part]
        )
    gate_pre = pre[:, :width]
    up_pre = pre[:, width:]
    sigma = 1.0 / (1.0 + jnp.exp(-gate_pre))
    silu = gate_pre * sigma
    act = silu * up_pre
    act_weighted = (act * weight).astype(jnp.bfloat16)
    actw_ref[...] = act_weighted
    out = matmul(act_weighted, wd_ref[...]).astype(jnp.bfloat16)
    if sideways:
        for place in range(quarters):
            rowgrad_ref[place, :, :, part:] = (
                out[:, place * part:(place + 1) * part].reshape(step, cap, part)
            )
    else:
        other_ref[...] = out.reshape(step, cap, model)
    dot = jnp.sum(grad_act * act, axis=1, keepdims=True)
    grad_act = grad_act * weight
    grad_up = grad_act * silu
    grad_gate = grad_act * up_pre * (sigma + silu * (1.0 - sigma))
    row_dot = jnp.sum(grad_gate * gate_pre + grad_up * up_pre, axis=1, keepdims=True)
    row_dot_high = row_dot.astype(jnp.bfloat16).astype(jnp.float32)
    pre_grad = jnp.concatenate([grad_gate, grad_up], axis=1).astype(jnp.bfloat16)
    dgu_ref[...] = pre_grad
    row_grad = matmul(pre_grad, wgu_ref[...]).astype(jnp.bfloat16)
    sums = jnp.where(column == expert, dot, 0.0)
    sums = jnp.where(column == half, row_dot_high, sums)
    sums = jnp.where(column == half + 1, row_dot - row_dot_high, sums)
    sums = sums.astype(jnp.bfloat16).reshape(step, cap, LANES)
    if sideways:
        for place in range(quarters):
            rowgrad_ref[place, :, :, :part] = (
                row_grad[:, place * part:(place + 1) * part].reshape(step, cap, part)
            )
        other_ref[...] = sums
    else:
        rowgrad_ref[:, :, :model] = row_grad.reshape(step, cap, model)
        rowgrad_ref[:, :, model:model + LANES] = sums
        rowgrad_ref[:, :, model + LANES:] = rest[0][...]


def expert_rows(number, first, x, mask, router, g, weights, before=None):
    sources, experts, cap, model = x.shape
    quarters, _, _, part = g.shape
    gate_up, down = weights
    width = down.shape[1]
    step = 8
    rows = step * cap
    total = sources * cap
    sideways = before is None

    def flat_block(columns):
        return pl.BlockSpec((rows, columns), lambda b, f: (b, 0))

    def whole(*shape):
        return pl.BlockSpec((None,) + shape, lambda b, f: (number, 0, 0))

    def kind(*shape):
        return jax.ShapeDtypeStruct(shape, jnp.bfloat16)

    def part_block(columns):
        return pl.BlockSpec((quarters, step, cap, columns), lambda b, f: (0, b, 0, 0))

    def row_block(columns):
        return pl.BlockSpec((step, cap, columns), lambda b, f: (b, 0, 0))

    def expert_block(columns):
        return pl.BlockSpec((step, None, cap, columns), lambda b, f: (b, number, 0, 0))

    in_specs = [
        expert_block(model), expert_block(LANES), pl.BlockSpec(router.shape, lambda b, f: (0, 0)),
        part_block(part), whole(2 * width, model), whole(width, model),
    ]
    inputs = () if sideways else (before,)
    in_specs += [row_block(LANES)] * len(inputs)
    return pl.pallas_call(
        functools.partial(expert_rows_kernel, sideways),
        grid_spec=pltpu.PrefetchScalarGridSpec(
            num_scalar_prefetch=1,
            grid=(sources // step,),
            in_specs=in_specs,
            out_specs=[flat_block(2 * width), flat_block(width)] + (
                [part_block(2 * part), row_block(LANES)] if sideways
                else [row_block(model + 2 * LANES), row_block(model)]
            ),
        ),
        out_shape=[kind(total, 2 * width), kind(total, width)] + (
            [kind(quarters, sources, cap, 2 * part), kind(sources, cap, LANES)] if sideways
            else [kind(sources, cap, model + 2 * LANES), kind(sources, cap, model)]
        ),
        compiler_params=pltpu.CompilerParams(vmem_limit_bytes=VMEM_BYTES),
        cost_estimate=pl.CostEstimate(
            flops=2 * total * model * width * 6, bytes_accessed=30_000_000,
            transcendentals=total * width,
        ),
        name=f"expert_rows_{number}",
    )(first + number, x, mask, router, g, gate_up, down, *inputs)


def expert_weights_kernel(x_ref, g_ref, dgu_ref, actw_ref, *rest):
    gate_ref, up_ref, down_ref = rest[-3:]
    rows, width = actw_ref.shape
    hidden = gate_ref.shape[0]
    grad = matmul_tn(dgu_ref[...], x_ref[...].reshape(rows, x_ref.shape[-1]))
    gate_ref[...] = grad[:hidden, :]
    up_ref[...] = grad[width:width + hidden, :]
    g_rows = g_ref[...].reshape(rows, g_ref.shape[-1])
    down_ref[...] = matmul_tn(actw_ref[...], g_rows)[:hidden, :]


def expert_weights(number, x, g, dgu, actw, hidden, before=()):
    quarters = g.shape[0]
    sources, experts, cap, model = x.shape
    total, width = actw.shape
    steps = 8
    part = model // steps
    per = steps // quarters
    x_block = pl.BlockSpec((sources, None, cap, part), lambda b: (0, number, 0, b))
    in_specs = [
        x_block,
        pl.BlockSpec((None, sources, cap, part), lambda b: (b // per, 0, 0, b % per)),
        pl.BlockSpec((total, 2 * width), lambda b: (0, 0)),
        pl.BlockSpec((total, width), lambda b: (0, 0)),
    ] + [pl.BlockSpec(memory_space=pl.ANY)] * len(before)
    return pl.pallas_call(
        expert_weights_kernel,
        grid=(steps,),
        in_specs=in_specs,
        out_specs=[pl.BlockSpec((None, hidden, part), lambda b: (number, 0, b))] * 3,
        out_shape=[jax.ShapeDtypeStruct((experts, hidden, model), jnp.float32)] * 3,
        compiler_params=pltpu.CompilerParams(vmem_limit_bytes=VMEM_BYTES),
        cost_estimate=pl.CostEstimate(
            flops=2 * total * model * width * 3, bytes_accessed=22_000_000, transcendentals=0
        ),
        input_output_aliases={4 + place: place for place in range(len(before))},
        name=f"expert_weights_{number}",
    )(x, g, dgu, actw, *before)


def shared_weights_kernel(n_ref, c_ref, gate_ref, up_ref, act_ref, out_ref):
    chunk = out_ref.shape[1] // 3
    for place, (rows, grads) in enumerate(
        ((n_ref, gate_ref), (n_ref, up_ref), (c_ref, act_ref))
    ):
        grad = matmul_tn(rows[...], grads[...]).astype(jnp.bfloat16)
        for group in range(out_ref.shape[0]):
            out_ref[group, place * chunk:(place + 1) * chunk, :] = (
                grad[group * chunk:(group + 1) * chunk, :]
            )


def shared_weights(normed, cotangent, gate_grad, up_grad, act, groups):
    tokens, model = normed.shape
    width = gate_grad.shape[1]
    block = 256
    chunk = model // groups
    per = block // chunk
    rows = pl.BlockSpec((tokens, block), lambda i: (0, i))
    grads = pl.BlockSpec((tokens, width), lambda i: (0, 0))
    return pl.pallas_call(
        shared_weights_kernel,
        grid=(model // block,),
        in_specs=[rows, rows, grads, grads, grads],
        out_specs=pl.BlockSpec((per, 3 * chunk, width), lambda i: (i, 0, 0)),
        out_shape=jax.ShapeDtypeStruct((groups, 3 * chunk, width), jnp.bfloat16),
        compiler_params=pltpu.CompilerParams(vmem_limit_bytes=VMEM_BYTES),
        cost_estimate=pl.CostEstimate(
            flops=6 * tokens * model * width, bytes_accessed=14_000_000, transcendentals=0
        ),
        name="shared_weights",
    )(normed, cotangent, gate_grad, up_grad, act)


def combine_kernel(rank_ref, pick_ref, other_pick_ref, back_ref, sums_ref, other_sums_ref, shared_ref, dots_ref,
                   own_ref, extra_ref, *sends):
    step = pl.program_id(0)
    count = pl.num_programs(0)
    place = lax.rem(step - rank_ref[0] + count, count)
    part = own_ref.shape[1]
    value = matmul(pick_ref[...], back_ref[...]) + shared_ref[...]

    @pl.when(place == 0)
    def _():
        own_ref[...] = value

    for number, send in enumerate(sends):
        @pl.when(place == number + 1)
        def _():
            send[:, :part] = value.astype(jnp.bfloat16)

    @pl.when(step == count - 1)
    def _():
        mark = LANES // 2
        sums = matmul(pick_ref[...], sums_ref[...]) + matmul(
            other_pick_ref[...], other_sums_ref[...]
        )
        column = lax.broadcasted_iota(jnp.int32, sums.shape, 1)
        mean = dots_ref[...] + jnp.sum(
            jnp.where((column == mark) | (column == mark + 1), sums, 0.0), axis=1, keepdims=True
        )
        mean_high = mean.astype(jnp.bfloat16).astype(jnp.float32)
        extra = jnp.where(column < mark, sums, 0.0)
        extra = jnp.where(column == mark, mean_high, extra)
        extra = jnp.where(column == mark + 1, mean - mean_high, extra).astype(jnp.bfloat16)
        extra_ref[...] = extra
        for send in sends:
            send[:, part:] = extra


def combine_rows(rank, pick, other_pick, back, shared, dots, count):
    tokens, slots = pick.shape
    model = shared.shape[1]
    part = model // count
    sent = jax.ShapeDtypeStruct((tokens, part + LANES), jnp.bfloat16)
    sent_block = pl.BlockSpec((tokens, part + LANES), lambda i, r: (0, 0))
    return pl.pallas_call(
        combine_kernel,
        grid_spec=pltpu.PrefetchScalarGridSpec(
            num_scalar_prefetch=1,
            grid=(count,),
            in_specs=[
                pl.BlockSpec((tokens, slots), lambda i, r: (0, 0)),
                pl.BlockSpec((tokens, slots), lambda i, r: (0, 0)),
                pl.BlockSpec((slots, part), lambda i, r: (0, i)),
                pl.BlockSpec((slots, LANES), lambda i, r: (0, model // LANES)),
                pl.BlockSpec((slots, LANES), lambda i, r: (0, model // LANES + 1)),
                pl.BlockSpec((tokens, part), lambda i, r: (0, i)),
                pl.BlockSpec((tokens, 1), lambda i, r: (0, 0)),
            ],
            out_specs=[
                pl.BlockSpec((tokens, part), lambda i, r: (0, 0)),
                pl.BlockSpec((tokens, LANES), lambda i, r: (0, 0)),
            ] + [sent_block] * (count - 1),
        ),
        out_shape=[
            jax.ShapeDtypeStruct((tokens, part), jnp.float32),
            jax.ShapeDtypeStruct((tokens, LANES), jnp.bfloat16),
        ] + [sent] * (count - 1),
        compiler_params=pltpu.CompilerParams(vmem_limit_bytes=VMEM_BYTES),
        cost_estimate=pl.CostEstimate(
            flops=2 * tokens * slots * model, bytes_accessed=9_000_000, transcendentals=0
        ),
        name="combine_rows",
    )(rank.reshape(1), pick, other_pick, back, back, back, shared, dots)


def branch_kernel(rank_ref, pick_ref, back_ref, shared_ref, own_ref, *sends):
    step = pl.program_id(0)
    count = pl.num_programs(0)
    place = lax.rem(step - rank_ref[0] + count, count)
    value = matmul(pick_ref[...], back_ref[...]) + shared_ref[...]

    @pl.when(place == 0)
    def _():
        own_ref[...] = value

    for number, send in enumerate(sends):
        @pl.when(place == number + 1)
        def _():
            send[...] = value.astype(jnp.bfloat16)


def branch_rows(rank, pick, back, shared, count):
    tokens, slots = pick.shape
    model = shared.shape[1]
    part = model // count
    fixed = pl.BlockSpec((tokens, part), lambda i, r: (0, 0))
    return pl.pallas_call(
        branch_kernel,
        grid_spec=pltpu.PrefetchScalarGridSpec(
            num_scalar_prefetch=1,
            grid=(count,),
            in_specs=[
                pl.BlockSpec((tokens, slots), lambda i, r: (0, 0)),
                pl.BlockSpec((slots, part), lambda i, r: (0, i)),
                pl.BlockSpec((tokens, part), lambda i, r: (0, i)),
            ],
            out_specs=[fixed] * count,
        ),
        out_shape=[jax.ShapeDtypeStruct((tokens, part), jnp.float32)]
        + [jax.ShapeDtypeStruct((tokens, part), jnp.bfloat16)] * (count - 1),
        compiler_params=pltpu.CompilerParams(vmem_limit_bytes=VMEM_BYTES),
        cost_estimate=pl.CostEstimate(flops=0, bytes_accessed=4_000_000, transcendentals=0),
        name="branch_rows",
    )(rank.reshape(1), pick, back, shared)


def token_kernel(own_ref, latent_grad_ref, w_latent_ref, mean_ref, token_ref, scale_ref, gain_ref, hidden_ref,
                 *rest):
    *pieces, out_ref = rest
    grad = own_ref[...] + matmul_nt(latent_grad_ref[...], w_latent_ref[...])
    for piece in pieces:
        grad = grad + piece[...].astype(jnp.float32)
    scale = scale_ref[...]
    unit = token_ref[...].astype(jnp.float32) * scale
    grad = hidden_ref[...] + scale * (grad * gain_ref[...] - unit * mean_ref[...])
    out_ref[...] = grad.astype(jnp.bfloat16)


def output_kernel(own_ref, hidden_ref, pick_ref, back_ref, *rest):
    *pieces, out_ref = rest
    low = back_ref.shape[1] - out_ref.shape[1]
    value = hidden_ref[...] + own_ref[...] + matmul(pick_ref[...], back_ref[:, low:])
    for piece in pieces:
        value = value + piece[...].astype(jnp.float32)
    out_ref[...] = value.astype(jnp.bfloat16)


def attention_forward_kernel(rank_ref, token_ref, gain_ref, latent_gain_ref, cosine_ref, ahead_ref,
                             behind_ref, key_cosine_ref, key_sine_ref, w_latent_ref, w_query_ref,
                             w_keyvalue_ref, w_output_ref,
                             normed_ref, scale_ref, query_ref, query_low_ref, latent_ref,
                             latent_normed_ref, keyvalue_ref, key_rope_ref, weights_ref, mixed_ref,
                             own_ref, *rest):
    *sends, latent_buf, query_buf, keyvalue_buf, output_buf, sems = rest
    copies = [
        pltpu.make_async_copy(source, buffer, sems.at[number])
        for number, (source, buffer) in enumerate((
            (w_latent_ref, latent_buf), (w_query_ref, query_buf), (w_keyvalue_ref, keyvalue_buf),
            (w_output_ref, output_buf),
        ))
    ]
    for copy in copies:
        copy.start()
    tokens = token_ref[...].astype(jnp.float32)
    scale = lax.rsqrt(jnp.mean(tokens * tokens, axis=1, keepdims=True) + EPS)
    scale_ref[...] = scale
    normed = (tokens * scale * gain_ref[...]).astype(jnp.bfloat16)
    normed_ref[...] = normed
    copies[0].wait()
    latent = matmul_nt(normed, latent_buf[...])
    latent_ref[...] = latent
    compressed = latent[:, :KV_RANK]
    latent_scale = lax.rsqrt(jnp.mean(compressed * compressed, axis=1, keepdims=True) + EPS)
    latent_normed = (compressed * latent_scale * latent_gain_ref[...]).astype(jnp.bfloat16)
    latent_normed_ref[...] = latent_normed
    half = ROPE // 2
    former = latent[:, KV_RANK:KV_RANK + half]
    latter = latent[:, KV_RANK + half:]
    key_cosine, key_sine = key_cosine_ref[...], key_sine_ref[...]
    key_rope = jnp.concatenate(
        [former * key_cosine - latter * key_sine, latter * key_cosine + former * key_sine], axis=1
    ).astype(jnp.bfloat16)
    key_rope_ref[...] = key_rope
    copies[1].wait()
    query = matmul(normed, query_buf[...])
    query_ref[...] = query
    wide = query.shape[1]
    query_low_ref[...] = (
        query * cosine_ref[...] + pltpu.roll(query, wide - half, 1) * ahead_ref[...]
        + pltpu.roll(query, half, 1) * behind_ref[...]
    ).astype(jnp.bfloat16)
    copies[2].wait()
    keyvalue_ref[...] = matmul(latent_normed, keyvalue_buf[...]).astype(jnp.bfloat16)
    rows = tokens.shape[0]
    causal = (
        lax.broadcasted_iota(jnp.int32, (rows, rows), 0)
        >= lax.broadcasted_iota(jnp.int32, (rows, rows), 1)
    )
    qk_width = NOPE + ROPE
    for head in range(wide // qk_width):
        low = head * (NOPE + VDIM)
        query_head = query_low_ref[:, head * qk_width:(head + 1) * qk_width]
        key_head = jnp.concatenate([keyvalue_ref[:, low:low + NOPE], key_rope], axis=1)
        scores = matmul_nt(query_head, key_head) * (qk_width ** -0.5)
        scores = jnp.where(causal, scores, MASKED)
        terms = jnp.exp(scores - jnp.max(scores, axis=1, keepdims=True))
        weights = terms / jnp.sum(terms, axis=1, keepdims=True)
        weights_ref[head] = weights
        mixed_ref[:, head * VDIM:(head + 1) * VDIM] = matmul(
            weights.astype(jnp.bfloat16), keyvalue_ref[:, low + NOPE:low + NOPE + VDIM]
        ).astype(jnp.bfloat16)
    copies[3].wait()
    part = own_ref.shape[1]
    count = len(sends) + 1
    for number in range(count):
        value = matmul(mixed_ref[...], output_buf[:, number * part:(number + 1) * part])
        place = lax.rem(number - rank_ref[0] + count, count)

        @pl.when(place == 0)
        def _():
            own_ref[...] = value

        for index, send in enumerate(sends):
            @pl.when(place == index + 1)
            def _():
                send[...] = value.astype(jnp.bfloat16)


def rotary_constants(rows, heads):
    half = ROPE // 2
    frequency = np.float32(THETA) ** (np.arange(half, dtype=np.float32) * np.float32(-2.0 / ROPE))
    angles = np.arange(rows, dtype=np.float32)[:, None] * frequency[None, :]
    cosine, sine = np.cos(angles), np.sin(angles)
    blank = np.zeros((rows, NOPE), np.float32)
    zero = np.zeros((rows, half), np.float32)

    def tiled(*pieces):
        return np.tile(np.concatenate(pieces, axis=1), (1, heads)).astype(np.float32)

    return (
        tiled(blank + 1.0, cosine, cosine), tiled(blank, -sine, zero), tiled(blank, zero, sine),
        cosine, sine,
    )


def full_specs(arrays):
    return [pl.BlockSpec(a.shape, lambda i, r, n=len(a.shape): (0,) * n) for a in arrays]


def attention_forward(rank, tokens, gain, latent_gain, tables, w_latent, w_query, w_keyvalue, w_output,
                      count):
    rows, model = tokens.shape
    part = model // count
    latent_width = w_latent.shape[1]
    query_width = w_query.shape[1]
    heads = query_width // (NOPE + ROPE)
    bf16, f32 = jnp.bfloat16, jnp.float32
    out_shape = [
        jax.ShapeDtypeStruct(shape, kind)
        for shape, kind in (
            ((rows, model), bf16), ((rows, 1), f32), ((rows, query_width), f32),
            ((rows, query_width), bf16), ((rows, latent_width), f32), ((rows, KV_RANK), bf16),
            ((rows, w_keyvalue.shape[1]), bf16), ((rows, ROPE), bf16), ((heads, rows, rows), f32),
            ((rows, heads * VDIM), bf16), ((rows, part), f32),
        ) + (((rows, part), bf16),) * (count - 1)
    ]
    inputs = [tokens, gain.reshape(1, -1), latent_gain.reshape(1, -1), *tables]
    streamed = [w_latent.T, w_query, w_keyvalue, w_output]
    return pl.pallas_call(
        attention_forward_kernel,
        grid_spec=pltpu.PrefetchScalarGridSpec(
            num_scalar_prefetch=1,
            grid=(1,),
            in_specs=full_specs(inputs) + [pl.BlockSpec(memory_space=pl.ANY)] * len(streamed),
            out_specs=full_specs(out_shape),
            scratch_shapes=[pltpu.VMEM(a.shape, a.dtype) for a in streamed]
            + [pltpu.SemaphoreType.DMA((len(streamed),))],
        ),
        out_shape=out_shape,
        compiler_params=pltpu.CompilerParams(vmem_limit_bytes=VMEM_BYTES),
        cost_estimate=pl.CostEstimate(
            flops=5_000_000_000, bytes_accessed=16_000_000, transcendentals=300_000
        ),
        name="attention_forward",
    )(rank.reshape(1), *inputs, *streamed)


def attention_backward_kernel(rank_ref, *refs):
    count = 4
    pieces, refs = refs[:count], refs[count:]
    (weights_ref, keyvalue_ref, key_rope_ref, query_low_ref, query_ref, token_ref, scale_ref, cosine_ref,
     ahead_ref, behind_ref, w_output_ref, w_keyvalue_ref, w_query_ref,
     branch_ref, gain_ref, query_grad_ref, keyvalue_grad_ref, own_ref, latent_ref, *rest) = refs
    *sends, output_buf, keyvalue_buf, query_buf, grad_buf, sems = rest
    copies = [
        pltpu.make_async_copy(source, buffer, sems.at[number])
        for number, (source, buffer) in enumerate((
            (w_output_ref, output_buf), (w_keyvalue_ref, keyvalue_buf), (w_query_ref, query_buf),
        ))
    ]
    for copy in copies:
        copy.start()
    rows, model = branch_ref.shape
    part = own_ref.shape[1]
    for place in range(count):
        columns = slice(place * part, (place + 1) * part)
        turn = lax.rem(rank_ref[0] - place + count, count)
        for number, piece in enumerate(pieces):
            @pl.when(turn == number)
            def _():
                branch_ref[:, columns] = piece[:rows, :]
                sums = piece[rows:, :].astype(jnp.float32)
                gain_ref[:, columns] = sums[0:1] + sums[1:2]
    copies[0].wait()
    mixed_grad = matmul_nt(branch_ref[...], output_buf[...]).astype(jnp.bfloat16)
    qk_width = NOPE + ROPE
    soft = qk_width ** -0.5
    key_rope = key_rope_ref[...]
    rope_grad = jnp.zeros((rows, ROPE), jnp.float32)
    for head in range(weights_ref.shape[0]):
        low = head * (NOPE + VDIM)
        columns = slice(head * qk_width, (head + 1) * qk_width)
        weights = weights_ref[head]
        out_grad = mixed_grad[:, head * VDIM:(head + 1) * VDIM]
        keyvalue_grad_ref[:, low + NOPE:low + NOPE + VDIM] = matmul_tn(
            weights.astype(jnp.bfloat16), out_grad
        ).astype(jnp.bfloat16)
        prob_grad = matmul_nt(out_grad, keyvalue_ref[:, low + NOPE:low + NOPE + VDIM])
        row_term = jnp.sum(weights * prob_grad, axis=1, keepdims=True)
        score_grad = (weights * (prob_grad - row_term)).astype(jnp.bfloat16)
        key_head = jnp.concatenate([keyvalue_ref[:, low:low + NOPE], key_rope], axis=1)
        grad_buf[:, columns] = matmul(score_grad, key_head) * soft
        key_grad = matmul_tn(score_grad, query_low_ref[:, columns]) * soft
        keyvalue_grad_ref[:, low:low + NOPE] = key_grad[:, :NOPE].astype(jnp.bfloat16)
        rope_grad += key_grad[:, NOPE:]
    grad = grad_buf[...]
    wide = grad.shape[1]
    half = ROPE // 2
    query_grad = (
        grad * cosine_ref[...] - pltpu.roll(grad, wide - half, 1) * ahead_ref[...]
        - pltpu.roll(grad, half, 1) * behind_ref[...]
    ).astype(jnp.bfloat16)
    query_grad_ref[...] = query_grad
    mean = jnp.sum(query_grad.astype(jnp.float32) * query_ref[...], axis=1, keepdims=True)
    mean_high = mean.astype(jnp.bfloat16).astype(jnp.float32)
    copies[1].wait()
    latent_part = matmul_nt(keyvalue_grad_ref[...], keyvalue_buf[...])
    width = latent_part.shape[1]
    column = lax.broadcasted_iota(jnp.int32, (rows, LANES - ROPE), 1)
    sums = jnp.where(column == 0, mean_high, jnp.where(column == 1, mean - mean_high, 0.0))
    latent_ref[:rows, :width] = latent_part.astype(jnp.bfloat16)
    latent_ref[:rows, width:] = jnp.concatenate([rope_grad, sums], axis=1).astype(jnp.bfloat16)
    copies[2].wait()
    gains = []
    scale = scale_ref[...]
    for number in range(count):
        columns = slice(number * part, (number + 1) * part)
        value = matmul_nt(query_grad, query_buf[columns, :])
        unit = token_ref[:, columns].astype(jnp.float32) * scale
        gains.append(jnp.sum(value * unit, axis=0, keepdims=True))
        place = lax.rem(number - rank_ref[0] + count, count)

        @pl.when(place == 0)
        def _():
            own_ref[...] = value

        for index, send in enumerate(sends):
            @pl.when(place == index + 1)
            def _():
                send[...] = value.astype(jnp.bfloat16)
    highs = [gain.astype(jnp.bfloat16).astype(jnp.float32) for gain in gains]
    lows = [gain - high for gain, high in zip(gains, highs)]
    spare = latent_ref.shape[0] - rows
    latent_ref[rows:, :width] = jnp.concatenate(
        highs + lows + [jnp.zeros((spare - 2 * count, part), jnp.float32)], axis=0
    ).astype(jnp.bfloat16)
    latent_ref[rows:, width:] = jnp.zeros((spare, LANES), jnp.bfloat16)


def attention_backward(rank, pieces, weights, keyvalue, key_rope, query_low, query, tokens, scale, tables,
                       w_output, w_keyvalue, w_query):
    rows, model = tokens.shape
    count = len(pieces)
    part = model // count
    wide = query.shape[1]
    kv_width = keyvalue.shape[1]
    sent_rows = pieces[0].shape[0]
    bf16, f32 = jnp.bfloat16, jnp.float32
    sent_width = KV_RANK + LANES
    out_shape = [
        jax.ShapeDtypeStruct(shape, kind)
        for shape, kind in (
            ((rows, model), bf16), ((1, model), f32), ((rows, wide), bf16), ((rows, kv_width), bf16),
            ((rows, part), f32), ((sent_rows, sent_width), bf16),
        ) + (((rows, part), bf16),) * (count - 1)
    ]
    inputs = [*pieces, weights, keyvalue, key_rope, query_low, query, tokens, scale, *tables[:3]]
    streamed = [w_output, w_keyvalue, w_query]
    return pl.pallas_call(
        attention_backward_kernel,
        grid_spec=pltpu.PrefetchScalarGridSpec(
            num_scalar_prefetch=1,
            grid=(1,),
            in_specs=full_specs(inputs) + [pl.BlockSpec(memory_space=pl.ANY)] * len(streamed),
            out_specs=full_specs(out_shape),
            scratch_shapes=[pltpu.VMEM(a.shape, a.dtype) for a in streamed]
            + [pltpu.VMEM((rows, wide), f32), pltpu.SemaphoreType.DMA((len(streamed),))],
        ),
        out_shape=out_shape,
        compiler_params=pltpu.CompilerParams(vmem_limit_bytes=VMEM_BYTES),
        cost_estimate=pl.CostEstimate(
            flops=4_000_000_000, bytes_accessed=20_000_000, transcendentals=0
        ),
        name="attention_backward",
    )(rank.reshape(1), *inputs, *streamed)


def single_call(kernel, arrays, shapes, name):
    def specs(values):
        return [pl.BlockSpec(a.shape, lambda i, n=len(a.shape): (0,) * n) for a in values]

    return pl.pallas_call(
        kernel,
        grid=(1,),
        in_specs=specs(arrays),
        out_specs=specs(shapes),
        out_shape=shapes,
        compiler_params=pltpu.CompilerParams(vmem_limit_bytes=VMEM_BYTES),
        cost_estimate=pl.CostEstimate(flops=0, bytes_accessed=4_000_000, transcendentals=0),
        name=name,
    )(*arrays)


def hidden_kernel(own_ref, token_ref, *rest):
    *pieces, hidden_ref, sent_ref = rest
    value = own_ref[...] + token_ref[...].astype(jnp.float32)
    for piece in pieces:
        value = value + piece[...].astype(jnp.float32)
    hidden_ref[...] = value
    part = value.shape[1]
    total = jnp.sum(value * value, axis=1, keepdims=True)
    high = total.astype(jnp.bfloat16).astype(jnp.float32)
    column = lax.broadcasted_iota(jnp.int32, (value.shape[0], LANES), 1)
    sums = jnp.where(column == 0, high, jnp.where(column == 1, total - high, 0.0))
    sent_ref[:, :part] = value.astype(jnp.bfloat16)
    sent_ref[:, part:] = sums.astype(jnp.bfloat16)


def hidden_rows(own, token_block, pieces):
    tokens, part = own.shape
    shapes = [
        jax.ShapeDtypeStruct((tokens, part), jnp.float32),
        jax.ShapeDtypeStruct((tokens, part + LANES), jnp.bfloat16),
    ]
    return single_call(hidden_kernel, [own, token_block, *pieces], shapes, "hidden_rows")


def owner_rows_kernel(first_ref, block_ref, mask_ref, *out_refs):
    sources, rows, _ = block_ref.shape
    _, cap, part = out_refs[0].shape
    experts = len(out_refs)
    line = lax.broadcasted_iota(jnp.int32, (8, LANES), 0)
    column = lax.broadcasted_iota(jnp.int32, (8, LANES), 1)
    select = ((column == line + first_ref[0]) & (line < experts)).astype(jnp.bfloat16)
    earlier = (
        lax.broadcasted_iota(jnp.int32, (rows, rows), 0)
        < lax.broadcasted_iota(jnp.int32, (rows, rows), 1)
    ).astype(jnp.bfloat16)
    slot = lax.broadcasted_iota(jnp.int32, (cap, rows), 0).astype(jnp.float32)
    chosen = jnp.concatenate(
        [matmul_nt(select, block_ref[source, :, part:]) for source in range(sources)], axis=0
    )
    place = matmul(chosen.astype(jnp.bfloat16), earlier)
    for source in range(sources):
        picks = [
            jnp.where((slot == place[line:line + 1]) & (chosen[line:line + 1] > 0.5), 1.0, 0.0)
            for line in range(8 * source, 8 * source + experts)
        ]
        picks = jnp.concatenate(picks, axis=0).astype(jnp.bfloat16)
        out = matmul(picks, block_ref[source]).astype(jnp.bfloat16)
        mask_ref[source] = out[:, part:].reshape(experts, cap, LANES)
        for number, out_ref in enumerate(out_refs):
            out_ref[source] = out[number * cap:(number + 1) * cap, :part]


def owner_rows(first, gathered, experts, cap):
    groups, rows, wide = gathered.shape
    part = wide - LANES
    step = 16
    return pl.pallas_call(
        owner_rows_kernel,
        grid_spec=pltpu.PrefetchScalarGridSpec(
            num_scalar_prefetch=1,
            grid=(groups // step,),
            in_specs=[pl.BlockSpec((step, rows, wide), lambda i, f: (i, 0, 0))],
            out_specs=[pl.BlockSpec((step, experts, cap, LANES), lambda i, f: (i, 0, 0, 0))]
            + [pl.BlockSpec((step, cap, part), lambda i, f: (i, 0, 0))] * experts,
        ),
        out_shape=[jax.ShapeDtypeStruct((groups, experts, cap, LANES), jnp.bfloat16)]
        + [jax.ShapeDtypeStruct((groups, cap, part), jnp.bfloat16)] * experts,
        compiler_params=pltpu.CompilerParams(vmem_limit_bytes=VMEM_BYTES),
        cost_estimate=pl.CostEstimate(
            flops=2 * groups * experts * cap * rows * part, bytes_accessed=13_000_000,
            transcendentals=0,
        ),
        name="owner_rows",
    )(first, gathered)


def route_rows_kernel(rank_ref, dispatch_ref, gain_ref, router_ref, *rest):
    pieces, (rows_ref, wide_ref, logit_ref, scale_ref) = rest[:-4], rest[-4:]
    count = len(pieces)
    part = pieces[0].shape[1] - LANES
    model = count * part

    @pl.when(pl.program_id(0) == 0)
    def _():
        total = sum(jnp.sum(piece[:, part:].astype(jnp.float32), axis=1, keepdims=True)
                    for piece in pieces)
        scale = lax.rsqrt(total / model + EPS)
        scale_ref[...] = scale
        logits = jnp.zeros(logit_ref.shape, jnp.float32)
        for place in range(count):
            turn = lax.rem(rank_ref[0] - place + count, count)
            block = pieces[0][:, :part].astype(jnp.float32)
            for number in range(1, count):
                block = jnp.where(turn == number, pieces[number][:, :part].astype(jnp.float32),
                                  block)
            columns = slice(place * part, (place + 1) * part)
            block = (block * scale * gain_ref[:, columns]).astype(jnp.bfloat16)
            wide_ref[:, columns] = block
            logits += matmul(block, router_ref[columns, :])
        logit_ref[...] = logits

    rows_ref[...] = matmul(dispatch_ref[...], wide_ref[...]).astype(jnp.bfloat16)


def route_rows(rank, dispatch, gain, router, pieces):
    slots, tokens = dispatch.shape
    model, experts = router.shape
    block = 512

    def whole(*shape):
        return pl.BlockSpec(shape, lambda i, r: (0, 0))

    return pl.pallas_call(
        route_rows_kernel,
        grid_spec=pltpu.PrefetchScalarGridSpec(
            num_scalar_prefetch=1,
            grid=(slots // block,),
            in_specs=[
                pl.BlockSpec((block, tokens), lambda i, r: (i, 0)),
                whole(1, model), whole(model, experts),
            ] + [whole(*piece.shape) for piece in pieces],
            out_specs=[
                pl.BlockSpec((block, model), lambda i, r: (i, 0)),
                whole(tokens, model), whole(tokens, experts), whole(tokens, 1),
            ],
        ),
        out_shape=[
            jax.ShapeDtypeStruct((slots, model), jnp.bfloat16),
            jax.ShapeDtypeStruct((tokens, model), jnp.bfloat16),
            jax.ShapeDtypeStruct((tokens, experts), jnp.float32),
            jax.ShapeDtypeStruct((tokens, 1), jnp.float32),
        ],
        compiler_params=pltpu.CompilerParams(vmem_limit_bytes=VMEM_BYTES),
        cost_estimate=pl.CostEstimate(
            flops=2 * slots * tokens * model, bytes_accessed=13_000_000, transcendentals=0
        ),
        name="route_rows",
    )(rank.reshape(1), dispatch, gain.reshape(1, model), router, *pieces)


def norm_back_kernel(own_ref, extra_ref, pick_ref, back_ref, mask_ref, logit_ref, scale_ref, hidden_ref,
                     gain_ref, router_ref, cotangent_ref, *rest):
    *pieces, grad_ref, sent_ref, logit_grad_ref = rest
    part = own_ref.shape[1]
    rows, experts = mask_ref.shape
    model = part * (len(pieces) + 1)
    norm_grad = own_ref[...] + matmul(pick_ref[...], back_ref[:, :part])
    extra = extra_ref[...].astype(jnp.float32)
    for piece in pieces:
        norm_grad = norm_grad + piece[:, :part].astype(jnp.float32)
        extra = extra + piece[:, part:].astype(jnp.float32)
    logits = logit_ref[...]
    sigmas = mask_ref[...] / (1.0 + jnp.exp(-logits))
    total = jnp.sum(sigmas, axis=1, keepdims=True)
    gate_grad = extra[:, :experts]
    weighted_sum = jnp.sum(gate_grad * sigmas, axis=1, keepdims=True)
    sigma_grad = ROUTE_SCALE * (gate_grad / total - weighted_sum / (total * total))
    logit_grad = (sigma_grad * sigmas * (1.0 - sigmas)).astype(jnp.bfloat16)
    logit_grad_ref[...] = logit_grad
    norm_grad = norm_grad + matmul_nt(logit_grad, router_ref[...])
    mean = (
        jnp.sum(extra[:, experts:experts + 2], axis=1, keepdims=True)
        + jnp.sum(logit_grad.astype(jnp.float32) * logits, axis=1, keepdims=True)
    ) / model
    scale = scale_ref[...]
    unit = hidden_ref[...] * scale
    gain_grad = jnp.sum(norm_grad * unit, axis=0, keepdims=True)
    grad = cotangent_ref[...].astype(jnp.float32) + scale * (norm_grad * gain_ref[...] - unit * mean)
    grad_ref[...] = grad
    sent_ref[:rows, :] = grad.astype(jnp.bfloat16)
    high = gain_grad.astype(jnp.bfloat16).astype(jnp.float32)
    row = lax.broadcasted_iota(jnp.int32, (sent_ref.shape[0] - rows, part), 0)
    sums = jnp.where(row == 0, high, jnp.where(row == 1, gain_grad - high, 0.0))
    sent_ref[rows:, :] = sums.astype(jnp.bfloat16)


def norm_back(own, extra, pick, back, mask, logits, scale, hidden, gain, router, cotangent, pieces):
    rows, part = own.shape
    bf16, f32 = jnp.bfloat16, jnp.float32
    shapes = [
        jax.ShapeDtypeStruct((rows, part), f32), jax.ShapeDtypeStruct((rows + 16, part), bf16),
        jax.ShapeDtypeStruct(mask.shape, bf16),
    ]
    inputs = [own, extra, pick, back, mask, logits, scale, hidden, gain.reshape(1, part), router, cotangent]
    return single_call(norm_back_kernel, inputs + list(pieces), shapes, "norm_back")


def put_pairs(first, grad, row, column, mine_ref, other_ref):
    rows = slice(row, row + grad.shape[2])
    columns = slice(column, column + grad.shape[3])
    even, odd = grad[:, 0], grad[:, 1]
    mine_ref[:, rows, columns] = jnp.where(first, even, odd).astype(jnp.bfloat16)
    other_ref[:, rows, columns] = jnp.where(first, odd, even).astype(jnp.bfloat16)


def branch_weights_kernel(core_ref, n_ref, b_ref, l_ref, query_ref, mixed_ref, kv_ref, mine_ref, other_ref):
    pairs, chunk, _ = mine_ref.shape
    first = core_ref[0] == 0

    def by_pairs(grad):
        return grad.reshape(pairs, 2, grad.shape[0] // (2 * pairs), grad.shape[1])

    low = 0
    for rows_ref, grads in ((n_ref, query_ref), (b_ref, mixed_ref)):
        grad = matmul_tn(rows_ref[...], grads[...])
        put_pairs(first, by_pairs(grad), 0, low, mine_ref, other_ref)
        low += grad.shape[1]
    grad = by_pairs(matmul_tn(l_ref[...], kv_ref[...]))
    kv_chunk = grad.shape[2]
    columns = grad.shape[3] * kv_chunk // chunk
    for place in range(chunk // kv_chunk):
        put_pairs(first, grad[:, :, :, place * columns:(place + 1) * columns], place * kv_chunk, low,
                  mine_ref, other_ref)


def paired_call(kernel, core, groups, columns, blocked, whole, extra_shapes, scratch, name):
    steps = 4
    model = blocked[0].shape[1]
    chunk = model // groups
    out = pl.BlockSpec((groups // 2 // steps, chunk, columns), lambda i, c: (i, 0, 0))

    def fixed(array):
        return pl.BlockSpec(array.shape, lambda i, c: (0, 0))

    return pl.pallas_call(
        kernel,
        grid_spec=pltpu.PrefetchScalarGridSpec(
            num_scalar_prefetch=1,
            grid=(steps,),
            in_specs=[
                pl.BlockSpec((a.shape[0], a.shape[1] // steps), lambda i, c: (0, i)) for a in blocked
            ] + [fixed(a) for a in whole],
            out_specs=[fixed(a) for a in extra_shapes] + [out] * 2,
            scratch_shapes=scratch,
        ),
        out_shape=list(extra_shapes)
        + [jax.ShapeDtypeStruct((groups // 2, chunk, columns), jnp.bfloat16)] * 2,
        compiler_params=pltpu.CompilerParams(vmem_limit_bytes=VMEM_BYTES),
        cost_estimate=pl.CostEstimate(flops=0, bytes_accessed=10_000_000, transcendentals=0),
        name=name,
    )(core.reshape(1), *blocked, *whole)


def branch_weights(core, groups, normed, branch, latent_normed, query, mixed, kv):
    columns = (
        query.shape[1] + mixed.shape[1] + kv.shape[1] * latent_normed.shape[1] // normed.shape[1]
    )
    return paired_call(
        branch_weights_kernel, core, groups, columns, [normed, branch, latent_normed],
        [query, mixed, kv], [], [], "branch_weights",
    )


def latent_weights_kernel(core_ref, n_ref, t_ref, token_ref, w_latent_ref, ffn_ref, logit_ref, latent_ref,
                          latent_gain_ref, cosine_ref, sine_ref, scale_ref, *rest):
    *pieces, latent_grad_ref, mean_ref, mine_ref, other_ref, gain_buf, latent_gain_buf = rest
    step = pl.program_id(0)
    count = len(pieces)
    pairs, chunk, _ = mine_ref.shape
    rows = latent_ref.shape[0]
    block = n_ref.shape[1]
    first = core_ref[0] == 0

    @pl.when(step == 0)
    def _():
        total = sum(piece[...].astype(jnp.float32) for piece in pieces)
        for number in range(count):
            gain_buf[number] = (
                total[rows + number:rows + number + 1, :block]
                + total[rows + count + number:rows + count + number + 1, :block]
            )
        latent = latent_ref[...]
        compressed = latent[:, :KV_RANK]
        scale = lax.rsqrt(jnp.mean(compressed * compressed, axis=1, keepdims=True) + EPS)
        unit = compressed * scale
        grad = total[:rows, :KV_RANK]
        gains = jnp.sum(grad * unit, axis=0, keepdims=True)
        width = KV_RANK // count
        for number in range(count):
            latent_gain_buf[number] = gains[:, number * width:(number + 1) * width]
        grad = grad * latent_gain_ref[...]
        grad = scale * (grad - unit * jnp.mean(unit * grad, axis=1, keepdims=True))
        half = ROPE // 2
        former = total[:rows, KV_RANK:KV_RANK + half]
        latter = total[:rows, KV_RANK + half:KV_RANK + ROPE]
        cosine, sine = cosine_ref[...], sine_ref[...]
        latent_grad = jnp.concatenate(
            [grad, former * cosine + latter * sine, latter * cosine - former * sine], axis=1
        ).astype(jnp.bfloat16)
        latent_grad_ref[...] = latent_grad
        sums = total[:rows, KV_RANK + ROPE:KV_RANK + ROPE + 2]
        mean_ref[...] = (
            jnp.sum(sums, axis=1, keepdims=True)
            + jnp.sum(latent_grad.astype(jnp.float32) * latent, axis=1, keepdims=True)
        ) / (block * count)

    def by_pairs(grad):
        return grad.reshape(pairs, 2, grad.shape[0] // (2 * pairs), grad.shape[1])

    low = 0
    for rows_ref, grads in ((n_ref, latent_grad_ref), (t_ref, logit_ref)):
        grad = matmul_tn(rows_ref[...], grads[...])
        put_pairs(first, by_pairs(grad), 0, low, mine_ref, other_ref)
        low += grad.shape[1]
    unit = token_ref[...].astype(jnp.float32) * scale_ref[...]
    routed = matmul(latent_grad_ref[...], w_latent_ref[...])
    gain = gain_buf[step] + jnp.sum(routed * unit, axis=0, keepdims=True)
    line = lax.broadcasted_iota(jnp.int32, (LANES, block), 0)
    gains = by_pairs(jnp.where(line == 0, gain, jnp.where(line == 1, ffn_ref[...], 0.0)).T)
    width = latent_gain_buf.shape[2]
    kv_chunk = width // (2 * pairs)
    line = lax.broadcasted_iota(jnp.int32, (LANES, width), 0)
    more = by_pairs(jnp.where(line == 2, latent_gain_buf[step], 0.0).T)
    gains = jnp.concatenate([gains[:, :, :kv_chunk] + more, gains[:, :, kv_chunk:]], axis=2)
    put_pairs(first, gains, 0, low, mine_ref, other_ref)


def latent_weights(core, groups, normed, normed_two, tokens, w_latent, ffn_gain, logit, latent, latent_gain,
                   cosine, sine, scale, pieces):
    count = len(pieces)
    shapes = [
        jax.ShapeDtypeStruct(latent.shape, jnp.bfloat16),
        jax.ShapeDtypeStruct(scale.shape, jnp.float32),
    ]
    scratch = [
        pltpu.VMEM((count, 1, normed.shape[1] // count), jnp.float32),
        pltpu.VMEM((count, 1, KV_RANK // count), jnp.float32),
    ]
    return paired_call(
        latent_weights_kernel, core, groups, latent.shape[1] + logit.shape[1] + LANES,
        [normed, normed_two, tokens, w_latent.T, ffn_gain],
        [logit, latent, latent_gain.reshape(1, -1), cosine, sine, scale, *pieces], shapes, scratch,
        "latent_weights",
    )


def pair_kernel(mine_ref, got_ref, *rest):
    rest[-1][...] = (
        mine_ref[...].astype(jnp.float32) + got_ref[...].astype(jnp.float32)
    ).astype(jnp.bfloat16)


def pair_sum(mine, got, columns, place, whole=None):
    chips, rows, width = mine.shape
    steps = 4
    block = pl.BlockSpec((chips // steps, rows, width), lambda i: (i, 0, 0))
    before = () if whole is None else (whole,)
    return pl.pallas_call(
        pair_kernel,
        grid=(steps,),
        in_specs=[block, block] + [pl.BlockSpec(memory_space=pl.ANY)] * len(before),
        out_specs=pl.BlockSpec((chips // steps, rows, width), lambda i: (i, 0, place)),
        out_shape=jax.ShapeDtypeStruct((chips, rows, columns), jnp.bfloat16),
        input_output_aliases={2: 0} if before else {},
        compiler_params=pltpu.CompilerParams(vmem_limit_bytes=VMEM_BYTES),
        cost_estimate=pl.CostEstimate(flops=0, bytes_accessed=14_000_000, transcendentals=0),
        name="pair_sum",
    )(mine, got, *before)


def final_kernel(edges, part_ref, query_ref, output_ref, kv_ref, latent_ref, router_ref,
                 *rest):
    *gain_refs, total_ref = rest
    step = pl.program_id(0)

    @pl.when(step == 0)
    def _():
        total_ref[...] = jnp.zeros_like(total_ref)

    total = total_ref[...]
    for number in range(part_ref.shape[0]):
        total = total + part_ref[number].astype(jnp.float32)
    total_ref[...] = total

    @pl.when(step == pl.num_programs(0) - 1)
    def _():
        outs = (query_ref, output_ref, kv_ref, latent_ref, router_ref)
        for out, low, high in zip(outs, edges[:5], edges[1:6]):
            if out is not kv_ref:
                out[...] = total_ref[:, low:high]
                continue
            chunk = out.shape[0]
            for place in range(total_ref.shape[0] // chunk):
                out[:, place * (high - low):(place + 1) * (high - low)] = (
                    total_ref[place * chunk:(place + 1) * chunk, low:high]
                )
        gains = total_ref[:, edges[5]:].T
        for number, gain_ref in enumerate(gain_refs):
            gain_ref[...] = gains[number:number + 1, :]


def final_sums(parts, edges, shapes):
    chips, rows, columns = parts.shape
    step = 4
    return pl.pallas_call(
        functools.partial(final_kernel, edges),
        grid=(chips // step,),
        in_specs=[pl.BlockSpec((step, rows, columns), lambda i: (i, 0, 0))],
        out_specs=[pl.BlockSpec(a.shape, lambda i: (0, 0)) for a in shapes],
        out_shape=shapes,
        scratch_shapes=[pltpu.VMEM((rows, columns), jnp.float32)],
        compiler_params=pltpu.CompilerParams(vmem_limit_bytes=VMEM_BYTES),
        cost_estimate=pl.CostEstimate(flops=0, bytes_accessed=6_000_000, transcendentals=0),
        name="final_sums",
    )(parts)


def ordered_kernel(rank_ref, *refs):
    *pieces, out_ref = refs
    count = len(pieces)
    part = pieces[0].shape[1]
    for place in range(count):
        turn = lax.rem(rank_ref[0] - place + count, count)
        for number, piece in enumerate(pieces):
            @pl.when(turn == number)
            def _():
                out_ref[:, place * part:(place + 1) * part] = piece[...]


def ordered_columns(rank, pieces):
    rows, part = pieces[0].shape
    shape = jax.ShapeDtypeStruct((rows, part * len(pieces)), pieces[0].dtype)
    return pl.pallas_call(
        ordered_kernel,
        grid_spec=pltpu.PrefetchScalarGridSpec(
            num_scalar_prefetch=1, grid=(1,), in_specs=full_specs(pieces),
            out_specs=full_specs([shape])[0],
        ),
        out_shape=shape,
        compiler_params=pltpu.CompilerParams(vmem_limit_bytes=VMEM_BYTES),
        cost_estimate=pl.CostEstimate(flops=0, bytes_accessed=2_000_000, transcendentals=0),
        name="ordered_columns",
    )(rank.reshape(1), *pieces)


def swap_cores(rows, groups):
    return lax.ppermute(rows, "expert", [(index, index ^ 1) for index in range(groups)])


def shards(
    tokens,
    cotangent,
    attn_gain,
    w_query,
    w_latent,
    latent_gain,
    w_keyvalue,
    w_output,
    ffn_gain,
    w_router,
    shared_gate,
    shared_up,
    shared_down,
    expert_gate,
    expert_up,
    expert_down,
    routes,
):
    bf16 = jnp.bfloat16
    f32 = jnp.float32
    tok_rows, model_width = tokens.shape
    top_count = routes.shape[1]
    expert_count = w_router.shape[1]
    local_experts, _, hidden_width = expert_gate.shape
    groups = lax.axis_size("expert")
    ranks = lax.axis_size("tensor")
    rank = lax.axis_index("tensor")
    group = lax.axis_index("expert")
    part = model_width // ranks
    capacity = (4 * tok_rows * top_count + 3 * expert_count - 1) // (3 * expert_count)
    slot_count = expert_count * capacity
    per_group = local_experts * capacity
    qk_width = NOPE + ROPE
    local_heads = w_query.shape[1] // qk_width

    expert_ids = jnp.arange(expert_count, dtype=jnp.int32)
    selector = routes[:, :, None] == expert_ids[None, None, :]
    chosen_mask = jnp.sum(selector.astype(f32), axis=1)

    cotangent_part = column_block(cotangent, rank, part)
    chosen_low = jnp.pad(chosen_mask.astype(bf16), ((0, 0), (0, LANES - expert_count)))
    all_grads = lax.all_gather(
        jnp.concatenate([cotangent_part, chosen_low], axis=1), "expert", axis=0
    )

    tables = rotary_constants(tok_rows, local_heads)
    (normed, scale_one, query_pre, query_low, latent, latent_normed, keyvalue, key_rope, weights_full,
     attn_mixed, attended, *sends) = attention_forward(
        rank, tokens, attn_gain, latent_gain, tables, w_latent, w_query, w_keyvalue, w_output, ranks
    )

    token_ids = jnp.arange(tok_rows, dtype=jnp.int32)
    before = (token_ids[:, None] > token_ids[None, :]).astype(bf16)
    earlier = matmul(before, after(chosen_mask, attended).astype(bf16))
    place = jnp.sum(jnp.where(selector, earlier[:, None, :], 0.0), axis=-1).astype(jnp.int32)

    def one_hot(target, sideways):
        shape = (tok_rows, groups * capacity) if sideways else (slot_count, tok_rows)
        slot_ids = jnp.arange(shape[1] if sideways else shape[0], dtype=jnp.int32)
        found = jnp.zeros(shape, jnp.bool_)
        for choice in range(top_count):
            if sideways:
                found = found | (target[:, choice][:, None] == slot_ids[None, :])
            else:
                found = found | (slot_ids[:, None] == target[:, choice][None, :])
        return found.astype(bf16)

    dispatch = one_hot(routes * capacity + place, False)
    pick, next_pick = (
        one_hot(
            jnp.where(lax.rem(routes, local_experts) == number,
                      routes // local_experts * capacity + place, -1),
            True,
        )
        for number in range(local_experts)
    )

    sends = [shift_ranks(sent, step + 1, ranks) for step, sent in enumerate(sends)]
    hidden_part, sent = hidden_rows(attended, column_block(tokens, rank, part), sends)
    first = (group * local_experts).reshape(1)
    pieces = [sent] + [shift_ranks(sent, step, ranks) for step in range(1, ranks)]

    rows_sent, normed_two, logits, scale_two = route_rows(
        rank, dispatch, ffn_gain, w_router, pieces
    )
    unit_two_part = hidden_part * scale_two
    sigmas = jax.nn.sigmoid(logits) * chosen_mask
    sigma_total = jnp.sum(sigmas, axis=-1, keepdims=True)
    arrived = lax.all_to_all(
        rows_sent.reshape(groups, per_group, -1), "expert", split_axis=0, concat_axis=0, tiled=True
    )
    chosen_rows, *grad_quarters = owner_rows(
        first, after(all_grads, normed_two), local_experts, capacity
    )
    grads_arrived = [lax.all_gather(rows, "tensor", axis=0) for rows in grad_quarters]

    shared_gate_pre = matmul(normed_two, shared_gate)
    shared_up_pre = matmul(normed_two, shared_up)
    shared_act = (jax.nn.silu(shared_gate_pre) * shared_up_pre).astype(bf16)
    shared_part = matmul(shared_act, shared_down)
    grad_shared_act = matmul_nt(cotangent, shared_down)
    shared_gate_grad, shared_up_grad = silu_back(grad_shared_act, shared_gate_pre, shared_up_pre)
    norm_part = matmul_nt(shared_gate_grad, shared_gate) + matmul_nt(shared_up_grad, shared_up)
    shared_dot = jnp.sum(
        shared_gate_grad.astype(f32) * shared_gate_pre + shared_up_grad.astype(f32) * shared_up_pre,
        axis=-1, keepdims=True,
    )
    shared_grads = shared_weights(
        normed_two, cotangent, shared_gate_grad, shared_up_grad, shared_act, groups
    )

    width = -(-hidden_width // LANES) * LANES
    widen = ((0, 0), (0, width - hidden_width), (0, 0))
    gate_up = jnp.concatenate(
        [jnp.pad(expert_gate.transpose(0, 2, 1), widen), jnp.pad(expert_up.transpose(0, 2, 1), widen)],
        axis=1,
    )
    weights = (gate_up, jnp.pad(expert_down, widen))
    arrived = after(
        arrived, shared_grads, shared_part, norm_part, shared_dot, pick, next_pick, *weights
    ).reshape(groups, local_experts, capacity, -1)
    pre_grad, act_weighted, back, sums = expert_rows(
        0, first, arrived, chosen_rows, w_router, grads_arrived[0], weights
    )
    back = lax.psum_scatter(back, "tensor", scatter_dimension=0, tiled=True)[0]
    next_grad, next_weighted, direct, next_produced = expert_rows(
        1, first, arrived, chosen_rows, w_router, grads_arrived[1], weights, sums
    )
    direct = lax.all_to_all(direct, "expert", split_axis=0, concat_axis=0, tiled=True)
    weight_grads = expert_weights(
        1, arrived, grads_arrived[1], next_grad, next_weighted, hidden_width
    )
    weight_grads = expert_weights(
        0, arrived, grads_arrived[0], pre_grad, act_weighted, hidden_width, weight_grads
    )
    direct = after(direct, *weight_grads).reshape(groups * capacity, -1)
    grad_expert_gate, grad_expert_up, grad_expert_down = weight_grads
    back = lax.all_to_all(
        after(back, direct), "expert", split_axis=0, concat_axis=0, tiled=True
    ).reshape(groups * capacity, -1)

    router_rows = lax.dynamic_slice_in_dim(w_router, rank * part, part, axis=0)
    ffn_gain_part = lax.dynamic_slice_in_dim(ffn_gain, rank * part, part, axis=0)
    norm_grad, extra_low, *sends = combine_rows(
        rank, next_pick, pick, direct, after(norm_part, router_rows, ffn_gain_part), shared_dot, ranks
    )
    norm_pieces = [shift_ranks(sent, step + 1, ranks) for step, sent in enumerate(sends)]
    hidden_grad, sent, logit_grad = norm_back(
        norm_grad, extra_low, pick, back, chosen_mask, logits, scale_two, hidden_part,
        ffn_gain_part, router_rows, cotangent_part, norm_pieces,
    )
    pieces = [sent] + [shift_ranks(sent, step, ranks) for step in range(1, ranks)]

    (branch_low, grad_ffn_gain, query_pre_grad, keyvalue_grad, normed_grad, latent_sent,
     *sends) = attention_backward(
        rank, pieces, weights_full, keyvalue, key_rope, query_low, query_pre, tokens, scale_one, tables,
        w_output, w_keyvalue, w_query,
    )
    pieces = [latent_sent] + [shift_ranks(latent_sent, step, ranks) for step in range(1, ranks)]
    normed_pieces = [
        shift_ranks(after(sent, *pieces), step + 1, ranks) for step, sent in enumerate(sends)
    ]

    returned = lax.all_to_all(
        after(next_produced, back, *norm_pieces), "expert", split_axis=0, concat_axis=0, tiled=True
    ).reshape(groups * capacity, -1)
    latent_sent = after(latent_sent, returned)

    chunk = model_width // groups
    kv_chunk = KV_RANK // groups
    core = lax.rem(group, 2)
    mine, other = branch_weights(
        core, groups, normed, branch_low, latent_normed, query_pre_grad, attn_mixed, keyvalue_grad
    )
    late_columns = mine.shape[2] + w_latent.shape[1] + expert_count + LANES
    late = pair_sum(mine, swap_cores(other, groups), late_columns, 0)
    latent_grad, row_mean, mine, other = latent_weights(
        core, groups, normed, normed_two, tokens, w_latent, grad_ffn_gain, logit_grad, latent,
        latent_gain, tables[3], tables[4], scale_one, pieces,
    )
    shared_width = shared_gate.shape[1]
    early = lax.psum_scatter(
        after(shared_grads, direct).reshape(groups * 3 * chunk, shared_width), "expert",
        scatter_dimension=0, tiled=True,
    )
    branch, *sends = branch_rows(rank, next_pick, after(returned, mine), shared_part, ranks)
    late = pair_sum(
        mine, swap_cores(after(other, returned), groups), late_columns,
        2, late,
    )
    late = lax.all_to_all(
        late, "expert", split_axis=0, concat_axis=0, tiled=True,
        axis_index_groups=[list(range(first_core, groups, 2)) for first_core in range(2)],
    )

    latent_rows = lax.dynamic_slice_in_dim(w_latent, rank * part, part, axis=0)
    attn_gain_part = lax.dynamic_slice_in_dim(attn_gain, rank * part, part, axis=0)
    block = jax.ShapeDtypeStruct((tok_rows, part), bf16)
    grad_tokens = single_call(
        token_kernel,
        [normed_grad, latent_grad, latent_rows, row_mean, column_block(tokens, rank, part), scale_one,
         attn_gain_part.reshape(1, part), hidden_grad, *normed_pieces],
        [block], "token_rows",
    )[0]
    grad_tokens = ordered_columns(
        rank, [grad_tokens] + [shift_ranks(grad_tokens, step, ranks) for step in range(1, ranks)]
    )
    sends = [shift_ranks(sent, step + 1, ranks) for step, sent in enumerate(sends)]
    output = single_call(
        output_kernel, [branch, hidden_part, pick, back, *sends],
        [block], "output_rows",
    )[0]
    output = ordered_columns(
        rank, [output] + [shift_ranks(output, step, ranks) for step in range(1, ranks)]
    )

    early = after(early, output).astype(f32)
    grad_shared_gate = early[:chunk]
    grad_shared_up = early[chunk:2 * chunk]
    grad_shared_down = early[2 * chunk:].T

    edges = [0]
    for columns in (
        query_pre_grad.shape[1], attn_mixed.shape[1],
        keyvalue_grad.shape[1] * KV_RANK // model_width, latent_grad.shape[1], expert_count, LANES,
    ):
        edges.append(edges[-1] + columns)
    shapes = [
        jax.ShapeDtypeStruct((chunk, high - low), f32) for low, high in zip(edges[:-1], edges[1:])
    ]
    shapes[2] = jax.ShapeDtypeStruct((kv_chunk, keyvalue_grad.shape[1]), f32)
    shapes[5:] = [jax.ShapeDtypeStruct((1, chunk), f32)] * 3
    grad_query, grad_output, grad_keyvalue, grad_latent, grad_router, *gains = final_sums(
        after(late, grad_shared_gate, grad_shared_up, grad_shared_down), tuple(edges), shapes
    )
    return (
        output,
        grad_tokens,
        gains[0].reshape(chunk),
        grad_query,
        grad_latent,
        gains[2][0, :kv_chunk],
        grad_keyvalue,
        grad_output.T,
        gains[1].reshape(chunk),
        grad_router,
        grad_shared_gate,
        grad_shared_up,
        grad_shared_down,
        grad_expert_gate.transpose(0, 2, 1),
        grad_expert_up.transpose(0, 2, 1),
        grad_expert_down,
    )


def solution(mesh):
    return jax.shard_map(
        shards,
        mesh=mesh,
        in_specs=(
            P("expert", None),
            P("expert", None),
            P(),
            P(None, "tensor"),
            P(),
            P(),
            P(None, "tensor"),
            P("tensor", None),
            P(),
            P(),
            P(None, "tensor"),
            P(None, "tensor"),
            P("tensor", None),
            P("expert", None, "tensor"),
            P("expert", None, "tensor"),
            P("expert", "tensor", None),
            P("expert", None),
        ),
        out_specs=(
            P("expert", None),
            P("expert", None),
            P("expert"),
            P("expert", "tensor"),
            P("expert", None),
            P("expert"),
            P("expert", "tensor"),
            P("tensor", "expert"),
            P("expert"),
            P("expert", None),
            P("expert", "tensor"),
            P("expert", "tensor"),
            P("tensor", "expert"),
            P("expert", None, "tensor"),
            P("expert", None, "tensor"),
            P("expert", "tensor", None),
        ),
        check_vma=False,
    )
```

```python
import functools

import jax
import jax.numpy as jnp
import numpy as np
from jax import lax
from jax.experimental import pallas as pl
from jax.experimental.pallas import tpu as pltpu
from jax.sharding import PartitionSpec as P

NOPE = 128
ROPE = 64
VDIM = 128
KV_RANK = 512


EPS = 1e-06
THETA = 50000.0
ROUTE_SCALE = 2.446
MASKED = -1e30
LANES = 128
VMEM_BYTES = 60 * 1024 * 1024


def silu_back(grad_act, gate_pre, up_pre):
    sigma_gate = jax.nn.sigmoid(gate_pre)
    grad_up = grad_act * gate_pre * sigma_gate
    grad_gate = grad_act * up_pre * sigma_gate * (1.0 + gate_pre * (1.0 - sigma_gate))
    return (grad_gate.astype(jnp.bfloat16), grad_up.astype(jnp.bfloat16))


def matmul(left_side, right_side):
    return jnp.dot(left_side, right_side, preferred_element_type=jnp.float32)


def matmul_tn(left_side, right_side):
    return lax.dot_general(
        left_side, right_side, (((0,), (0,)), ((), ())), preferred_element_type=jnp.float32
    )


def matmul_nt(left_side, right_side):
    return lax.dot_general(
        left_side, right_side, (((1,), (1,)), ((), ())), preferred_element_type=jnp.float32
    )


def after(value, *others):
    return lax.optimization_barrier((value,) + others)[0]


def shift_ranks(values, step, count):
    return lax.ppermute(values, "tensor", [(i, (i + step) % count) for i in range(count)])


def column_block(values, index, width):
    return lax.dynamic_slice_in_dim(values, index * width, width, axis=1)


def expert_rows_kernel(sideways, first_ref, x_ref, mask_ref, router_ref, g_ref, wgu_ref, wd_ref, *rest):
    dgu_ref, actw_ref, rowgrad_ref, other_ref = rest[-4:]
    quarters, step, cap, part = g_ref.shape
    rows = step * cap
    width, model = wd_ref.shape
    half = LANES // 2
    expert = first_ref[0]
    experts = router_ref.shape[1]
    x_rows = x_ref[...].reshape(rows, model)
    mask = mask_ref[...].reshape(rows, LANES)[:, :experts].astype(jnp.float32)
    sigmas = mask / (1.0 + jnp.exp(-matmul(x_rows, router_ref[...])))
    total = jnp.sum(sigmas, axis=1, keepdims=True)
    column = lax.broadcasted_iota(jnp.int32, sigmas.shape, 1)
    own = jnp.sum(jnp.where(column == expert, sigmas, 0.0), axis=1, keepdims=True)
    weight = jnp.where(total > 0.0, ROUTE_SCALE * own / jnp.where(total > 0.0, total, 1.0), 0.0)
    column = lax.broadcasted_iota(jnp.int32, (rows, LANES), 1)

    pre = matmul_nt(x_rows, wgu_ref[...])
    grad_act = matmul_nt(g_ref[0].reshape(rows, part), wd_ref[:, :part])
    for place in range(1, quarters):
        grad_act += matmul_nt(
            g_ref[place].reshape(rows, part), wd_ref[:, place * part:(place + 1) * part]
        )
    gate_pre = pre[:, :width]
    up_pre = pre[:, width:]
    sigma = 1.0 / (1.0 + jnp.exp(-gate_pre))
    silu = gate_pre * sigma
    act = silu * up_pre
    act_weighted = (act * weight).astype(jnp.bfloat16)
    actw_ref[...] = act_weighted
    out = matmul(act_weighted, wd_ref[...]).astype(jnp.bfloat16)
    if sideways:
        for place in range(quarters):
            rowgrad_ref[place, :, :, part:] = (
                out[:, place * part:(place + 1) * part].reshape(step, cap, part)
            )
    else:
        other_ref[...] = out.reshape(step, cap, model)
    dot = jnp.sum(grad_act * act, axis=1, keepdims=True)
    grad_act = grad_act * weight
    grad_up = grad_act * silu
    grad_gate = grad_act * up_pre * (sigma + silu * (1.0 - sigma))
    row_dot = jnp.sum(grad_gate * gate_pre + grad_up * up_pre, axis=1, keepdims=True)
    row_dot_high = row_dot.astype(jnp.bfloat16).astype(jnp.float32)
    pre_grad = jnp.concatenate([grad_gate, grad_up], axis=1).astype(jnp.bfloat16)
    dgu_ref[...] = pre_grad
    row_grad = matmul(pre_grad, wgu_ref[...]).astype(jnp.bfloat16)
    mark = half if sideways else half + 2
    sums = jnp.where(column == expert, dot, 0.0)
    sums = jnp.where(column == mark, row_dot_high, sums)
    sums = jnp.where(column == mark + 1, row_dot - row_dot_high, sums)
    sums = sums.astype(jnp.bfloat16).reshape(step, cap, LANES)
    if sideways:
        for place in range(quarters):
            rowgrad_ref[place, :, :, :part] = (
                row_grad[:, place * part:(place + 1) * part].reshape(step, cap, part)
            )
        other_ref[...] = sums
    else:
        rowgrad_ref[:, :, :model] = row_grad.reshape(step, cap, model)
        rowgrad_ref[:, :, model:] = sums + rest[0][...]


def expert_rows(number, first, x, mask, router, g, weights, before=None):
    sources, experts, cap, model = x.shape
    quarters, _, _, part = g.shape
    gate_up, down = weights
    width = down.shape[1]
    step = 8
    rows = step * cap
    total = sources * cap
    sideways = before is None

    def flat_block(columns):
        return pl.BlockSpec((rows, columns), lambda b, f: (b, 0))

    def whole(*shape):
        return pl.BlockSpec((None,) + shape, lambda b, f: (number, 0, 0))

    def kind(*shape):
        return jax.ShapeDtypeStruct(shape, jnp.bfloat16)

    def part_block(columns):
        return pl.BlockSpec((quarters, step, cap, columns), lambda b, f: (0, b, 0, 0))

    def row_block(columns):
        return pl.BlockSpec((step, cap, columns), lambda b, f: (b, 0, 0))

    def expert_block(columns):
        return pl.BlockSpec((step, None, cap, columns), lambda b, f: (b, number, 0, 0))

    in_specs = [
        expert_block(model), expert_block(LANES), pl.BlockSpec(router.shape, lambda b, f: (0, 0)),
        part_block(part), whole(2 * width, model), whole(width, model),
    ]
    inputs = () if sideways else (before,)
    in_specs += [row_block(LANES)] * len(inputs)
    return pl.pallas_call(
        functools.partial(expert_rows_kernel, sideways),
        grid_spec=pltpu.PrefetchScalarGridSpec(
            num_scalar_prefetch=1,
            grid=(sources // step,),
            in_specs=in_specs,
            out_specs=[flat_block(2 * width), flat_block(width)] + (
                [part_block(2 * part), row_block(LANES)] if sideways
                else [row_block(model + LANES), row_block(model)]
            ),
        ),
        out_shape=[kind(total, 2 * width), kind(total, width)] + (
            [kind(quarters, sources, cap, 2 * part), kind(sources, cap, LANES)] if sideways
            else [kind(sources, cap, model + LANES), kind(sources, cap, model)]
        ),
        compiler_params=pltpu.CompilerParams(vmem_limit_bytes=VMEM_BYTES),
        cost_estimate=pl.CostEstimate(
            flops=2 * total * model * width * 6, bytes_accessed=30_000_000,
            transcendentals=total * width,
        ),
        name=f"expert_rows_{number}",
    )(first + number, x, mask, router, g, gate_up, down, *inputs)


def expert_weights_kernel(x_ref, g_ref, dgu_ref, actw_ref, *rest):
    gate_ref, up_ref, down_ref = rest[-3:]
    rows, width = actw_ref.shape
    hidden = gate_ref.shape[0]
    grad = matmul_tn(dgu_ref[...], x_ref[...].reshape(rows, x_ref.shape[-1]))
    gate_ref[...] = grad[:hidden, :]
    up_ref[...] = grad[width:width + hidden, :]
    g_rows = g_ref[...].reshape(rows, g_ref.shape[-1])
    down_ref[...] = matmul_tn(actw_ref[...], g_rows)[:hidden, :]


def expert_weights(number, x, g, dgu, actw, hidden, before=()):
    quarters = g.shape[0]
    sources, experts, cap, model = x.shape
    total, width = actw.shape
    steps = 8
    part = model // steps
    per = steps // quarters
    x_block = pl.BlockSpec((sources, None, cap, part), lambda b: (0, number, 0, b))
    in_specs = [
        x_block,
        pl.BlockSpec((None, sources, cap, part), lambda b: (b // per, 0, 0, b % per)),
        pl.BlockSpec((total, 2 * width), lambda b: (0, 0)),
        pl.BlockSpec((total, width), lambda b: (0, 0)),
    ] + [pl.BlockSpec(memory_space=pl.ANY)] * len(before)
    return pl.pallas_call(
        expert_weights_kernel,
        grid=(steps,),
        in_specs=in_specs,
        out_specs=[pl.BlockSpec((None, hidden, part), lambda b: (number, 0, b))] * 3,
        out_shape=[jax.ShapeDtypeStruct((experts, hidden, model), jnp.float32)] * 3,
        compiler_params=pltpu.CompilerParams(vmem_limit_bytes=VMEM_BYTES),
        cost_estimate=pl.CostEstimate(
            flops=2 * total * model * width * 3, bytes_accessed=22_000_000, transcendentals=0
        ),
        input_output_aliases={4 + place: place for place in range(len(before))},
        name=f"expert_weights_{number}",
    )(x, g, dgu, actw, *before)


def shared_weights_kernel(n_ref, c_ref, gate_ref, up_ref, act_ref, out_ref):
    chunk = out_ref.shape[1] // 3
    for place, (rows, grads) in enumerate(
        ((n_ref, gate_ref), (n_ref, up_ref), (c_ref, act_ref))
    ):
        grad = matmul_tn(rows[...], grads[...]).astype(jnp.bfloat16)
        for group in range(out_ref.shape[0]):
            out_ref[group, place * chunk:(place + 1) * chunk, :] = (
                grad[group * chunk:(group + 1) * chunk, :]
            )


def shared_weights(normed, cotangent, gate_grad, up_grad, act, groups):
    tokens, model = normed.shape
    width = gate_grad.shape[1]
    block = 256
    chunk = model // groups
    per = block // chunk
    rows = pl.BlockSpec((tokens, block), lambda i: (0, i))
    grads = pl.BlockSpec((tokens, width), lambda i: (0, 0))
    return pl.pallas_call(
        shared_weights_kernel,
        grid=(model // block,),
        in_specs=[rows, rows, grads, grads, grads],
        out_specs=pl.BlockSpec((per, 3 * chunk, width), lambda i: (i, 0, 0)),
        out_shape=jax.ShapeDtypeStruct((groups, 3 * chunk, width), jnp.bfloat16),
        compiler_params=pltpu.CompilerParams(vmem_limit_bytes=VMEM_BYTES),
        cost_estimate=pl.CostEstimate(
            flops=6 * tokens * model * width, bytes_accessed=14_000_000, transcendentals=0
        ),
        name="shared_weights",
    )(normed, cotangent, gate_grad, up_grad, act)


def combine_kernel(rank_ref, pick_ref, other_pick_ref, back_ref, sums_ref, shared_ref, dots_ref,
                   own_ref, extra_ref, *sends):
    step = pl.program_id(0)
    count = pl.num_programs(0)
    place = lax.rem(step - rank_ref[0] + count, count)
    part = own_ref.shape[1]
    value = matmul(pick_ref[...], back_ref[...]) + shared_ref[...]

    @pl.when(place == 0)
    def _():
        own_ref[...] = value

    for number, send in enumerate(sends):
        @pl.when(place == number + 1)
        def _():
            send[:, :part] = value.astype(jnp.bfloat16)

    @pl.when(step == count - 1)
    def _():
        mark = LANES // 2
        column = lax.broadcasted_iota(jnp.int32, (pick_ref.shape[0], LANES), 1)
        own = ((column < mark) & (lax.rem(column, 2) == 1)) | (column >= mark + 2)
        sums = jnp.where(
            own, matmul(pick_ref[...], sums_ref[...]), matmul(other_pick_ref[...], sums_ref[...])
        )
        mean = dots_ref[...] + jnp.sum(
            jnp.where((column >= mark) & (column < mark + 4), sums, 0.0), axis=1, keepdims=True
        )
        mean_high = mean.astype(jnp.bfloat16).astype(jnp.float32)
        extra = jnp.where(column < mark, sums, 0.0)
        extra = jnp.where(column == mark, mean_high, extra)
        extra = jnp.where(column == mark + 1, mean - mean_high, extra).astype(jnp.bfloat16)
        extra_ref[...] = extra
        for send in sends:
            send[:, part:] = extra


def combine_rows(rank, pick, other_pick, back, shared, dots, count):
    tokens, slots = pick.shape
    model = shared.shape[1]
    part = model // count
    sent = jax.ShapeDtypeStruct((tokens, part + LANES), jnp.bfloat16)
    sent_block = pl.BlockSpec((tokens, part + LANES), lambda i, r: (0, 0))
    return pl.pallas_call(
        combine_kernel,
        grid_spec=pltpu.PrefetchScalarGridSpec(
            num_scalar_prefetch=1,
            grid=(count,),
            in_specs=[
                pl.BlockSpec((tokens, slots), lambda i, r: (0, 0)),
                pl.BlockSpec((tokens, slots), lambda i, r: (0, 0)),
                pl.BlockSpec((slots, part), lambda i, r: (0, i)),
                pl.BlockSpec((slots, LANES), lambda i, r: (0, model // LANES)),
                pl.BlockSpec((tokens, part), lambda i, r: (0, i)),
                pl.BlockSpec((tokens, 1), lambda i, r: (0, 0)),
            ],
            out_specs=[
                pl.BlockSpec((tokens, part), lambda i, r: (0, 0)),
                pl.BlockSpec((tokens, LANES), lambda i, r: (0, 0)),
            ] + [sent_block] * (count - 1),
        ),
        out_shape=[
            jax.ShapeDtypeStruct((tokens, part), jnp.float32),
            jax.ShapeDtypeStruct((tokens, LANES), jnp.bfloat16),
        ] + [sent] * (count - 1),
        compiler_params=pltpu.CompilerParams(vmem_limit_bytes=VMEM_BYTES),
        cost_estimate=pl.CostEstimate(
            flops=2 * tokens * slots * model, bytes_accessed=9_000_000, transcendentals=0
        ),
        name="combine_rows",
    )(rank.reshape(1), pick, other_pick, back, back, shared, dots)


def branch_kernel(rank_ref, pick_ref, back_ref, shared_ref, own_ref, *sends):
    step = pl.program_id(0)
    count = pl.num_programs(0)
    place = lax.rem(step - rank_ref[0] + count, count)
    value = matmul(pick_ref[...], back_ref[...]) + shared_ref[...]

    @pl.when(place == 0)
    def _():
        own_ref[...] = value

    for number, send in enumerate(sends):
        @pl.when(place == number + 1)
        def _():
            send[...] = value.astype(jnp.bfloat16)


def branch_rows(rank, pick, back, shared, count):
    tokens, slots = pick.shape
    model = shared.shape[1]
    part = model // count
    fixed = pl.BlockSpec((tokens, part), lambda i, r: (0, 0))
    return pl.pallas_call(
        branch_kernel,
        grid_spec=pltpu.PrefetchScalarGridSpec(
            num_scalar_prefetch=1,
            grid=(count,),
            in_specs=[
                pl.BlockSpec((tokens, slots), lambda i, r: (0, 0)),
                pl.BlockSpec((slots, part), lambda i, r: (0, i)),
                pl.BlockSpec((tokens, part), lambda i, r: (0, i)),
            ],
            out_specs=[fixed] * count,
        ),
        out_shape=[jax.ShapeDtypeStruct((tokens, part), jnp.float32)]
        + [jax.ShapeDtypeStruct((tokens, part), jnp.bfloat16)] * (count - 1),
        compiler_params=pltpu.CompilerParams(vmem_limit_bytes=VMEM_BYTES),
        cost_estimate=pl.CostEstimate(flops=0, bytes_accessed=4_000_000, transcendentals=0),
        name="branch_rows",
    )(rank.reshape(1), pick, back, shared)


def token_kernel(own_ref, latent_grad_ref, w_latent_ref, mean_ref, token_ref, scale_ref, gain_ref, hidden_ref,
                 *rest):
    *pieces, out_ref = rest
    grad = own_ref[...] + matmul_nt(latent_grad_ref[...], w_latent_ref[...])
    for piece in pieces:
        grad = grad + piece[...].astype(jnp.float32)
    scale = scale_ref[...]
    unit = token_ref[...].astype(jnp.float32) * scale
    grad = hidden_ref[...] + scale * (grad * gain_ref[...] - unit * mean_ref[...])
    out_ref[...] = grad.astype(jnp.bfloat16)


def output_kernel(own_ref, hidden_ref, pick_ref, back_ref, *rest):
    *pieces, out_ref = rest
    low = back_ref.shape[1] - out_ref.shape[1]
    value = hidden_ref[...] + own_ref[...] + matmul(pick_ref[...], back_ref[:, low:])
    for piece in pieces:
        value = value + piece[...].astype(jnp.float32)
    out_ref[...] = value.astype(jnp.bfloat16)


def attention_forward_kernel(rank_ref, token_ref, gain_ref, latent_gain_ref, cosine_ref, ahead_ref,
                             behind_ref, key_cosine_ref, key_sine_ref, w_latent_ref, w_query_ref,
                             w_keyvalue_ref, w_output_ref,
                             normed_ref, scale_ref, query_ref, query_low_ref, latent_ref,
                             latent_normed_ref, keyvalue_ref, key_rope_ref, weights_ref, mixed_ref,
                             own_ref, *rest):
    *sends, latent_buf, query_buf, keyvalue_buf, output_buf, sems = rest
    copies = [
        pltpu.make_async_copy(source, buffer, sems.at[number])
        for number, (source, buffer) in enumerate((
            (w_latent_ref, latent_buf), (w_query_ref, query_buf), (w_keyvalue_ref, keyvalue_buf),
            (w_output_ref, output_buf),
        ))
    ]
    for copy in copies:
        copy.start()
    tokens = token_ref[...].astype(jnp.float32)
    scale = lax.rsqrt(jnp.mean(tokens * tokens, axis=1, keepdims=True) + EPS)
    scale_ref[...] = scale
    normed = (tokens * scale * gain_ref[...]).astype(jnp.bfloat16)
    normed_ref[...] = normed
    copies[0].wait()
    latent = matmul_nt(normed, latent_buf[...])
    latent_ref[...] = latent
    compressed = latent[:, :KV_RANK]
    latent_scale = lax.rsqrt(jnp.mean(compressed * compressed, axis=1, keepdims=True) + EPS)
    latent_normed = (compressed * latent_scale * latent_gain_ref[...]).astype(jnp.bfloat16)
    latent_normed_ref[...] = latent_normed
    half = ROPE // 2
    former = latent[:, KV_RANK:KV_RANK + half]
    latter = latent[:, KV_RANK + half:]
    key_cosine, key_sine = key_cosine_ref[...], key_sine_ref[...]
    key_rope = jnp.concatenate(
        [former * key_cosine - latter * key_sine, latter * key_cosine + former * key_sine], axis=1
    ).astype(jnp.bfloat16)
    key_rope_ref[...] = key_rope
    copies[1].wait()
    query = matmul(normed, query_buf[...])
    query_ref[...] = query
    wide = query.shape[1]
    query_low_ref[...] = (
        query * cosine_ref[...] + pltpu.roll(query, wide - half, 1) * ahead_ref[...]
        + pltpu.roll(query, half, 1) * behind_ref[...]
    ).astype(jnp.bfloat16)
    copies[2].wait()
    keyvalue_ref[...] = matmul(latent_normed, keyvalue_buf[...]).astype(jnp.bfloat16)
    rows = tokens.shape[0]
    causal = (
        lax.broadcasted_iota(jnp.int32, (rows, rows), 0)
        >= lax.broadcasted_iota(jnp.int32, (rows, rows), 1)
    )
    qk_width = NOPE + ROPE
    for head in range(wide // qk_width):
        low = head * (NOPE + VDIM)
        query_head = query_low_ref[:, head * qk_width:(head + 1) * qk_width]
        key_head = jnp.concatenate([keyvalue_ref[:, low:low + NOPE], key_rope], axis=1)
        scores = matmul_nt(query_head, key_head) * (qk_width ** -0.5)
        scores = jnp.where(causal, scores, MASKED)
        terms = jnp.exp(scores - jnp.max(scores, axis=1, keepdims=True))
        weights = terms / jnp.sum(terms, axis=1, keepdims=True)
        weights_ref[head] = weights
        mixed_ref[:, head * VDIM:(head + 1) * VDIM] = matmul(
            weights.astype(jnp.bfloat16), keyvalue_ref[:, low + NOPE:low + NOPE + VDIM]
        ).astype(jnp.bfloat16)
    copies[3].wait()
    part = own_ref.shape[1]
    count = len(sends) + 1
    for number in range(count):
        value = matmul(mixed_ref[...], output_buf[:, number * part:(number + 1) * part])
        place = lax.rem(number - rank_ref[0] + count, count)

        @pl.when(place == 0)
        def _():
            own_ref[...] = value

        for index, send in enumerate(sends):
            @pl.when(place == index + 1)
            def _():
                send[...] = value.astype(jnp.bfloat16)


def rotary_constants(rows, heads):
    half = ROPE // 2
    frequency = np.float32(THETA) ** (np.arange(half, dtype=np.float32) * np.float32(-2.0 / ROPE))
    angles = np.arange(rows, dtype=np.float32)[:, None] * frequency[None, :]
    cosine, sine = np.cos(angles), np.sin(angles)
    blank = np.zeros((rows, NOPE), np.float32)
    zero = np.zeros((rows, half), np.float32)

    def tiled(*pieces):
        return np.tile(np.concatenate(pieces, axis=1), (1, heads)).astype(np.float32)

    return (
        tiled(blank + 1.0, cosine, cosine), tiled(blank, -sine, zero), tiled(blank, zero, sine),
        cosine, sine,
    )


def full_specs(arrays):
    return [pl.BlockSpec(a.shape, lambda i, r, n=len(a.shape): (0,) * n) for a in arrays]


def attention_forward(rank, tokens, gain, latent_gain, tables, w_latent, w_query, w_keyvalue, w_output,
                      count):
    rows, model = tokens.shape
    part = model // count
    latent_width = w_latent.shape[1]
    query_width = w_query.shape[1]
    heads = query_width // (NOPE + ROPE)
    bf16, f32 = jnp.bfloat16, jnp.float32
    out_shape = [
        jax.ShapeDtypeStruct(shape, kind)
        for shape, kind in (
            ((rows, model), bf16), ((rows, 1), f32), ((rows, query_width), f32),
            ((rows, query_width), bf16), ((rows, latent_width), f32), ((rows, KV_RANK), bf16),
            ((rows, w_keyvalue.shape[1]), bf16), ((rows, ROPE), bf16), ((heads, rows, rows), f32),
            ((rows, heads * VDIM), bf16), ((rows, part), f32),
        ) + (((rows, part), bf16),) * (count - 1)
    ]
    inputs = [tokens, gain.reshape(1, -1), latent_gain.reshape(1, -1), *tables]
    streamed = [w_latent.T, w_query, w_keyvalue, w_output]
    return pl.pallas_call(
        attention_forward_kernel,
        grid_spec=pltpu.PrefetchScalarGridSpec(
            num_scalar_prefetch=1,
            grid=(1,),
            in_specs=full_specs(inputs) + [pl.BlockSpec(memory_space=pl.ANY)] * len(streamed),
            out_specs=full_specs(out_shape),
            scratch_shapes=[pltpu.VMEM(a.shape, a.dtype) for a in streamed]
            + [pltpu.SemaphoreType.DMA((len(streamed),))],
        ),
        out_shape=out_shape,
        compiler_params=pltpu.CompilerParams(vmem_limit_bytes=VMEM_BYTES),
        cost_estimate=pl.CostEstimate(
            flops=5_000_000_000, bytes_accessed=16_000_000, transcendentals=300_000
        ),
        name="attention_forward",
    )(rank.reshape(1), *inputs, *streamed)


def attention_backward_kernel(rank_ref, *refs):
    count = 4
    pieces, refs = refs[:count], refs[count:]
    (weights_ref, keyvalue_ref, key_rope_ref, query_low_ref, query_ref, token_ref, scale_ref, cosine_ref,
     ahead_ref, behind_ref, w_output_ref, w_keyvalue_ref, w_query_ref,
     branch_ref, gain_ref, query_grad_ref, keyvalue_grad_ref, own_ref, latent_ref, *rest) = refs
    *sends, output_buf, keyvalue_buf, query_buf, grad_buf, sems = rest
    copies = [
        pltpu.make_async_copy(source, buffer, sems.at[number])
        for number, (source, buffer) in enumerate((
            (w_output_ref, output_buf), (w_keyvalue_ref, keyvalue_buf), (w_query_ref, query_buf),
        ))
    ]
    for copy in copies:
        copy.start()
    rows, model = branch_ref.shape
    part = own_ref.shape[1]
    for place in range(count):
        columns = slice(place * part, (place + 1) * part)
        turn = lax.rem(rank_ref[0] - place + count, count)
        for number, piece in enumerate(pieces):
            @pl.when(turn == number)
            def _():
                branch_ref[:, columns] = piece[:rows, :]
                sums = piece[rows:, :].astype(jnp.float32)
                gain_ref[:, columns] = sums[0:1] + sums[1:2]
    copies[0].wait()
    mixed_grad = matmul_nt(branch_ref[...], output_buf[...]).astype(jnp.bfloat16)
    qk_width = NOPE + ROPE
    soft = qk_width ** -0.5
    key_rope = key_rope_ref[...]
    rope_grad = jnp.zeros((rows, ROPE), jnp.float32)
    for head in range(weights_ref.shape[0]):
        low = head * (NOPE + VDIM)
        columns = slice(head * qk_width, (head + 1) * qk_width)
        weights = weights_ref[head]
        out_grad = mixed_grad[:, head * VDIM:(head + 1) * VDIM]
        keyvalue_grad_ref[:, low + NOPE:low + NOPE + VDIM] = matmul_tn(
            weights.astype(jnp.bfloat16), out_grad
        ).astype(jnp.bfloat16)
        prob_grad = matmul_nt(out_grad, keyvalue_ref[:, low + NOPE:low + NOPE + VDIM])
        row_term = jnp.sum(weights * prob_grad, axis=1, keepdims=True)
        score_grad = (weights * (prob_grad - row_term)).astype(jnp.bfloat16)
        key_head = jnp.concatenate([keyvalue_ref[:, low:low + NOPE], key_rope], axis=1)
        grad_buf[:, columns] = matmul(score_grad, key_head) * soft
        key_grad = matmul_tn(score_grad, query_low_ref[:, columns]) * soft
        keyvalue_grad_ref[:, low:low + NOPE] = key_grad[:, :NOPE].astype(jnp.bfloat16)
        rope_grad += key_grad[:, NOPE:]
    grad = grad_buf[...]
    wide = grad.shape[1]
    half = ROPE // 2
    query_grad = (
        grad * cosine_ref[...] - pltpu.roll(grad, wide - half, 1) * ahead_ref[...]
        - pltpu.roll(grad, half, 1) * behind_ref[...]
    ).astype(jnp.bfloat16)
    query_grad_ref[...] = query_grad
    mean = jnp.sum(query_grad.astype(jnp.float32) * query_ref[...], axis=1, keepdims=True)
    mean_high = mean.astype(jnp.bfloat16).astype(jnp.float32)
    copies[1].wait()
    latent_part = matmul_nt(keyvalue_grad_ref[...], keyvalue_buf[...])
    width = latent_part.shape[1]
    column = lax.broadcasted_iota(jnp.int32, (rows, LANES - ROPE), 1)
    sums = jnp.where(column == 0, mean_high, jnp.where(column == 1, mean - mean_high, 0.0))
    latent_ref[:rows, :width] = latent_part.astype(jnp.bfloat16)
    latent_ref[:rows, width:] = jnp.concatenate([rope_grad, sums], axis=1).astype(jnp.bfloat16)
    copies[2].wait()
    gains = []
    scale = scale_ref[...]
    for number in range(count):
        columns = slice(number * part, (number + 1) * part)
        value = matmul_nt(query_grad, query_buf[columns, :])
        unit = token_ref[:, columns].astype(jnp.float32) * scale
        gains.append(jnp.sum(value * unit, axis=0, keepdims=True))
        place = lax.rem(number - rank_ref[0] + count, count)

        @pl.when(place == 0)
        def _():
            own_ref[...] = value

        for index, send in enumerate(sends):
            @pl.when(place == index + 1)
            def _():
                send[...] = value.astype(jnp.bfloat16)
    highs = [gain.astype(jnp.bfloat16).astype(jnp.float32) for gain in gains]
    lows = [gain - high for gain, high in zip(gains, highs)]
    spare = latent_ref.shape[0] - rows
    latent_ref[rows:, :width] = jnp.concatenate(
        highs + lows + [jnp.zeros((spare - 2 * count, part), jnp.float32)], axis=0
    ).astype(jnp.bfloat16)
    latent_ref[rows:, width:] = jnp.zeros((spare, LANES), jnp.bfloat16)


def attention_backward(rank, pieces, weights, keyvalue, key_rope, query_low, query, tokens, scale, tables,
                       w_output, w_keyvalue, w_query):
    rows, model = tokens.shape
    count = len(pieces)
    part = model // count
    wide = query.shape[1]
    kv_width = keyvalue.shape[1]
    sent_rows = pieces[0].shape[0]
    bf16, f32 = jnp.bfloat16, jnp.float32
    sent_width = KV_RANK + LANES
    out_shape = [
        jax.ShapeDtypeStruct(shape, kind)
        for shape, kind in (
            ((rows, model), bf16), ((1, model), f32), ((rows, wide), bf16), ((rows, kv_width), bf16),
            ((rows, part), f32), ((sent_rows, sent_width), bf16),
        ) + (((rows, part), bf16),) * (count - 1)
    ]
    inputs = [*pieces, weights, keyvalue, key_rope, query_low, query, tokens, scale, *tables[:3]]
    streamed = [w_output, w_keyvalue, w_query]
    return pl.pallas_call(
        attention_backward_kernel,
        grid_spec=pltpu.PrefetchScalarGridSpec(
            num_scalar_prefetch=1,
            grid=(1,),
            in_specs=full_specs(inputs) + [pl.BlockSpec(memory_space=pl.ANY)] * len(streamed),
            out_specs=full_specs(out_shape),
            scratch_shapes=[pltpu.VMEM(a.shape, a.dtype) for a in streamed]
            + [pltpu.VMEM((rows, wide), f32), pltpu.SemaphoreType.DMA((len(streamed),))],
        ),
        out_shape=out_shape,
        compiler_params=pltpu.CompilerParams(vmem_limit_bytes=VMEM_BYTES),
        cost_estimate=pl.CostEstimate(
            flops=4_000_000_000, bytes_accessed=20_000_000, transcendentals=0
        ),
        name="attention_backward",
    )(rank.reshape(1), *inputs, *streamed)


def single_call(kernel, arrays, shapes, name):
    def specs(values):
        return [pl.BlockSpec(a.shape, lambda i, n=len(a.shape): (0,) * n) for a in values]

    return pl.pallas_call(
        kernel,
        grid=(1,),
        in_specs=specs(arrays),
        out_specs=specs(shapes),
        out_shape=shapes,
        compiler_params=pltpu.CompilerParams(vmem_limit_bytes=VMEM_BYTES),
        cost_estimate=pl.CostEstimate(flops=0, bytes_accessed=4_000_000, transcendentals=0),
        name=name,
    )(*arrays)


def hidden_kernel(own_ref, token_ref, *rest):
    *pieces, hidden_ref, sent_ref = rest
    value = own_ref[...] + token_ref[...].astype(jnp.float32)
    for piece in pieces:
        value = value + piece[...].astype(jnp.float32)
    hidden_ref[...] = value
    part = value.shape[1]
    total = jnp.sum(value * value, axis=1, keepdims=True)
    high = total.astype(jnp.bfloat16).astype(jnp.float32)
    column = lax.broadcasted_iota(jnp.int32, (value.shape[0], LANES), 1)
    sums = jnp.where(column == 0, high, jnp.where(column == 1, total - high, 0.0))
    sent_ref[:, :part] = value.astype(jnp.bfloat16)
    sent_ref[:, part:] = sums.astype(jnp.bfloat16)


def hidden_rows(own, token_block, pieces):
    tokens, part = own.shape
    shapes = [
        jax.ShapeDtypeStruct((tokens, part), jnp.float32),
        jax.ShapeDtypeStruct((tokens, part + LANES), jnp.bfloat16),
    ]
    return single_call(hidden_kernel, [own, token_block, *pieces], shapes, "hidden_rows")


def owner_rows_kernel(first_ref, block_ref, mask_ref, *out_refs):
    sources, rows, _ = block_ref.shape
    _, cap, part = out_refs[0].shape
    experts = len(out_refs)
    line = lax.broadcasted_iota(jnp.int32, (8, LANES), 0)
    column = lax.broadcasted_iota(jnp.int32, (8, LANES), 1)
    select = ((column == line + first_ref[0]) & (line < experts)).astype(jnp.bfloat16)
    earlier = (
        lax.broadcasted_iota(jnp.int32, (rows, rows), 0)
        < lax.broadcasted_iota(jnp.int32, (rows, rows), 1)
    ).astype(jnp.bfloat16)
    slot = lax.broadcasted_iota(jnp.int32, (cap, rows), 0).astype(jnp.float32)
    chosen = jnp.concatenate(
        [matmul_nt(select, block_ref[source, :, part:]) for source in range(sources)], axis=0
    )
    place = matmul(chosen.astype(jnp.bfloat16), earlier)
    for source in range(sources):
        picks = [
            jnp.where((slot == place[line:line + 1]) & (chosen[line:line + 1] > 0.5), 1.0, 0.0)
            for line in range(8 * source, 8 * source + experts)
        ]
        picks = jnp.concatenate(picks, axis=0).astype(jnp.bfloat16)
        out = matmul(picks, block_ref[source]).astype(jnp.bfloat16)
        mask_ref[source] = out[:, part:].reshape(experts, cap, LANES)
        for number, out_ref in enumerate(out_refs):
            out_ref[source] = out[number * cap:(number + 1) * cap, :part]


def owner_rows(first, gathered, experts, cap):
    groups, rows, wide = gathered.shape
    part = wide - LANES
    step = 16
    return pl.pallas_call(
        owner_rows_kernel,
        grid_spec=pltpu.PrefetchScalarGridSpec(
            num_scalar_prefetch=1,
            grid=(groups // step,),
            in_specs=[pl.BlockSpec((step, rows, wide), lambda i, f: (i, 0, 0))],
            out_specs=[pl.BlockSpec((step, experts, cap, LANES), lambda i, f: (i, 0, 0, 0))]
            + [pl.BlockSpec((step, cap, part), lambda i, f: (i, 0, 0))] * experts,
        ),
        out_shape=[jax.ShapeDtypeStruct((groups, experts, cap, LANES), jnp.bfloat16)]
        + [jax.ShapeDtypeStruct((groups, cap, part), jnp.bfloat16)] * experts,
        compiler_params=pltpu.CompilerParams(vmem_limit_bytes=VMEM_BYTES),
        cost_estimate=pl.CostEstimate(
            flops=2 * groups * experts * cap * rows * part, bytes_accessed=13_000_000,
            transcendentals=0,
        ),
        name="owner_rows",
    )(first, gathered)


def route_rows_kernel(rank_ref, dispatch_ref, gain_ref, router_ref, *rest):
    pieces, (rows_ref, wide_ref, logit_ref, scale_ref) = rest[:-4], rest[-4:]
    count = len(pieces)
    part = pieces[0].shape[1] - LANES
    model = count * part

    @pl.when(pl.program_id(0) == 0)
    def _():
        total = sum(jnp.sum(piece[:, part:].astype(jnp.float32), axis=1, keepdims=True)
                    for piece in pieces)
        scale = lax.rsqrt(total / model + EPS)
        scale_ref[...] = scale
        logits = jnp.zeros(logit_ref.shape, jnp.float32)
        for place in range(count):
            turn = lax.rem(rank_ref[0] - place + count, count)
            block = pieces[0][:, :part].astype(jnp.float32)
            for number in range(1, count):
                block = jnp.where(turn == number, pieces[number][:, :part].astype(jnp.float32),
                                  block)
            columns = slice(place * part, (place + 1) * part)
            block = (block * scale * gain_ref[:, columns]).astype(jnp.bfloat16)
            wide_ref[:, columns] = block
            logits += matmul(block, router_ref[columns, :])
        logit_ref[...] = logits

    rows_ref[...] = matmul(dispatch_ref[...], wide_ref[...]).astype(jnp.bfloat16)


def route_rows(rank, dispatch, gain, router, pieces):
    slots, tokens = dispatch.shape
    model, experts = router.shape
    block = 512

    def whole(*shape):
        return pl.BlockSpec(shape, lambda i, r: (0, 0))

    return pl.pallas_call(
        route_rows_kernel,
        grid_spec=pltpu.PrefetchScalarGridSpec(
            num_scalar_prefetch=1,
            grid=(slots // block,),
            in_specs=[
                pl.BlockSpec((block, tokens), lambda i, r: (i, 0)),
                whole(1, model), whole(model, experts),
            ] + [whole(*piece.shape) for piece in pieces],
            out_specs=[
                pl.BlockSpec((block, model), lambda i, r: (i, 0)),
                whole(tokens, model), whole(tokens, experts), whole(tokens, 1),
            ],
        ),
        out_shape=[
            jax.ShapeDtypeStruct((slots, model), jnp.bfloat16),
            jax.ShapeDtypeStruct((tokens, model), jnp.bfloat16),
            jax.ShapeDtypeStruct((tokens, experts), jnp.float32),
            jax.ShapeDtypeStruct((tokens, 1), jnp.float32),
        ],
        compiler_params=pltpu.CompilerParams(vmem_limit_bytes=VMEM_BYTES),
        cost_estimate=pl.CostEstimate(
            flops=2 * slots * tokens * model, bytes_accessed=13_000_000, transcendentals=0
        ),
        name="route_rows",
    )(rank.reshape(1), dispatch, gain.reshape(1, model), router, *pieces)


def norm_back_kernel(own_ref, extra_ref, pick_ref, back_ref, mask_ref, logit_ref, scale_ref, hidden_ref,
                     gain_ref, router_ref, cotangent_ref, *rest):
    *pieces, grad_ref, sent_ref, logit_grad_ref = rest
    part = own_ref.shape[1]
    rows, experts = mask_ref.shape
    model = part * (len(pieces) + 1)
    norm_grad = own_ref[...] + matmul(pick_ref[...], back_ref[:, :part])
    extra = extra_ref[...].astype(jnp.float32)
    for piece in pieces:
        norm_grad = norm_grad + piece[:, :part].astype(jnp.float32)
        extra = extra + piece[:, part:].astype(jnp.float32)
    logits = logit_ref[...]
    sigmas = mask_ref[...] / (1.0 + jnp.exp(-logits))
    total = jnp.sum(sigmas, axis=1, keepdims=True)
    gate_grad = extra[:, :experts]
    weighted_sum = jnp.sum(gate_grad * sigmas, axis=1, keepdims=True)
    sigma_grad = ROUTE_SCALE * (gate_grad / total - weighted_sum / (total * total))
    logit_grad = (sigma_grad * sigmas * (1.0 - sigmas)).astype(jnp.bfloat16)
    logit_grad_ref[...] = logit_grad
    norm_grad = norm_grad + matmul_nt(logit_grad, router_ref[...])
    mean = (
        jnp.sum(extra[:, experts:experts + 2], axis=1, keepdims=True)
        + jnp.sum(logit_grad.astype(jnp.float32) * logits, axis=1, keepdims=True)
    ) / model
    scale = scale_ref[...]
    unit = hidden_ref[...] * scale
    gain_grad = jnp.sum(norm_grad * unit, axis=0, keepdims=True)
    grad = cotangent_ref[...].astype(jnp.float32) + scale * (norm_grad * gain_ref[...] - unit * mean)
    grad_ref[...] = grad
    sent_ref[:rows, :] = grad.astype(jnp.bfloat16)
    high = gain_grad.astype(jnp.bfloat16).astype(jnp.float32)
    row = lax.broadcasted_iota(jnp.int32, (sent_ref.shape[0] - rows, part), 0)
    sums = jnp.where(row == 0, high, jnp.where(row == 1, gain_grad - high, 0.0))
    sent_ref[rows:, :] = sums.astype(jnp.bfloat16)


def norm_back(own, extra, pick, back, mask, logits, scale, hidden, gain, router, cotangent, pieces):
    rows, part = own.shape
    bf16, f32 = jnp.bfloat16, jnp.float32
    shapes = [
        jax.ShapeDtypeStruct((rows, part), f32), jax.ShapeDtypeStruct((rows + 16, part), bf16),
        jax.ShapeDtypeStruct(mask.shape, bf16),
    ]
    inputs = [own, extra, pick, back, mask, logits, scale, hidden, gain.reshape(1, part), router, cotangent]
    return single_call(norm_back_kernel, inputs + list(pieces), shapes, "norm_back")


def put_pairs(first, grad, row, column, mine_ref, other_ref):
    rows = slice(row, row + grad.shape[2])
    columns = slice(column, column + grad.shape[3])
    even, odd = grad[:, 0], grad[:, 1]
    mine_ref[:, rows, columns] = jnp.where(first, even, odd).astype(jnp.bfloat16)
    other_ref[:, rows, columns] = jnp.where(first, odd, even).astype(jnp.bfloat16)


def branch_weights_kernel(core_ref, n_ref, b_ref, l_ref, query_ref, mixed_ref, kv_ref, mine_ref, other_ref):
    pairs, chunk, _ = mine_ref.shape
    first = core_ref[0] == 0

    def by_pairs(grad):
        return grad.reshape(pairs, 2, grad.shape[0] // (2 * pairs), grad.shape[1])

    low = 0
    for rows_ref, grads in ((n_ref, query_ref), (b_ref, mixed_ref)):
        grad = matmul_tn(rows_ref[...], grads[...])
        put_pairs(first, by_pairs(grad), 0, low, mine_ref, other_ref)
        low += grad.shape[1]
    grad = by_pairs(matmul_tn(l_ref[...], kv_ref[...]))
    kv_chunk = grad.shape[2]
    columns = grad.shape[3] * kv_chunk // chunk
    for place in range(chunk // kv_chunk):
        put_pairs(first, grad[:, :, :, place * columns:(place + 1) * columns], place * kv_chunk, low,
                  mine_ref, other_ref)


def paired_call(kernel, core, groups, columns, blocked, whole, extra_shapes, scratch, name):
    steps = 4
    model = blocked[0].shape[1]
    chunk = model // groups
    out = pl.BlockSpec((groups // 2 // steps, chunk, columns), lambda i, c: (i, 0, 0))

    def fixed(array):
        return pl.BlockSpec(array.shape, lambda i, c: (0, 0))

    return pl.pallas_call(
        kernel,
        grid_spec=pltpu.PrefetchScalarGridSpec(
            num_scalar_prefetch=1,
            grid=(steps,),
            in_specs=[
                pl.BlockSpec((a.shape[0], a.shape[1] // steps), lambda i, c: (0, i)) for a in blocked
            ] + [fixed(a) for a in whole],
            out_specs=[fixed(a) for a in extra_shapes] + [out] * 2,
            scratch_shapes=scratch,
        ),
        out_shape=list(extra_shapes)
        + [jax.ShapeDtypeStruct((groups // 2, chunk, columns), jnp.bfloat16)] * 2,
        compiler_params=pltpu.CompilerParams(vmem_limit_bytes=VMEM_BYTES),
        cost_estimate=pl.CostEstimate(flops=0, bytes_accessed=10_000_000, transcendentals=0),
        name=name,
    )(core.reshape(1), *blocked, *whole)


def branch_weights(core, groups, normed, branch, latent_normed, query, mixed, kv):
    columns = (
        query.shape[1] + mixed.shape[1] + kv.shape[1] * latent_normed.shape[1] // normed.shape[1]
    )
    return paired_call(
        branch_weights_kernel, core, groups, columns, [normed, branch, latent_normed],
        [query, mixed, kv], [], [], "branch_weights",
    )


def latent_weights_kernel(core_ref, n_ref, t_ref, token_ref, w_latent_ref, ffn_ref, logit_ref, latent_ref,
                          latent_gain_ref, cosine_ref, sine_ref, scale_ref, *rest):
    *pieces, latent_grad_ref, mean_ref, mine_ref, other_ref, gain_buf, latent_gain_buf = rest
    step = pl.program_id(0)
    count = len(pieces)
    pairs, chunk, _ = mine_ref.shape
    rows = latent_ref.shape[0]
    block = n_ref.shape[1]
    first = core_ref[0] == 0

    @pl.when(step == 0)
    def _():
        total = sum(piece[...].astype(jnp.float32) for piece in pieces)
        for number in range(count):
            gain_buf[number] = (
                total[rows + number:rows + number + 1, :block]
                + total[rows + count + number:rows + count + number + 1, :block]
            )
        latent = latent_ref[...]
        compressed = latent[:, :KV_RANK]
        scale = lax.rsqrt(jnp.mean(compressed * compressed, axis=1, keepdims=True) + EPS)
        unit = compressed * scale
        grad = total[:rows, :KV_RANK]
        gains = jnp.sum(grad * unit, axis=0, keepdims=True)
        width = KV_RANK // count
        for number in range(count):
            latent_gain_buf[number] = gains[:, number * width:(number + 1) * width]
        grad = grad * latent_gain_ref[...]
        grad = scale * (grad - unit * jnp.mean(unit * grad, axis=1, keepdims=True))
        half = ROPE // 2
        former = total[:rows, KV_RANK:KV_RANK + half]
        latter = total[:rows, KV_RANK + half:KV_RANK + ROPE]
        cosine, sine = cosine_ref[...], sine_ref[...]
        latent_grad = jnp.concatenate(
            [grad, former * cosine + latter * sine, latter * cosine - former * sine], axis=1
        ).astype(jnp.bfloat16)
        latent_grad_ref[...] = latent_grad
        sums = total[:rows, KV_RANK + ROPE:KV_RANK + ROPE + 2]
        mean_ref[...] = (
            jnp.sum(sums, axis=1, keepdims=True)
            + jnp.sum(latent_grad.astype(jnp.float32) * latent, axis=1, keepdims=True)
        ) / (block * count)

    def by_pairs(grad):
        return grad.reshape(pairs, 2, grad.shape[0] // (2 * pairs), grad.shape[1])

    low = 0
    for rows_ref, grads in ((n_ref, latent_grad_ref), (t_ref, logit_ref)):
        grad = matmul_tn(rows_ref[...], grads[...])
        put_pairs(first, by_pairs(grad), 0, low, mine_ref, other_ref)
        low += grad.shape[1]
    unit = token_ref[...].astype(jnp.float32) * scale_ref[...]
    routed = matmul(latent_grad_ref[...], w_latent_ref[...])
    gain = gain_buf[step] + jnp.sum(routed * unit, axis=0, keepdims=True)
    line = lax.broadcasted_iota(jnp.int32, (LANES, block), 0)
    gains = by_pairs(jnp.where(line == 0, gain, jnp.where(line == 1, ffn_ref[...], 0.0)).T)
    width = latent_gain_buf.shape[2]
    kv_chunk = width // (2 * pairs)
    line = lax.broadcasted_iota(jnp.int32, (LANES, width), 0)
    more = by_pairs(jnp.where(line == 2, latent_gain_buf[step], 0.0).T)
    gains = jnp.concatenate([gains[:, :, :kv_chunk] + more, gains[:, :, kv_chunk:]], axis=2)
    put_pairs(first, gains, 0, low, mine_ref, other_ref)


def latent_weights(core, groups, normed, normed_two, tokens, w_latent, ffn_gain, logit, latent, latent_gain,
                   cosine, sine, scale, pieces):
    count = len(pieces)
    shapes = [
        jax.ShapeDtypeStruct(latent.shape, jnp.bfloat16),
        jax.ShapeDtypeStruct(scale.shape, jnp.float32),
    ]
    scratch = [
        pltpu.VMEM((count, 1, normed.shape[1] // count), jnp.float32),
        pltpu.VMEM((count, 1, KV_RANK // count), jnp.float32),
    ]
    return paired_call(
        latent_weights_kernel, core, groups, latent.shape[1] + logit.shape[1] + LANES,
        [normed, normed_two, tokens, w_latent.T, ffn_gain],
        [logit, latent, latent_gain.reshape(1, -1), cosine, sine, scale, *pieces], shapes, scratch,
        "latent_weights",
    )


def pair_kernel(mine_ref, got_ref, *rest):
    rest[-1][...] = (
        mine_ref[...].astype(jnp.float32) + got_ref[...].astype(jnp.float32)
    ).astype(jnp.bfloat16)


def pair_sum(mine, got, columns, place, whole=None):
    chips, rows, width = mine.shape
    steps = 4
    block = pl.BlockSpec((chips // steps, rows, width), lambda i: (i, 0, 0))
    before = () if whole is None else (whole,)
    return pl.pallas_call(
        pair_kernel,
        grid=(steps,),
        in_specs=[block, block] + [pl.BlockSpec(memory_space=pl.ANY)] * len(before),
        out_specs=pl.BlockSpec((chips // steps, rows, width), lambda i: (i, 0, place)),
        out_shape=jax.ShapeDtypeStruct((chips, rows, columns), jnp.bfloat16),
        input_output_aliases={2: 0} if before else {},
        compiler_params=pltpu.CompilerParams(vmem_limit_bytes=VMEM_BYTES),
        cost_estimate=pl.CostEstimate(flops=0, bytes_accessed=14_000_000, transcendentals=0),
        name="pair_sum",
    )(mine, got, *before)


def final_kernel(edges, part_ref, query_ref, output_ref, kv_ref, latent_ref, router_ref,
                 *rest):
    *gain_refs, total_ref = rest
    step = pl.program_id(0)

    @pl.when(step == 0)
    def _():
        total_ref[...] = jnp.zeros_like(total_ref)

    total = total_ref[...]
    for number in range(part_ref.shape[0]):
        total = total + part_ref[number].astype(jnp.float32)
    total_ref[...] = total

    @pl.when(step == pl.num_programs(0) - 1)
    def _():
        outs = (query_ref, output_ref, kv_ref, latent_ref, router_ref)
        for out, low, high in zip(outs, edges[:5], edges[1:6]):
            if out is not kv_ref:
                out[...] = total_ref[:, low:high]
                continue
            chunk = out.shape[0]
            for place in range(total_ref.shape[0] // chunk):
                out[:, place * (high - low):(place + 1) * (high - low)] = (
                    total_ref[place * chunk:(place + 1) * chunk, low:high]
                )
        gains = total_ref[:, edges[5]:].T
        for number, gain_ref in enumerate(gain_refs):
            gain_ref[...] = gains[number:number + 1, :]


def final_sums(parts, edges, shapes):
    chips, rows, columns = parts.shape
    step = 4
    return pl.pallas_call(
        functools.partial(final_kernel, edges),
        grid=(chips // step,),
        in_specs=[pl.BlockSpec((step, rows, columns), lambda i: (i, 0, 0))],
        out_specs=[pl.BlockSpec(a.shape, lambda i: (0, 0)) for a in shapes],
        out_shape=shapes,
        scratch_shapes=[pltpu.VMEM((rows, columns), jnp.float32)],
        compiler_params=pltpu.CompilerParams(vmem_limit_bytes=VMEM_BYTES),
        cost_estimate=pl.CostEstimate(flops=0, bytes_accessed=6_000_000, transcendentals=0),
        name="final_sums",
    )(parts)


def ordered_kernel(rank_ref, *refs):
    *pieces, out_ref = refs
    count = len(pieces)
    part = pieces[0].shape[1]
    for place in range(count):
        turn = lax.rem(rank_ref[0] - place + count, count)
        for number, piece in enumerate(pieces):
            @pl.when(turn == number)
            def _():
                out_ref[:, place * part:(place + 1) * part] = piece[...]


def ordered_columns(rank, pieces):
    rows, part = pieces[0].shape
    shape = jax.ShapeDtypeStruct((rows, part * len(pieces)), pieces[0].dtype)
    return pl.pallas_call(
        ordered_kernel,
        grid_spec=pltpu.PrefetchScalarGridSpec(
            num_scalar_prefetch=1, grid=(1,), in_specs=full_specs(pieces),
            out_specs=full_specs([shape])[0],
        ),
        out_shape=shape,
        compiler_params=pltpu.CompilerParams(vmem_limit_bytes=VMEM_BYTES),
        cost_estimate=pl.CostEstimate(flops=0, bytes_accessed=2_000_000, transcendentals=0),
        name="ordered_columns",
    )(rank.reshape(1), *pieces)


def swap_cores(rows, groups):
    return lax.ppermute(rows, "expert", [(index, index ^ 1) for index in range(groups)])


def shards(
    tokens,
    cotangent,
    attn_gain,
    w_query,
    w_latent,
    latent_gain,
    w_keyvalue,
    w_output,
    ffn_gain,
    w_router,
    shared_gate,
    shared_up,
    shared_down,
    expert_gate,
    expert_up,
    expert_down,
    routes,
):
    bf16 = jnp.bfloat16
    f32 = jnp.float32
    tok_rows, model_width = tokens.shape
    top_count = routes.shape[1]
    expert_count = w_router.shape[1]
    local_experts, _, hidden_width = expert_gate.shape
    groups = lax.axis_size("expert")
    ranks = lax.axis_size("tensor")
    rank = lax.axis_index("tensor")
    group = lax.axis_index("expert")
    part = model_width // ranks
    capacity = (4 * tok_rows * top_count + 3 * expert_count - 1) // (3 * expert_count)
    slot_count = expert_count * capacity
    per_group = local_experts * capacity
    qk_width = NOPE + ROPE
    local_heads = w_query.shape[1] // qk_width

    expert_ids = jnp.arange(expert_count, dtype=jnp.int32)
    selector = routes[:, :, None] == expert_ids[None, None, :]
    chosen_mask = jnp.sum(selector.astype(f32), axis=1)

    cotangent_part = column_block(cotangent, rank, part)
    chosen_low = jnp.pad(chosen_mask.astype(bf16), ((0, 0), (0, LANES - expert_count)))
    all_grads = lax.all_gather(
        jnp.concatenate([cotangent_part, chosen_low], axis=1), "expert", axis=0
    )

    tables = rotary_constants(tok_rows, local_heads)
    (normed, scale_one, query_pre, query_low, latent, latent_normed, keyvalue, key_rope, weights_full,
     attn_mixed, attended, *sends) = attention_forward(
        rank, tokens, attn_gain, latent_gain, tables, w_latent, w_query, w_keyvalue, w_output, ranks
    )

    token_ids = jnp.arange(tok_rows, dtype=jnp.int32)
    before = (token_ids[:, None] > token_ids[None, :]).astype(bf16)
    earlier = matmul(before, after(chosen_mask, attended).astype(bf16))
    place = jnp.sum(jnp.where(selector, earlier[:, None, :], 0.0), axis=-1).astype(jnp.int32)

    def one_hot(target, sideways):
        shape = (tok_rows, groups * capacity) if sideways else (slot_count, tok_rows)
        slot_ids = jnp.arange(shape[1] if sideways else shape[0], dtype=jnp.int32)
        found = jnp.zeros(shape, jnp.bool_)
        for choice in range(top_count):
            if sideways:
                found = found | (target[:, choice][:, None] == slot_ids[None, :])
            else:
                found = found | (slot_ids[:, None] == target[:, choice][None, :])
        return found.astype(bf16)

    dispatch = one_hot(routes * capacity + place, False)
    pick, next_pick = (
        one_hot(
            jnp.where(lax.rem(routes, local_experts) == number,
                      routes // local_experts * capacity + place, -1),
            True,
        )
        for number in range(local_experts)
    )

    sends = [shift_ranks(sent, step + 1, ranks) for step, sent in enumerate(sends)]
    hidden_part, sent = hidden_rows(attended, column_block(tokens, rank, part), sends)
    first = (group * local_experts).reshape(1)
    pieces = [sent] + [shift_ranks(sent, step, ranks) for step in range(1, ranks)]

    rows_sent, normed_two, logits, scale_two = route_rows(
        rank, dispatch, ffn_gain, w_router, pieces
    )
    unit_two_part = hidden_part * scale_two
    sigmas = jax.nn.sigmoid(logits) * chosen_mask
    sigma_total = jnp.sum(sigmas, axis=-1, keepdims=True)
    arrived = lax.all_to_all(
        rows_sent.reshape(groups, per_group, -1), "expert", split_axis=0, concat_axis=0, tiled=True
    )
    chosen_rows, *grad_quarters = owner_rows(
        first, after(all_grads, normed_two), local_experts, capacity
    )
    grads_arrived = [lax.all_gather(rows, "tensor", axis=0) for rows in grad_quarters]

    shared_gate_pre = matmul(normed_two, shared_gate)
    shared_up_pre = matmul(normed_two, shared_up)
    shared_act = (jax.nn.silu(shared_gate_pre) * shared_up_pre).astype(bf16)
    shared_part = matmul(shared_act, shared_down)
    grad_shared_act = matmul_nt(cotangent, shared_down)
    shared_gate_grad, shared_up_grad = silu_back(grad_shared_act, shared_gate_pre, shared_up_pre)
    norm_part = matmul_nt(shared_gate_grad, shared_gate) + matmul_nt(shared_up_grad, shared_up)
    shared_dot = jnp.sum(
        shared_gate_grad.astype(f32) * shared_gate_pre + shared_up_grad.astype(f32) * shared_up_pre,
        axis=-1, keepdims=True,
    )
    shared_grads = shared_weights(
        normed_two, cotangent, shared_gate_grad, shared_up_grad, shared_act, groups
    )

    width = -(-hidden_width // LANES) * LANES
    widen = ((0, 0), (0, width - hidden_width), (0, 0))
    gate_up = jnp.concatenate(
        [jnp.pad(expert_gate.transpose(0, 2, 1), widen), jnp.pad(expert_up.transpose(0, 2, 1), widen)],
        axis=1,
    )
    weights = (gate_up, jnp.pad(expert_down, widen))
    arrived = after(
        arrived, shared_grads, shared_part, norm_part, shared_dot, pick, next_pick, *weights
    ).reshape(groups, local_experts, capacity, -1)
    pre_grad, act_weighted, back, sums = expert_rows(
        0, first, arrived, chosen_rows, w_router, grads_arrived[0], weights
    )
    back = lax.psum_scatter(back, "tensor", scatter_dimension=0, tiled=True)[0]
    next_grad, next_weighted, direct, next_produced = expert_rows(
        1, first, arrived, chosen_rows, w_router, grads_arrived[1], weights, sums
    )
    direct = lax.all_to_all(direct, "expert", split_axis=0, concat_axis=0, tiled=True)
    weight_grads = expert_weights(
        1, arrived, grads_arrived[1], next_grad, next_weighted, hidden_width
    )
    weight_grads = expert_weights(
        0, arrived, grads_arrived[0], pre_grad, act_weighted, hidden_width, weight_grads
    )
    direct = after(direct, *weight_grads).reshape(groups * capacity, -1)
    grad_expert_gate, grad_expert_up, grad_expert_down = weight_grads
    back = lax.all_to_all(
        after(back, direct), "expert", split_axis=0, concat_axis=0, tiled=True
    ).reshape(groups * capacity, -1)

    router_rows = lax.dynamic_slice_in_dim(w_router, rank * part, part, axis=0)
    ffn_gain_part = lax.dynamic_slice_in_dim(ffn_gain, rank * part, part, axis=0)
    norm_grad, extra_low, *sends = combine_rows(
        rank, next_pick, pick, direct, after(norm_part, router_rows, ffn_gain_part), shared_dot, ranks
    )
    norm_pieces = [shift_ranks(sent, step + 1, ranks) for step, sent in enumerate(sends)]
    hidden_grad, sent, logit_grad = norm_back(
        norm_grad, extra_low, pick, back, chosen_mask, logits, scale_two, hidden_part,
        ffn_gain_part, router_rows, cotangent_part, norm_pieces,
    )
    pieces = [sent] + [shift_ranks(sent, step, ranks) for step in range(1, ranks)]

    (branch_low, grad_ffn_gain, query_pre_grad, keyvalue_grad, normed_grad, latent_sent,
     *sends) = attention_backward(
        rank, pieces, weights_full, keyvalue, key_rope, query_low, query_pre, tokens, scale_one, tables,
        w_output, w_keyvalue, w_query,
    )
    pieces = [latent_sent] + [shift_ranks(latent_sent, step, ranks) for step in range(1, ranks)]
    normed_pieces = [
        shift_ranks(after(sent, *pieces), step + 1, ranks) for step, sent in enumerate(sends)
    ]

    returned = lax.all_to_all(
        after(next_produced, back, *norm_pieces), "expert", split_axis=0, concat_axis=0, tiled=True
    ).reshape(groups * capacity, -1)
    latent_sent = after(latent_sent, returned)

    chunk = model_width // groups
    kv_chunk = KV_RANK // groups
    core = lax.rem(group, 2)
    mine, other = branch_weights(
        core, groups, normed, branch_low, latent_normed, query_pre_grad, attn_mixed, keyvalue_grad
    )
    late_columns = mine.shape[2] + w_latent.shape[1] + expert_count + LANES
    late = pair_sum(mine, swap_cores(other, groups), late_columns, 0)
    latent_grad, row_mean, mine, other = latent_weights(
        core, groups, normed, normed_two, tokens, w_latent, grad_ffn_gain, logit_grad, latent,
        latent_gain, tables[3], tables[4], scale_one, pieces,
    )
    shared_width = shared_gate.shape[1]
    early = lax.psum_scatter(
        after(shared_grads, direct).reshape(groups * 3 * chunk, shared_width), "expert",
        scatter_dimension=0, tiled=True,
    )
    branch, *sends = branch_rows(rank, next_pick, after(returned, mine), shared_part, ranks)
    late = pair_sum(
        mine, swap_cores(after(other, returned), groups), late_columns,
        2, late,
    )
    late = lax.all_to_all(
        late, "expert", split_axis=0, concat_axis=0, tiled=True,
        axis_index_groups=[list(range(first_core, groups, 2)) for first_core in range(2)],
    )

    latent_rows = lax.dynamic_slice_in_dim(w_latent, rank * part, part, axis=0)
    attn_gain_part = lax.dynamic_slice_in_dim(attn_gain, rank * part, part, axis=0)
    block = jax.ShapeDtypeStruct((tok_rows, part), bf16)
    grad_tokens = single_call(
        token_kernel,
        [normed_grad, latent_grad, latent_rows, row_mean, column_block(tokens, rank, part), scale_one,
         attn_gain_part.reshape(1, part), hidden_grad, *normed_pieces],
        [block], "token_rows",
    )[0]
    grad_tokens = ordered_columns(
        rank, [grad_tokens] + [shift_ranks(grad_tokens, step, ranks) for step in range(1, ranks)]
    )
    sends = [shift_ranks(sent, step + 1, ranks) for step, sent in enumerate(sends)]
    output = single_call(
        output_kernel, [branch, hidden_part, pick, back, *sends],
        [block], "output_rows",
    )[0]
    output = ordered_columns(
        rank, [output] + [shift_ranks(output, step, ranks) for step in range(1, ranks)]
    )

    early = after(early, output).astype(f32)
    grad_shared_gate = early[:chunk]
    grad_shared_up = early[chunk:2 * chunk]
    grad_shared_down = early[2 * chunk:].T

    edges = [0]
    for columns in (
        query_pre_grad.shape[1], attn_mixed.shape[1],
        keyvalue_grad.shape[1] * KV_RANK // model_width, latent_grad.shape[1], expert_count, LANES,
    ):
        edges.append(edges[-1] + columns)
    shapes = [
        jax.ShapeDtypeStruct((chunk, high - low), f32) for low, high in zip(edges[:-1], edges[1:])
    ]
    shapes[2] = jax.ShapeDtypeStruct((kv_chunk, keyvalue_grad.shape[1]), f32)
    shapes[5:] = [jax.ShapeDtypeStruct((1, chunk), f32)] * 3
    grad_query, grad_output, grad_keyvalue, grad_latent, grad_router, *gains = final_sums(
        after(late, grad_shared_gate, grad_shared_up, grad_shared_down), tuple(edges), shapes
    )
    return (
        output,
        grad_tokens,
        gains[0].reshape(chunk),
        grad_query,
        grad_latent,
        gains[2][0, :kv_chunk],
        grad_keyvalue,
        grad_output.T,
        gains[1].reshape(chunk),
        grad_router,
        grad_shared_gate,
        grad_shared_up,
        grad_shared_down,
        grad_expert_gate.transpose(0, 2, 1),
        grad_expert_up.transpose(0, 2, 1),
        grad_expert_down,
    )


def solution(mesh):
    return jax.shard_map(
        shards,
        mesh=mesh,
        in_specs=(
            P("expert", None),
            P("expert", None),
            P(),
            P(None, "tensor"),
            P(),
            P(),
            P(None, "tensor"),
            P("tensor", None),
            P(),
            P(),
            P(None, "tensor"),
            P(None, "tensor"),
            P("tensor", None),
            P("expert", None, "tensor"),
            P("expert", None, "tensor"),
            P("expert", "tensor", None),
            P("expert", None),
        ),
        out_specs=(
            P("expert", None),
            P("expert", None),
            P("expert"),
            P("expert", "tensor"),
            P("expert", None),
            P("expert"),
            P("expert", "tensor"),
            P("tensor", "expert"),
            P("expert"),
            P("expert", None),
            P("expert", "tensor"),
            P("expert", "tensor"),
            P("tensor", "expert"),
            P("expert", None, "tensor"),
            P("expert", None, "tensor"),
            P("expert", "tensor", None),
        ),
        check_vma=False,
    )
```
